32 devices in a mesh: shard: 4 (over x, core), replica: 8 (over z, y).
Axes of the slice: x: 2, y: 2, z: 4, core: 2. Of those that a mesh axis runs over, the one named last changes fastest.
Arguments:
- tokens: bfloat16 [32768, 896], P(('shard', 'replica')), may hold values from -6 to 6
- segments: int32 [32, 1024], P(('shard', 'replica')), may hold values from 0 to 3, never falling along the last dimension, each value on 1 to 768 neighbouring positions
- cotangent: bfloat16 [32768, 896], P(('shard', 'replica')), may hold values from -6 to 6
- gain_attn: float32 [896], replicated, may hold values from 0.1 to 1.9
- gain_ffn: float32 [896], replicated, may hold values from 0.1 to 1.9
- w_query: bfloat16 [896, 896], P('shard'), may hold values from -0.1875 to 0.1875
- bias_query: float32 [896], replicated, may hold values from -3 to 3
- w_key: bfloat16 [896, 128], P('shard'), may hold values from -0.1875 to 0.1875
- bias_key: float32 [128], replicated, may hold values from -3 to 3
- w_value: bfloat16 [896, 128], P('shard'), may hold values from -0.1875 to 0.1875
- bias_value: float32 [128], replicated, may hold values from -3 to 3
- w_output: bfloat16 [896, 896], P('shard'), may hold values from -1.5 to 1.5
- w_gate: bfloat16 [896, 4864], P('shard'), may hold values from -0.1875 to 0.1875
- w_up: bfloat16 [896, 4864], P('shard'), may hold values from -0.1875 to 0.1875
- w_down: bfloat16 [4864, 896], P('shard'), may hold values from -0.078125 to 0.078125
Outputs:
- output: bfloat16 [32768, 896], P(('shard', 'replica'))
- grad_tokens: float32 [32768, 896], P(('shard', 'replica'))
- grad_gain_attn: float32 [896], replicated
- grad_gain_ffn: float32 [896], replicated
- grad_w_query: float32 [896, 896], P('shard')
- grad_bias_query: float32 [896], replicated
- grad_w_key: float32 [896, 128], P('shard')
- grad_bias_key: float32 [128], replicated
- grad_w_value: float32 [896, 128], P('shard')
- grad_bias_value: float32 [128], replicated
- grad_w_output: float32 [896, 896], P('shard')
- grad_w_gate: float32 [896, 4864], P('shard')
- grad_w_up: float32 [896, 4864], P('shard')
- grad_w_down: float32 [4864, 896], P('shard')
The draws below stay inside these ranges and needn't reach their ends.
Inputs may be any that keep to these rules, and one draw needn't show every extreme that they name: `segments`: each row is one device's pack: document numbers never fall along it, each document has 1 to 768 tokens, and one has exactly 768.
All inputs are finite; a program needn't handle non-finite values.
Results may differ from the reference program's by a relative error of at most 0.024.
Values may be sent and summed in bfloat16 or wider, within the bound.
No kernel may reach another device: no remote copies, remote signals or barrier semaphores. Data moves between devices by JAX's collectives and lax.ppermute only.
A program may use at most 256 MiB of HBM per device.

```python
import math
import jax
import jax.numpy as jnp
import numpy as np
from jax import lax

D = 896
FF = 4864
HEADS = 14
KVHEADS = 2
HD = 64
TOK_DEV = 1024
SEQ_DEV = 4
QW = 896
KVW = 128
LONGEST = 768
PACKS = 32
TOKENS = 32768


def steps_of(key, extent, cuts, smallest, largest):
    def one(position, blocks):
        heights = jax.random.uniform(jax.random.fold_in(jax.random.fold_in(key, 6), position), (blocks,), jnp.float32, smallest / len(cuts), largest / len(cuts))
        return jnp.repeat(jnp.exp(heights), extent[position] // blocks).reshape((-1,) + (1,) * (len(extent) - position - 1))

    level = one(*cuts[0])
    for cut in cuts[1:]:
        level = level * one(*cut)
    return level


def profile(count, total, limit, slope):
    weights = [(1 << 20) // math.isqrt(standing ** slope) + 1 for standing in range(2, count + 1)]
    surplus, holding = total - limit - (count - 1), [1] * (count - 1)
    while surplus > 0:
        candidates = [i for i in range(count - 1) if holding[i] < limit]
        whole, budget = sum([weights[i] for i in candidates]), surplus
        for i in candidates:
            more = min(limit - holding[i], max(1, budget * weights[i] // whole), surplus)
            holding[i] = holding[i] + more
            surplus = surplus - more
    return np.array([limit] + holding)


def ragged_sizes(own_key, count, total, limit, lean):
    if count == 2:
        one = jax.random.randint(own_key, (), max(1, total - limit), min(limit, total - 1) + 1)
        return jnp.stack([one, total - one])
    lengths = jnp.asarray(profile(count, total, limit, lean), jnp.int32)
    couples = (count - 1) // 2
    source_of, taker = lengths[1:1 + 2 * couples:2], lengths[2:2 + 2 * couples:2]
    room = jnp.minimum(source_of - 1, limit - taker)
    moved = jax.random.randint(jax.random.fold_in(own_key, 1), (couples,), 0, 1 << 20) % (room + 1)
    lengths = lengths.at[1:1 + 2 * couples:2].set(source_of - moved).at[2:2 + 2 * couples:2].set(taker + moved)
    return lengths[jax.random.permutation(jax.random.fold_in(own_key, 2), count)]


def gaussian(own_key, dims, deviation, reach, shards=(), kind=jnp.bfloat16):
    level = steps_of(own_key, dims, shards, -0.22, 0.18) if shards else 1.0
    drawn = jax.random.normal(own_key, dims, jnp.float32) * deviation * level
    return jnp.minimum(jnp.maximum(drawn, -reach), reach).astype(kind)


def setup_inputs(seed: int = 0) -> dict:
    key_of = jax.random.split(jax.random.key(seed), 16)
    tokens = gaussian(key_of[0], (TOKENS, D), 1.0, 6.0, ((0, 32),))
    segments = jax.vmap(lambda own: jnp.searchsorted(jnp.cumsum(ragged_sizes(own, SEQ_DEV, TOK_DEV, LONGEST, 2)), jnp.arange(TOK_DEV), side="right"))(jax.random.split(key_of[1], PACKS)).reshape((PACKS, TOK_DEV)).astype(jnp.int32)
    cotangent = gaussian(key_of[2], (TOKENS, D), 1.0, 6.0, ((0, 32),))
    gain_attn = jnp.clip(1.0 + 0.18 * jax.random.normal(key_of[3], (D,), jnp.float32), 0.1, 1.9)
    gain_ffn = jnp.clip(1.0 + 0.18 * jax.random.normal(key_of[4], (D,), jnp.float32), 0.1, 1.9)
    w_query = gaussian(key_of[5], (D, QW), D ** -0.5, 0.1875, ((0, 4),))
    bias_query = gaussian(key_of[6], (QW,), 0.5, 3.0, (), jnp.float32)
    w_key = gaussian(key_of[7], (D, KVW), D ** -0.5, 0.1875, ((0, 4),))
    bias_key = gaussian(key_of[8], (KVW,), 0.5, 3.0, (), jnp.float32)
    w_value = gaussian(key_of[9], (D, KVW), D ** -0.5, 0.1875, ((0, 4),))
    bias_value = gaussian(key_of[10], (KVW,), 0.5, 3.0, (), jnp.float32)
    w_output = gaussian(key_of[11], (QW, D), (QW // 64) ** -0.5, 1.5, ((0, 4),))
    w_gate = gaussian(key_of[12], (D, FF), D ** -0.5, 0.1875, ((0, 4),))
    w_up = gaussian(key_of[13], (D, FF), D ** -0.5, 0.1875, ((0, 4),))
    w_down = gaussian(key_of[14], (FF, D), FF ** -0.5, 0.078125, ((0, 4),))
    return dict(tokens=tokens, segments=segments, cotangent=cotangent, gain_attn=gain_attn, gain_ffn=gain_ffn, w_query=w_query, bias_query=bias_query, w_key=w_key, bias_key=bias_key, w_value=w_value, bias_value=bias_value, w_output=w_output, w_gate=w_gate, w_up=w_up, w_down=w_down)


epsilon = 1e-06
rope_base = 1000000.0
masked_score = -1e+30
highest = lax.Precision.HIGHEST

@jax.custom_vjp
def low(v):
    return lax.optimization_barrier(v.astype(jnp.bfloat16)).astype(jnp.float32)

@jax.custom_vjp
def low_back(v):
    return v

def low_keep(v):
    return (low(v), None)

def low_pass(kept, grad):
    return (grad,)

def back_keep(v):
    return (v, None)

def back_low(kept, grad):
    return (low(grad),)
low.defvjp(low_keep, low_pass)
low_back.defvjp(back_keep, back_low)

def matmul(left, right):
    return jnp.dot(left, right, precision=highest, preferred_element_type=jnp.float32)

def rms_norm(values, gain_vector):
    return values * lax.rsqrt(lax.optimization_barrier(jnp.mean(values * values, axis=-1, keepdims=True)) + epsilon) * gain_vector

def rotate(values, cosine_table, sine_table):
    half_width = values.shape[-1] // 2
    first_half = values[..., :half_width]
    second_half = values[..., half_width:]
    return jnp.concatenate([first_half * cosine_table - second_half * sine_table, second_half * cosine_table + first_half * sine_table], axis=-1)

def pack_tables(doc_ids):
    row_count = doc_ids.shape[0]
    row_ids = jnp.arange(row_count, dtype=jnp.int32)
    same_doc = doc_ids[:, None] == doc_ids[None, :]
    before = row_ids[None, :] < row_ids[:, None]
    places = lax.optimization_barrier(jnp.sum(jnp.where(same_doc & before, 1, 0).astype(jnp.int32), axis=1))
    allowed = same_doc & (row_ids[None, :] <= row_ids[:, None])
    frequency = rope_base ** (-jnp.arange(0, HD, 2).astype(jnp.float32) / HD)
    angles = places.astype(jnp.float32)[:, None] * frequency[None, :]
    return (allowed, jnp.cos(angles), jnp.sin(angles))

def attend_pack(bundle):
    query_proj, key_proj, value_proj, doc_ids = bundle
    row_count = query_proj.shape[0]
    group_size = HEADS // KVHEADS
    allowed, cosine_table, sine_table = pack_tables(doc_ids)
    queries = low(rotate(query_proj.reshape(row_count, HEADS, HD), cosine_table[:, None, :], sine_table[:, None, :]))
    key_rows = low(rotate(key_proj.reshape(row_count, KVHEADS, HD), cosine_table[:, None, :], sine_table[:, None, :]))
    value_rows = low(value_proj.reshape(row_count, KVHEADS, HD))
    queries = queries.reshape(row_count, KVHEADS, group_size, HD)
    scores = low_back(jnp.einsum('bkgd,rkd->kgbr', queries, key_rows, precision=highest) * 0.125)
    scores = jnp.where(allowed[None, None], scores, masked_score)
    shifted = scores - lax.optimization_barrier(jnp.max(scores, axis=-1, keepdims=True))
    exponent = jnp.exp(shifted)
    probabilities = low(exponent / lax.optimization_barrier(jnp.sum(exponent, axis=-1, keepdims=True)))
    mixed_heads = jnp.einsum('kgbr,rkd->bkgd', probabilities, value_rows, precision=highest)
    return low(low_back(mixed_heads.reshape(row_count, HEADS * HD)))

def reference(tokens, segments, cotangent, gain_attn, gain_ffn, w_query, bias_query, w_key, bias_key, w_value, bias_value, w_output, w_gate, w_up, w_down):
    floats = tuple((item.astype(jnp.float32) for item in (tokens, gain_attn, gain_ffn, w_query, bias_query, w_key, bias_key, w_value, bias_value, w_output, w_gate, w_up, w_down)))

    def forward(inputs, gain_one, gain_two, weight_query, vector_query, weight_key, vector_key, weight_value, vector_value, weight_output, weight_gate, weight_up, weight_down):
        normed = low(rms_norm(inputs, gain_one))
        query_proj = low_back(matmul(normed, weight_query) + vector_query)
        key_proj = low_back(matmul(normed, weight_key) + vector_key)
        value_proj = low_back(matmul(normed, weight_value) + vector_value)
        mixed_heads = lax.map(jax.checkpoint(attend_pack), (query_proj.reshape(PACKS, TOK_DEV, HEADS * HD), key_proj.reshape(PACKS, TOK_DEV, KVHEADS * HD), value_proj.reshape(PACKS, TOK_DEV, KVHEADS * HD), segments))
        mixed_heads = mixed_heads.reshape(TOKENS, HEADS * HD)
        residual = inputs + low_back(matmul(mixed_heads, weight_output))
        normed_two = low(rms_norm(residual, gain_two))
        gate_proj = low_back(matmul(normed_two, weight_gate))
        up_proj = low_back(matmul(normed_two, weight_up))
        hidden = low(gate_proj * jax.nn.sigmoid(gate_proj) * up_proj)
        return residual + low_back(matmul(hidden, weight_down))
    result, pullback = jax.vjp(forward, *floats)
    gradients = pullback(cotangent.astype(jnp.float32))
    return (result.astype(jnp.bfloat16), gradients[0], gradients[1], gradients[2], gradients[3], gradients[4], gradients[5], gradients[6], gradients[7], gradients[8], gradients[9], gradients[10], gradients[11], gradients[12])
```

```python
import functools

import jax
import jax.numpy as jnp
from jax import lax
from jax.experimental import pallas as pl
from jax.experimental.pallas import tpu as pltpu
from jax.sharding import PartitionSpec as P

HEADS,KVHEADS,HD=14,2,64
GROUP=HEADS//KVHEADS
PAIRS=HEADS//2
TILE=256
VMEM_CAP=56<<20
bf16,f32=jnp.bfloat16,jnp.float32
def nn(a,b): return lax.dot_general(a,b,(((1,),(0,)),((),())),preferred_element_type=f32)
def nt(a,b): return lax.dot_general(a,b,(((1,),(1,)),((),())),preferred_element_type=f32)
def tn(a,b): return lax.dot_general(a,b,(((0,),(0,)),((),())),preferred_element_type=f32)

def left_half(rows):
    return lax.broadcasted_iota(jnp.int32,(rows,2*HD),1)<HD

def attend_kernel(tiles,segc,segr,q,kx,vx,o,linv,*rest):
    probs,bias=rest[:tiles],rest[tiles]
    pair=pl.program_id(0)
    @pl.when(pair==0)
    def _():
        for i in range(tiles):
            w=(i+1)*TILE
            rows=lax.broadcasted_iota(jnp.int32,(TILE,w),0)+i*TILE
            cols=lax.broadcasted_iota(jnp.int32,(TILE,w),1)
            ok=(segc[i*TILE:w,:]==segr[:,:w])&(cols<=rows)
            bias[i*TILE:w,:w]=jnp.where(ok,0.0,-1e30)
    left=left_half(TILE)
    kinds=[2*(2*pair+side>=GROUP).astype(jnp.int32)+side for side in (0,1)]
    for i in range(tiles):
        w=(i+1)*TILE
        block=q[i*TILE:w,:]
        mixed=[]
        for side in (0,1):
            s=nt(block,kx[kinds[side],:w,:])+bias[i*TILE:w,:w]
            e=jnp.exp(s-jnp.max(s,axis=-1,keepdims=True)).astype(bf16)
            for j in range(i+1):
                probs[j][side,(i-j)*TILE:(i-j+1)*TILE,:]=e[:,j*TILE:(j+1)*TILE]
            mixed.append(nn(e,vx[kinds[side],:w,:]))
        totals=jnp.where(left,pltpu.roll(mixed[0],HD,1),pltpu.roll(mixed[1],HD,1))
        inverse=1.0/totals
        o[i*TILE:w,:]=(jnp.where(left,mixed[0],mixed[1])*inverse).astype(bf16)
        linv[i*TILE:w,:]=inverse

def attend(segments,q,kx,vx):
    t=q.shape[0]; tiles=t//TILE
    whole=lambda *s: pl.BlockSpec(s,lambda p:(0,)*len(s))
    lane=pl.BlockSpec((t,2*HD),lambda p:(0,p))
    pshape=[(HEADS,t-j*TILE,TILE) for j in range(tiles)]
    return pl.pallas_call(functools.partial(attend_kernel,tiles),grid=(PAIRS,),
        in_specs=[whole(t,1),whole(1,t),lane,whole(4,t,2*HD),whole(4,t,2*HD)],
        out_specs=[lane,lane]+[pl.BlockSpec((2,)+s[1:],lambda p:(p,0,0)) for s in pshape],
        out_shape=[jax.ShapeDtypeStruct(q.shape,bf16),jax.ShapeDtypeStruct(q.shape,f32)]+[jax.ShapeDtypeStruct(s,bf16) for s in pshape],
        scratch_shapes=[pltpu.VMEM((t,t),f32)],
        compiler_params=pltpu.CompilerParams(vmem_limit_bytes=VMEM_CAP),
        cost_estimate=pl.CostEstimate(flops=20*10**9,bytes_accessed=40*10**6,transcendentals=9*10**6),
        name="attend")(segments.reshape(t,1),segments.reshape(1,t),q,kx,vx)

def swap_halves(v,lanes):
    half=HD//2
    return jnp.where(lanes%HD<half,pltpu.roll(v,v.shape[1]-half,1),pltpu.roll(v,half,1))

def attend_back_kernel(tiles,q,do,o,kx,vz,cos,sin,*rest):
    probs=rest[:tiles]
    dq,dk,dv,ds0,ds1,dkacc,dvacc=rest[tiles:]
    pair=pl.program_id(0)
    t=q.shape[0]
    @pl.when(pair==0)
    def _():
        dkacc[...]=jnp.zeros_like(dkacc)
        dvacc[...]=jnp.zeros_like(dvacc)
    left=left_half(t)
    t_=do[...].astype(f32)*o[...].astype(f32)
    inner=[jnp.sum(jnp.where(left,t_,0.0),axis=-1,keepdims=True),jnp.sum(jnp.where(left,0.0,t_),axis=-1,keepdims=True)]
    kinds=[2*(2*pair+side>=GROUP).astype(jnp.int32)+side for side in (0,1)]
    for side,ds in ((0,ds0),(1,ds1)):
        kind=kinds[side]
        for j in range(tiles):
            lo=j*TILE
            p=probs[j][side]
            dp=nt(do[lo:,:],vz[kind,lo:lo+TILE,:])
            d=(p.astype(f32)*(dp-inner[side][lo:])).astype(bf16)
            ds[lo:,lo:lo+TILE]=d
            dkacc[kind,lo:lo+TILE,:]+=tn(d,q[lo:,:])
            dvacc[kind,lo:lo+TILE,:]+=tn(p,do[lo:,:])
    lanes=lax.broadcasted_iota(jnp.int32,(TILE,2*HD),1)
    for i in range(tiles):
        w=(i+1)*TILE
        g=(nn(ds0[i*TILE:w,:w],kx[kinds[0],:w,:])+nn(ds1[i*TILE:w,:w],kx[kinds[1],:w,:]))*0.125
        dq[i*TILE:w,:]=(g*cos[i*TILE:w,:]-swap_halves(g,lanes)*sin[i*TILE:w,:]).astype(bf16)
    @pl.when(pair==PAIRS-1)
    def _():
        lanes=lax.broadcasted_iota(jnp.int32,(t,2*HD),1)
        g=jnp.where(left,dkacc[0]+pltpu.roll(dkacc[1],HD,1),pltpu.roll(dkacc[2],HD,1)+dkacc[3])
        dk[...]=(g*cos[...]-swap_halves(g,lanes)*sin[...]).astype(bf16)
        dv[...]=jnp.where(left,dvacc[0]+pltpu.roll(dvacc[1],HD,1),pltpu.roll(dvacc[2],HD,1)+dvacc[3]).astype(bf16)

def attend_back(q,do,o,kx,vz,cos,sin,probs):
    t=q.shape[0]; tiles=t//TILE
    whole=lambda *s: pl.BlockSpec(s,lambda p:(0,)*len(s))
    lane=pl.BlockSpec((t,2*HD),lambda p:(0,p))
    return pl.pallas_call(functools.partial(attend_back_kernel,tiles),grid=(PAIRS,),
        in_specs=[lane,lane,lane,whole(4,t,2*HD),whole(4,t,2*HD),whole(t,2*HD),whole(t,2*HD)]+[pl.BlockSpec((2,)+p.shape[1:],lambda p:(p,0,0)) for p in probs],
        out_specs=[lane,whole(t,2*HD),whole(t,2*HD)],
        out_shape=[jax.ShapeDtypeStruct(q.shape,bf16)]+[jax.ShapeDtypeStruct((t,2*HD),bf16)]*2,
        scratch_shapes=[pltpu.VMEM((t,t),bf16)]*2+[pltpu.VMEM((4,t,2*HD),f32)]*2,
        compiler_params=pltpu.CompilerParams(vmem_limit_bytes=VMEM_CAP),
        cost_estimate=pl.CostEstimate(flops=30*10**9,bytes_accessed=40*10**6,transcendentals=0),
        name="attend_back")(q,do,o,kx,vz,cos,sin,*probs)

def pad_heads(rows,other):
    t=rows.shape[0]
    fill=jnp.full((t,HD),other,rows.dtype)
    out=[]
    for kv in range(KVHEADS):
        one=rows[:,kv*HD:(kv+1)*HD]
        out+= [jnp.concatenate([one,fill],1),jnp.concatenate([fill,one],1)]
    return jnp.stack(out)

BLK=256
def cuts(n):
    return [(a,min(a+BLK,n)) for a in range(0,n,BLK)]
def ffn_kernel(steps,place,n2,dy,gu0,gu1,gu2,gu3,d0,d1,d2,hid,dg,du,keep_gu,send_gu,keep_d,send_d,wgu,wd,ag,au,ad):
    step=pl.program_id(0)
    rows=gu0.shape[1]; half=d0.shape[0]; part=d1.shape[0]
    width=wgu.shape[2]
    @pl.when(step==0)
    def _():
        for n,piece in enumerate((gu0,gu1,gu2,gu3)):
            at=pl.ds(pl.multiple_of(place[n]*rows,16),rows)
            wgu[0,at,:]=piece[0]
            wgu[1,at,:]=piece[1]
        wd[pl.ds(pl.multiple_of(place[4]*half,16),half),:]=d0[...]
        wd[pl.ds(pl.multiple_of(place[5]*part,16),part),:]=d1[...]
        wd[pl.ds(pl.multiple_of(place[6]*part,16),part),:]=d2[...]
        ag[...]=jnp.zeros_like(ag); au[...]=jnp.zeros_like(au); ad[...]=jnp.zeros_like(ad)
    x=n2[...]; y=dy[...]
    for lo,hi in cuts(width):
        gate=nn(x,wgu[0,:,lo:hi]); up=nn(x,wgu[1,:,lo:hi]); dh=nt(y,wd[lo:hi,:])
        sig=jax.nn.sigmoid(gate); silu=gate*sig
        h=(silu*up).astype(bf16)
        g=(dh*up*(sig+silu*(1.0-sig))).astype(bf16)
        u=(dh*silu).astype(bf16)
        hid[:,lo:hi]=h; dg[:,lo:hi]=g; du[:,lo:hi]=u
        ad[lo:hi,:]+=tn(h,y)
        ag[:,lo:hi]+=tn(x,g)
        au[:,lo:hi]+=tn(x,u)
    @pl.when(step==steps-1)
    def _():
        mine,other=place[7],1-place[7]
        for ref,side in ((keep_gu,mine),(send_gu,other)):
            at=pl.ds(pl.multiple_of(side*2*rows,16),2*rows)
            ref[0]=ag[at,:].astype(bf16); ref[1]=au[at,:].astype(bf16)
        for ref,side in ((keep_d,mine),(send_d,other)):
            ref[...]=ad[pl.ds(pl.multiple_of(side*half,16),half),:].astype(bf16)
def ffn_part(place,n2,dy,gus,ds,tt=512):
    t,d=n2.shape; width=gus[0].shape[2]; half=ds[0].shape[0]; steps=t//tt
    whole=lambda *s: pl.BlockSpec(s,lambda i:(0,)*len(s))
    tok=lambda c: pl.BlockSpec((tt,c),lambda i:(i,0))
    S=jax.ShapeDtypeStruct
    return pl.pallas_call(functools.partial(ffn_kernel,steps),grid=(steps,),
      in_specs=[pl.BlockSpec(memory_space=pltpu.SMEM),tok(d),tok(d)]+[whole(*g.shape) for g in gus]+[whole(*g.shape) for g in ds],
      out_specs=[tok(width)]*3+[whole(2,d//2,width)]*2+[whole(half,d)]*2+[whole(2,d,width),whole(width,d)],
      out_shape=[S((t,width),bf16)]*3+[S((2,d//2,width),bf16)]*2+[S((half,d),bf16)]*2+[S((2,d,width),bf16),S((width,d),bf16)],
      scratch_shapes=[pltpu.VMEM((d,width),f32)]*2+[pltpu.VMEM((width,d),f32)],
      compiler_params=pltpu.CompilerParams(vmem_limit_bytes=VMEM_CAP),
      cost_estimate=pl.CostEstimate(flops=12*t*d*width,bytes_accessed=20*10**6,transcendentals=t*width),
      name="ffn_part")(place,n2,dy,*gus,*ds)
def tokens_sum_kernel(parts,*refs):
    out=refs[-1]
    total=None
    for n in range(parts):
        dg,du,w=refs[3*n:3*n+3]
        s=nt(dg[...],w[0])+nt(du[...],w[1])
        total=s if total is None else total+s
    out[...]=total.astype(out.dtype)
def back_tokens(dgs,dus,wgus,first,rows,dtype,tt=512):
    d=wgus[0].shape[1]; n0=first//tt
    ops,specs=[],[]
    fl=0
    for g,u,w in zip(dgs,dus,wgus):
        ops+=[g,u,w]; fl+=4*rows*d*g.shape[1]
        specs+=[pl.BlockSpec((tt,g.shape[1]),lambda i:(i+n0,0))]*2+[pl.BlockSpec(w.shape,lambda i:(0,0,0))]
    return pl.pallas_call(functools.partial(tokens_sum_kernel,len(dgs)),grid=(rows//tt,),in_specs=specs,
      out_specs=pl.BlockSpec((tt,d),lambda i:(i,0)),out_shape=jax.ShapeDtypeStruct((rows,d),dtype),
      compiler_params=pltpu.CompilerParams(vmem_limit_bytes=VMEM_CAP),
      cost_estimate=pl.CostEstimate(flops=fl,bytes_accessed=30*10**6,transcendentals=0),name="back_tokens")(*ops)
def down_kernel(parts,*refs):
    total=None
    for n in range(parts):
        s=nn(refs[2*n][...],refs[2*n+1][...])
        total=s if total is None else total+s
    refs[-1][...]=total.astype(refs[-1].dtype)
def down_tokens(hids,wds,first,rows,dtype,tt=512):
    d=wds[0].shape[1]; n0=first//tt
    ops,specs=[],[]
    fl=0
    for h,w in zip(hids,wds):
        ops+=[h,w]; fl+=2*rows*d*h.shape[1]
        specs+=[pl.BlockSpec((tt,h.shape[1]),lambda i:(i+n0,0)),pl.BlockSpec(w.shape,lambda i:(0,0))]
    return pl.pallas_call(functools.partial(down_kernel,len(hids)),grid=(rows//tt,),in_specs=specs,
      out_specs=pl.BlockSpec((tt,d),lambda i:(i,0)),out_shape=jax.ShapeDtypeStruct((rows,d),dtype),
      compiler_params=pltpu.CompilerParams(vmem_limit_bytes=VMEM_CAP),
      cost_estimate=pl.CostEstimate(flops=fl,bytes_accessed=20*10**6,transcendentals=0),name="down_tokens")(*ops)

epsilon = 1e-06
rope_base = 1000000.0


def rms_stats(values, gain_vector):
    inverse = lax.rsqrt(jnp.mean(values * values, axis=-1, keepdims=True) + epsilon)
    return (values * inverse * gain_vector, inverse)


def norm_back(values, inverse, gain_vector, upstream):
    scaled = upstream * gain_vector
    grad_gain = jnp.sum(upstream * values * inverse, axis=0)
    correction = jnp.sum(scaled * values, axis=-1, keepdims=True) / values.shape[-1]
    grad_values = inverse * scaled - values * (inverse * inverse * inverse) * correction
    return (grad_values, grad_gain)


def rotate(values, cosine_table, sine_table):
    half = values.shape[-1] // 2
    a, b = values[..., :half], values[..., half:]
    return jnp.concatenate([a * cosine_table - b * sine_table, b * cosine_table + a * sine_table], axis=-1)


def angles_of(doc_ids):
    t = doc_ids.shape[0]
    earlier = jnp.sum((doc_ids[None, :] < doc_ids[:, None]).astype(jnp.int32), axis=1)
    places = jnp.arange(t, dtype=jnp.int32) - earlier
    frequency = rope_base ** (-jnp.arange(0, HD, 2).astype(jnp.float32) / HD)
    return places.astype(jnp.float32)[:, None] * frequency[None, :]


def widths_of(rows):
    big = [256] * (rows // 256)
    rest = rows - sum(big)
    return big + ([rest] if rest else [])


class Links:
    def __init__(self, shards, replicas):
        self.shards, self.replicas = shards, replicas
        s, r = lax.axis_index("shard"), lax.axis_index("replica")
        self.x, self.c, self.y, self.z = s // 2, s % 2, r % 2, r // 2

    def core(self, v):
        return lax.ppermute(v, "shard", [(i, i ^ 1) for i in range(self.shards)])

    def across(self, v):
        return lax.ppermute(v, "shard", [(i, i ^ 2) for i in range(self.shards)])

    def beside(self, v):
        return lax.ppermute(v, "replica", [(i, i ^ 1) for i in range(self.replicas)])

    def line(self, v):
        if self.replicas == 8:
            v = v + lax.ppermute(v, "replica", [(0, 2), (1, 3), (6, 4), (7, 5)])
            v = v + lax.ppermute(v, "replica", [(2, 4), (4, 2), (3, 5), (5, 3)])
            ends = lax.ppermute(v, "replica", [(2, 0), (3, 1), (4, 6), (5, 7)])
            return jnp.where((self.z == 0) | (self.z == 3), ends, v)
        bit = 2
        while bit < self.replicas:
            v = v + lax.ppermute(v, "replica", [(i, i ^ bit) for i in range(self.replicas)])
            bit *= 2
        return v

    def both(self, v, axis):
        half = v.shape[axis] // 2
        take = lambda n: lax.dynamic_slice_in_dim(v, n * half, half, axis)
        return take(self.y), take(1 - self.y)

    def replica_sum(self, v, axis):
        keep, send = self.both(v, axis)
        total = self.line(keep + self.beside(send))
        return total, self.beside(total)

    def in_order(self, mine, other, axis):
        first = jnp.where(self.y == 0, mine, other)
        second = jnp.where(self.y == 0, other, mine)
        return jnp.concatenate([first, second], axis)

    def everywhere(self, v):
        v = v + self.core(v)
        v = v + self.across(v)
        v = v + self.beside(v)
        return self.line(v)


def product(left, right):
    return jnp.dot(left, right, preferred_element_type=jnp.float32)


def on_device(
    links_shape,
    tokens,
    segments,
    cotangent,
    gain_attn,
    gain_ffn,
    w_query,
    bias_query,
    w_key,
    bias_key,
    w_value,
    bias_value,
    w_output,
    w_gate,
    w_up,
    w_down,
):
    links = Links(*links_shape)
    x, c, y = links.x, links.c, links.y
    t, d = tokens.shape
    own = w_query.shape[0]
    inputs = tokens.astype(f32)
    doc_ids = segments[0]

    def gathered(local):
        opposite = links.across(local)
        pair = jnp.stack([local, opposite])
        partner = links.core(pair)
        rows = []
        for s in range(4):
            from_mine = jnp.where(x == s // 2, pair[0], pair[1])
            from_partner = jnp.where(x == s // 2, partner[0], partner[1])
            rows.append(jnp.where(c == s % 2, from_mine, from_partner))
        return jnp.concatenate(rows, 0)

    full_qkv = gathered(jnp.concatenate([w_query, w_key, w_value], 1))
    full_output = gathered(w_output)

    ff_rows = w_down.shape[0]
    widths = widths_of(ff_rows)
    offsets = [sum(widths[:n]) for n in range(len(widths))]

    def section(core, off, w):
        return jnp.stack(
            [
                jnp.concatenate(
                    [m[:, (2 * side + core) * ff_rows + off : (2 * side + core) * ff_rows + off + w] for side in (0, 1)], 1
                )
                for m in (w_gate, w_up)
            ]
        )

    gathered_parts = []
    for off, w in zip(offsets, widths):
        sec0, sec1 = section(0, off, w), section(1, off, w)
        mine = jnp.where(c == 0, sec0, sec1)
        core_rows = links.core(jnp.where(c == 0, sec1, sec0))
        x_rows = links.across(jnp.where(y == c, mine, core_rows))
        y_rows = links.beside(x_rows)
        down = w_down[off : off + w]
        x_down = links.across(lax.dynamic_slice_in_dim(down, y * (w // 2), w // 2, 0))
        y_down = links.beside(x_down)
        gathered_parts.append(([mine, core_rows, x_rows, y_rows], [down, x_down, y_down]))
    place = jnp.stack(
        [2 * x + c, 2 * x + 1 - c, 2 * (1 - x) + y, 2 * (1 - x) + 1 - y, x, 2 * (1 - x) + y, 2 * (1 - x) + 1 - y, x]
    ).astype(jnp.int32)

    dy_all = jnp.concatenate([cotangent, links.core(cotangent)], 0)

    angle = angles_of(doc_ids)
    cosine, sine = jnp.cos(angle), jnp.sin(angle)
    normed, inverse_one = rms_stats(inputs, gain_attn)
    normed_low = normed.astype(bf16)
    proj = product(normed_low, full_qkv) + jnp.concatenate([bias_query, bias_key, bias_value])
    qw, kw = w_query.shape[1], w_key.shape[1]
    cos_heads, sin_heads = cosine[:, None, :], sine[:, None, :]
    queries = rotate(proj[:, :qw].reshape(t, HEADS, HD), cos_heads, sin_heads).astype(bf16)
    queries = (queries.astype(f32) * 0.125).astype(bf16).reshape(t, qw)
    key_rows = rotate(proj[:, qw : qw + kw].reshape(t, KVHEADS, HD), cos_heads, sin_heads).astype(bf16).reshape(t, kw)
    value_rows = proj[:, qw + kw :].astype(bf16)
    kx, vx, vz = pad_heads(key_rows, 0), pad_heads(value_rows, 1), pad_heads(value_rows, 0)
    mixed_low, inverse_sums, *probs = attend(doc_ids, queries, kx, vx)
    residual = inputs + product(mixed_low, full_output)
    normed_two, inverse_two = rms_stats(residual, gain_ffn)
    normed_two_low = normed_two.astype(bf16)
    n2_all = jnp.concatenate([normed_two_low, links.core(normed_two_low)], 0)

    hids, dgs, dus, wgus, wds, gate_up, downs = [], [], [], [], [], [], []
    for gus, ds in gathered_parts:
        hid, dg, du, keep_gu, send_gu, keep_d, send_d, wgu, wd = ffn_part(place, n2_all, dy_all, gus, ds)
        hids.append(hid), dgs.append(dg), dus.append(du), wgus.append(wgu), wds.append(wd)
        half_gu, other_gu = links.replica_sum(keep_gu + links.across(send_gu), 1)
        own_rows = jnp.where(c == y, half_gu, other_gu)
        send_rows = jnp.where(c == y, other_gu, half_gu)
        gate_up.append((own_rows, links.core(send_rows)))
        half_d, other_d = links.replica_sum(keep_d + links.across(send_d), 0)
        downs.append(links.in_order(half_d, other_d, 0))

    send_dn2 = back_tokens(dgs, dus, wgus, t, t, bf16)
    grad_normed_two = back_tokens(dgs, dus, wgus, 0, t, f32) + links.core(send_dn2).astype(f32)
    send_out = down_tokens(hids, wds, t, t, bf16)
    output = (residual + down_tokens(hids, wds, 0, t, f32) + links.core(send_out).astype(f32)).astype(bf16)

    upstream = cotangent.astype(f32)
    grad_from_two, grad_gain_ffn = norm_back(residual, inverse_two, gain_ffn, grad_normed_two)
    grad_residual = upstream + grad_from_two
    grad_attn_low = grad_residual.astype(bf16)

    def product_right_t(left, right):
        return lax.dot_general(left, right, (((1,), (1,)), ((), ())), preferred_element_type=f32)

    def product_left_t(left, right):
        return lax.dot_general(left, right, (((0,), (0,)), ((), ())), preferred_element_type=f32)

    def owned(full):
        quarters = full.reshape(2, 2, own, full.shape[1])
        pick = lambda v, n, axis: lax.dynamic_index_in_dim(v, n, axis, keepdims=False)
        pair = pick(quarters, c, 1) + links.core(pick(quarters, 1 - c, 1))
        rows = pick(pair, x, 0) + links.across(pick(pair, 1 - x, 0))
        return links.in_order(*links.replica_sum(rows, 0), 0).astype(f32)

    grad_w_output = owned(product_left_t(mixed_low, grad_attn_low).astype(bf16))
    grad_mixed = product_right_t(grad_attn_low, full_output).astype(bf16)
    scaled_mixed = (grad_mixed.astype(f32) * inverse_sums).astype(bf16)
    cos_lanes = jnp.tile(cosine, (1, 4))
    sin_lanes = jnp.tile(jnp.concatenate([-sine, sine], 1), (1, 2))
    d_query, d_key, d_value = attend_back(queries, scaled_mixed, mixed_low, kx, vz, cos_lanes, sin_lanes, probs)
    d_qkv = jnp.concatenate([d_query, d_key, d_value], 1)
    grad_qkv = owned(product_left_t(normed_low, d_qkv).astype(bf16))
    grad_biases = jnp.sum(d_qkv.astype(f32), axis=0)
    grad_normed = product_right_t(d_qkv, full_qkv)
    grad_from_one, grad_gain_attn = norm_back(inputs, inverse_one, gain_attn, grad_normed)
    grad_tokens = grad_residual + grad_from_one

    small = links.everywhere(jnp.concatenate([grad_gain_attn, grad_gain_ffn, grad_biases])[None, :])[0]

    def assembled(which):
        columns = []
        for s in range(4):
            side, core = s // 2, s % 2
            for (mine, other), w in zip(gate_up, widths):
                piece = jnp.where(c == core, mine[which], other[which])
                columns.append(piece[:, side * w : (side + 1) * w])
        return jnp.concatenate(columns, 1).astype(f32)

    return (
        output,
        grad_tokens,
        small[:d],
        small[d : 2 * d],
        grad_qkv[:, :qw],
        small[2 * d : 2 * d + qw],
        grad_qkv[:, qw : qw + kw],
        small[2 * d + qw : 2 * d + qw + kw],
        grad_qkv[:, qw + kw :],
        small[2 * d + qw + kw :],
        grad_w_output,
        assembled(0),
        assembled(1),
        jnp.concatenate(downs, 0).astype(f32),
    )


def solution(mesh):
    tokens, rows, whole = P(("shard", "replica"), None), P("shard", None), P()
    return jax.shard_map(
        functools.partial(on_device, (mesh.shape["shard"], mesh.shape["replica"])),
        mesh=mesh,
        in_specs=(tokens, tokens, tokens, whole, whole, rows, whole, rows, whole, rows, whole, rows, rows, rows, rows),
        out_specs=(tokens, tokens, whole, whole, rows, whole, rows, whole, rows, whole, rows, rows, rows, rows),
        check_vma=False,
    )
```

```python
import functools

import jax
import jax.numpy as jnp
from jax import lax
from jax.experimental import pallas as pl
from jax.experimental.pallas import tpu as pltpu
from jax.sharding import PartitionSpec as P

HEADS, KVHEADS, HD = 14, 2, 64
GROUP = HEADS // KVHEADS
PAIRS = HEADS // 2
TILE = 256
BLK = 256
VMEM_CAP = 63 << 20
bf16, f32 = jnp.bfloat16, jnp.float32
epsilon = 1e-06
rope_base = 1000000.0


def nn(a, b):
    return lax.dot_general(a, b, (((1,), (0,)), ((), ())), preferred_element_type=f32)


def nt(a, b):
    return lax.dot_general(a, b, (((1,), (1,)), ((), ())), preferred_element_type=f32)


def tn(a, b):
    return lax.dot_general(a, b, (((0,), (0,)), ((), ())), preferred_element_type=f32)


def shaped(shape, dtype=bf16):
    return jax.ShapeDtypeStruct(shape, dtype)


def fixed(shape):
    return pl.BlockSpec(shape, lambda i: (0,) * len(shape))


def by_rows(rows, columns, first=0):
    return pl.BlockSpec((rows, columns), lambda i: (i + first, 0))


SCALARS = pl.BlockSpec(memory_space=pltpu.SMEM)
X, CORE, Y, Z = range(4)


FLOPS_PER_US = 500 * 10**6


class Order:
    def __init__(self):
        self.due = []

    def wait(self, *arrays):
        self.due += arrays


def call(order, body, name, us, grid, ins, outs, scratch=(), aliases=()):
    after = order.due
    n = len(after)

    def kernel(*refs):
        body(*refs[n:])

    result = pl.pallas_call(
        kernel,
        grid=(grid,),
        in_specs=[pl.BlockSpec(memory_space=pl.ANY)] * n + [s for _, s in ins],
        out_specs=[s for _, s in outs],
        out_shape=[s for s, _ in outs],
        scratch_shapes=list(scratch),
        input_output_aliases={n + a: b for a, b in aliases},
        compiler_params=pltpu.CompilerParams(vmem_limit_bytes=VMEM_CAP),
        cost_estimate=pl.CostEstimate(flops=int(us * FLOPS_PER_US), bytes_accessed=10**5, transcendentals=0),
        name=name,
    )(*after, *[a for a, _ in ins])
    order.due = [result[0]]
    return result


def gate(order, v):
    anywhere = pl.BlockSpec(memory_space=pl.ANY)

    def body(v, out):
        pass

    return call(order, body, "gate", 1, 1, [(v, anywhere)], [(shaped(v.shape, v.dtype), anywhere)], (), [(0, 0)])[0]


def widths_of(rows):
    if rows == 1216:
        return [(256, 0), (384, 256), (384, 640), (192, 1024)]
    cuts, at = [], 0
    while at < rows:
        w = min(256, rows - at)
        cuts.append((w, at))
        at += w
    return cuts


def split_weights(order, where, w_gate, w_up, w_down, cuts):
    own, d = w_gate.shape[0], w_down.shape[1]
    ff = w_down.shape[0]
    n = len(cuts)

    def body(where, gate, up, down, *refs):
        sends, mine, downs = refs[: 2 * n], refs[2 * n : 3 * n], refs[3 * n :]

        def put(targets, core, cut):
            w, off = cut
            for src, (ref, start) in zip((gate, up), targets):
                for side in (0, 1):
                    a = (2 * side + core) * ff + off
                    ref[:, start + side * w : start + side * w + w] = src[:, a : a + w]

        for core in (0, 1):

            @pl.when(where[CORE] == core)
            def _():
                for k, (cut, ref) in enumerate(zip(cuts, mine)):
                    put(((ref, 0), (ref, 2 * cut[0])), core, cut)
                    put(((sends[2 * k], 0), (sends[2 * k + 1], 0)), 1 - core, cut)

        for (w, off), part in zip(cuts, downs):
            for lo in range(0, w, 128):
                hi = min(lo + 128, w)
                part[:, lo:hi] = down[off + lo : off + hi, :].T

    whole = lambda a: (a, fixed(a.shape))
    return call(
        order,
        body,
        "split_weights",
        2 + 2 * n,
        1,
        [(where, SCALARS)] + [whole(a) for a in (w_gate, w_up, w_down)],
        [(shaped((own, 2 * w)), fixed((own, 2 * w))) for w, _ in cuts for _ in (0, 1)]
        + [(shaped((own, 4 * w)), fixed((own, 4 * w))) for w, _ in cuts]
        + [(shaped((d, w)), fixed((d, w))) for w, _ in cuts],
    )


def pack_weights(order, where, core_rows, mine, downs, groups, extra=()):
    own = mine[0].shape[0]
    widths = [m.shape[1] // 4 for m in mine]
    n = len(mine)

    def body(where, *refs):
        cores, refs = refs[: 2 * n], refs[2 * n :]
        mine, downs, extras, outs = refs[:n], refs[n : 2 * n], refs[2 * n : 2 * n + len(extra)], refs[2 * n + len(extra) :]
        for group, out in zip(groups, outs):
            at6 = 0
            for k in group:
                w = widths[k]

                @pl.when(where[CORE] == where[Y])
                def _():
                    out[:, at6 : at6 + 4 * w] = mine[k][...]

                @pl.when(where[CORE] != where[Y])
                def _():
                    out[:, at6 : at6 + 2 * w] = cores[2 * k][...]
                    out[:, at6 + 2 * w : at6 + 4 * w] = cores[2 * k + 1][...]

                for h in (0, 1):
                    rows = pl.ds(pl.multiple_of((2 * where[Y] + h) * own, 16), own)
                    out[:, at6 + (4 + h) * w : at6 + (5 + h) * w] = downs[k][rows, :]
                at6 += 6 * w
        if extras:
            outs[-1][:own, :] = extras[0][...]
            outs[-1][own:, :] = extras[1][...]

    whole = lambda a: (a, fixed(a.shape))
    totals = [sum(6 * widths[k] for k in group) for group in groups]
    return call(
        order,
        body,
        "pack_weights",
        2 + n,
        1,
        [(where, SCALARS)] + [whole(a) for a in (*core_rows, *mine, *downs, *extra)],
        [(shaped((own, m)), fixed((own, m))) for m in totals]
        + [(shaped((2 * own, e.shape[1])), fixed((2 * own, e.shape[1]))) for e in extra[:1]],
    )


def place_rows(where, refs, rows, target):
    x, c = where[0], where[1]
    for ref, s in zip(refs, (2 * x + c, 2 * (1 - x) + c, 2 * x + 1 - c, 2 * (1 - x) + 1 - c)):
        target[pl.ds(pl.multiple_of(s * rows, 16), rows), :] = ref


def project(order, where, tokens, gain, own_w, across_w, core_w, far_w, bias, cos, sin):
    t, d = tokens.shape
    rows, width = own_w.shape
    kw = KVHEADS * HD
    qw = width - 2 * kw

    def body(where, tokens, gain, own_w, across_w, core_w, far_w, bias, cos, sin, normed, q, kx, vx, vz, w):
        @pl.when(pl.program_id(0) == 0)
        def _():
            place_rows(where, (own_w[...], across_w[...], core_w[...], far_w[...]), rows, w)

        v = tokens[...].astype(f32)
        inverse = lax.rsqrt(jnp.mean(v * v, axis=-1, keepdims=True) + epsilon)
        n = (v * inverse * gain[...]).astype(bf16)
        normed[...] = n
        lanes = lax.broadcasted_iota(jnp.int32, (TILE, 2 * HD), 1)
        left = lanes < HD
        c, s = cos[...], sin[...]
        for p in range(width // 128):
            at = slice(p * 128, p * 128 + 128)
            u = nn(n, w[:, at]) + bias[:, at]
            if p * 128 < qw + kw:
                u = (u * c + swap_halves(u, lanes) * s).astype(bf16)
            if p * 128 < qw:
                q[:, at] = (u.astype(f32) * 0.125).astype(bf16)
                continue
            u = u.astype(f32)
            turned = pltpu.roll(u, HD, 1)
            first, second = (kx, 0.0), (vx, 1.0)
            for ref, fill in (first,) if p * 128 < qw + kw else (second, (vz, 0.0)):
                ref[0] = jnp.where(left, u, fill).astype(bf16)
                ref[1] = jnp.where(left, fill, turned).astype(bf16)
                ref[2] = jnp.where(left, turned, fill).astype(bf16)
                ref[3] = jnp.where(left, fill, u).astype(bf16)

    heads = (shaped((4, t, 2 * HD)), pl.BlockSpec((4, TILE, 2 * HD), lambda i: (0, i, 0)))
    return call(
        order,
        body,
        "project",
        10,
        t // TILE,
        [
            (where, SCALARS),
            (tokens, by_rows(TILE, d)),
            (gain, fixed(gain.shape)),
            (own_w, fixed(own_w.shape)),
            (across_w, fixed(across_w.shape)),
            (core_w, fixed(core_w.shape)),
            (far_w, fixed(far_w.shape)),
            (bias, fixed(bias.shape)),
            (cos, by_rows(TILE, 2 * HD)),
            (sin, by_rows(TILE, 2 * HD)),
        ],
        [
            (shaped((t, d)), by_rows(TILE, d)),
            (shaped((t, qw)), by_rows(TILE, qw)),
            heads,
            heads,
            heads,
            (shaped((d, width)), fixed((d, width))),
        ],
    )


def swap_halves(v, lanes):
    half = HD // 2
    return jnp.where(lanes % HD < half, pltpu.roll(v, v.shape[1] - half, 1), pltpu.roll(v, half, 1))


def kinds_of(pair):
    return [2 * (2 * pair + side >= GROUP).astype(jnp.int32) + side for side in (0, 1)]


def attend(order, segments, q, kx, vx, first, last):
    t = q.shape[0]
    tiles = t // TILE

    def body(segc, segr, q, kx, vx, o, o_rest, linv, *rest):
        probs, bias = rest[:tiles], rest[tiles]
        step = pl.program_id(0)
        pair = step + first

        @pl.when(step == 0)
        def _():
            for i in range(tiles):
                w = (i + 1) * TILE
                rows = lax.broadcasted_iota(jnp.int32, (TILE, w), 0) + i * TILE
                cols = lax.broadcasted_iota(jnp.int32, (TILE, w), 1)
                ok = (segc[i * TILE : w, :] == segr[:, :w]) & (cols <= rows)
                bias[i * TILE : w, :w] = jnp.where(ok, 0.0, -1e30)

        left = lax.broadcasted_iota(jnp.int32, (TILE, 2 * HD), 1) < HD
        kinds = kinds_of(pair)
        for i in range(tiles):
            w = (i + 1) * TILE
            block = q[i * TILE : w, :]
            mixed = []
            for side in (0, 1):
                s = nt(block, kx[kinds[side], :w, :]) + bias[i * TILE : w, :w]
                e = jnp.exp(s - jnp.max(s, axis=-1, keepdims=True)).astype(bf16)
                for j in range(i + 1):
                    probs[j][side, (i - j) * TILE : (i - j + 1) * TILE, :] = e[:, j * TILE : (j + 1) * TILE]
                mixed.append(nn(e, vx[kinds[side], :w, :]))
            totals = jnp.where(left, pltpu.roll(mixed[0], HD, 1), pltpu.roll(mixed[1], HD, 1))
            inverse = 1.0 / totals
            out = jnp.where(left, mixed[0], mixed[1]) * inverse
            low = out.astype(bf16)
            o[i * TILE : w, :] = low
            o_rest[i * TILE : w, :] = (out - low.astype(f32)).astype(bf16)
            linv[i * TILE : w, :] = inverse

    count = last - first
    lane = pl.BlockSpec((t, 2 * HD), lambda p: (0, p + first))
    out_lane = pl.BlockSpec((t, 2 * HD), lambda p: (0, p))
    out = (t, count * 2 * HD)
    pshape = [(2 * count, t - j * TILE, TILE) for j in range(tiles)]
    return call(
        order,
        body,
        "attend",
        4 * count,
        count,
        [
            (segments.reshape(t, 1), fixed((t, 1))),
            (segments.reshape(1, t), fixed((1, t))),
            (q, lane),
            (kx, fixed(kx.shape)),
            (vx, fixed(vx.shape)),
        ],
        [(shaped(out), out_lane), (shaped(out), out_lane), (shaped(out, f32), out_lane)]
        + [(shaped(s), pl.BlockSpec((2,) + s[1:], lambda p: (p, 0, 0))) for s in pshape],
        [pltpu.VMEM((t, t), f32)],
    )


def attend_back(order, q, do, o, o_rest, kx, vz, cos, sin, probs, first, last, running=()):
    t = q.shape[0]
    tiles = t // TILE
    count = last - first

    def body(q, do, o, o_rest, kx, vz, cos, sin, *rest):
        probs, rest = rest[:tiles], rest[tiles:]
        if running:
            dk_in, dv_in, rest = rest[0], rest[1], rest[2:]
        dq, dk, dv, ds0, ds1, dkacc, dvacc = rest
        step = pl.program_id(0)
        pair = step + first

        @pl.when(step == 0)
        def _():
            if running:
                dkacc[...] = dk_in[...]
                dvacc[...] = dv_in[...]
            else:
                dkacc[...] = jnp.zeros_like(dkacc)
                dvacc[...] = jnp.zeros_like(dvacc)

        left = lax.broadcasted_iota(jnp.int32, (t, 2 * HD), 1) < HD
        along = do[...].astype(f32) * (o[...].astype(f32) + o_rest[...].astype(f32))
        inner = [
            jnp.sum(jnp.where(left, along, 0.0), axis=-1, keepdims=True),
            jnp.sum(jnp.where(left, 0.0, along), axis=-1, keepdims=True),
        ]
        kinds = kinds_of(pair)
        for side, ds in ((0, ds0), (1, ds1)):
            kind = kinds[side]
            for j in range(tiles):
                lo = j * TILE
                p = probs[j][side]
                dp = nt(do[lo:, :], vz[kind, lo : lo + TILE, :])
                d = (p.astype(f32) * (dp - inner[side][lo:])).astype(bf16)
                ds[lo:, lo : lo + TILE] = d
                dkacc[kind, lo : lo + TILE, :] += tn(d, q[lo:, :])
                dvacc[kind, lo : lo + TILE, :] += tn(p, do[lo:, :])
        lanes = lax.broadcasted_iota(jnp.int32, (TILE, 2 * HD), 1)
        for i in range(tiles):
            w = (i + 1) * TILE
            at = slice(i * TILE, w)
            g = (nn(ds0[at, :w], kx[kinds[0], :w, :]) + nn(ds1[at, :w], kx[kinds[1], :w, :])) * 0.125
            dq[at, :] = (g * cos[at, :] - swap_halves(g, lanes) * sin[at, :]).astype(bf16)

        @pl.when(step == count - 1)
        def _():
            if not running:
                dk[...] = dkacc[...]
                dv[...] = dvacc[...]
                return
            lanes = lax.broadcasted_iota(jnp.int32, (t, 2 * HD), 1)
            one = lambda a: jnp.where(left, a[0] + pltpu.roll(a[1], HD, 1), pltpu.roll(a[2], HD, 1) + a[3])
            g = one(dkacc)
            dk[...] = (g * cos[...] - swap_halves(g, lanes) * sin[...]).astype(bf16)
            dv[...] = one(dvacc).astype(bf16)

    lane = pl.BlockSpec((t, 2 * HD), lambda p: (0, p + first))
    out_lane = pl.BlockSpec((t, 2 * HD), lambda p: (0, p))
    wide = (4, t, 2 * HD)
    sums = (shaped((t, 2 * HD)), fixed((t, 2 * HD))) if running else (shaped(wide, f32), fixed(wide))
    return call(
        order,
        body,
        "attend_back",
        6 * count,
        count,
        [(q, lane), (do, out_lane), (o, out_lane), (o_rest, out_lane), (kx, fixed(wide)), (vz, fixed(wide))]
        + [(cos, fixed(cos.shape)), (sin, fixed(sin.shape))]
        + [(p, pl.BlockSpec((2,) + p.shape[1:], lambda i: (i, 0, 0))) for p in probs]
        + [(r, fixed(wide)) for r in running],
        [(shaped((t, count * 2 * HD)), out_lane), sums, sums],
        [pltpu.VMEM((t, t), bf16)] * 2 + [pltpu.VMEM(wide, f32)] * 2,
    )


def join_output(order, where, tokens, mixed, own_w, across, core, gain):
    t, d = tokens.shape
    rows = own_w.shape[0]
    n = len(mixed)

    def body(where, tokens, own_w, across, core, gain, *refs):
        mixed, (resid, normed, w) = refs[:n], refs[n:]

        @pl.when(pl.program_id(0) == 0)
        def _():
            place_rows(where, (own_w[...], across[:rows, :], core[...], across[rows:, :]), rows, w)

        v, lo = tokens[...].astype(f32), 0
        for m in mixed:
            v = v + nn(m[...], w[lo : lo + m.shape[1], :])
            lo += m.shape[1]
        resid[...] = v
        inverse = lax.rsqrt(jnp.mean(v * v, axis=-1, keepdims=True) + epsilon)
        normed[...] = (v * inverse * gain[...]).astype(bf16)

    return call(
        order,
        body,
        "join_output",
        7,
        t // TILE,
        [(where, SCALARS), (tokens, by_rows(TILE, d))]
        + [(a, fixed(a.shape)) for a in (own_w, across, core, gain)]
        + [(m, by_rows(TILE, m.shape[1])) for m in mixed],
        [
            (shaped((t, d), f32), by_rows(TILE, d)),
            (shaped((t, d)), by_rows(TILE, d)),
            (shaped((4 * rows, d)), fixed((4 * rows, d))),
        ],
    )


def ffn_part(order, where, n2, dy, mine, core_rows, x_rows, y_rows, down, cut, at6, tt=512):
    t, d = n2[0].shape
    w, off = cut
    own = mine.shape[0]
    half = d // 2
    steps = t // tt

    def body(where, n2a, n2b, dya, dyb, mine, core_gate, core_up, x_rows, y_rows, down, hid, dgu, keep, send, wt, acc):
        step = pl.program_id(0)
        x, c, y = where[0], where[1], where[2]

        @pl.when(step == 0)
        def _():
            def put(ref, s, at=at6):
                wt[pl.ds(pl.multiple_of(s * own, 16), own), : 4 * w] = ref[:, at : at + 4 * w]

            put(mine, 2 * x + c, 0)
            other = pl.ds(pl.multiple_of((2 * x + 1 - c) * own, 16), own)
            wt[other, : 2 * w] = core_gate[...]
            wt[other, 2 * w : 4 * w] = core_up[...]
            put(x_rows, 2 * (1 - x) + y)
            put(y_rows, 2 * (1 - x) + 1 - y)
            for side in (0, 1):

                @pl.when(x == side)
                def _():
                    wt[:, (4 + side) * w : (5 + side) * w] = down[...]
                    lo = (5 - side) * w
                    for ref, h in ((x_rows, y), (y_rows, 1 - y)):
                        for part in (0, 1):
                            at = pl.ds(pl.multiple_of((2 * h + part) * own, 16), own)
                            wt[at, lo : lo + w] = ref[:, at6 + (4 + part) * w : at6 + (5 + part) * w]

            acc[...] = jnp.zeros_like(acc)

        first = step < steps
        a = jnp.where(first, n2a[...], n2b[...])
        b = jnp.where(first, dya[...], dyb[...])
        for lo in range(0, 2 * w, BLK):
            hi = min(lo + BLK, 2 * w)
            g, u, v = slice(lo, hi), slice(2 * w + lo, 2 * w + hi), slice(4 * w + lo, 4 * w + hi)
            gate, up, dh = nn(a, wt[:, g]), nn(a, wt[:, u]), nn(b, wt[:, v])
            sig = jax.nn.sigmoid(gate)
            silu = gate * sig
            h = (silu * up).astype(bf16)
            d_gate = (dh * up * (sig + silu * (1.0 - sig))).astype(bf16)
            d_up = (dh * silu).astype(bf16)
            hid[:, g] = h
            dgu[:, g] = d_gate
            dgu[:, u] = d_up
            acc[:, v] += tn(b, h)
            acc[:, g] += tn(a, d_gate)
            acc[:, u] += tn(a, d_up)

        @pl.when(step == 2 * steps - 1)
        def _():
            for ref, side in ((keep, x), (send, 1 - x)):
                at = pl.ds(pl.multiple_of(side * half, 16), half)
                ref[:, : 4 * w] = acc[at, : 4 * w].astype(bf16)
            for side in (0, 1):

                @pl.when(x == side)
                def _():
                    for ref, s in ((keep, side), (send, 1 - side)):
                        lanes = slice((4 + s) * w, (5 + s) * w)
                        ref[:, 4 * w : 5 * w] = acc[:half, lanes].astype(bf16)
                        ref[:, 5 * w :] = acc[half:, lanes].astype(bf16)

    whole = lambda a: (a, fixed(a.shape))
    early = pl.BlockSpec((tt, d), lambda i: (jnp.minimum(i, steps - 1), 0))
    late = pl.BlockSpec((tt, d), lambda i: (jnp.maximum(i - steps, 0), 0))
    return call(
        order,
        body,
        "ffn_part",
        5 + w // 16,
        2 * steps,
        [(where, SCALARS), (n2[0], early), (n2[1], late), (dy[0], early), (dy[1], late)]
        + [whole(a) for a in (mine, *core_rows, x_rows, y_rows, down)],
        [
            (shaped((2 * t, 2 * w)), by_rows(tt, 2 * w)),
            (shaped((2 * t, 4 * w)), by_rows(tt, 4 * w)),
            (shaped((half, 6 * w)), fixed((half, 6 * w))),
            (shaped((half, 6 * w)), fixed((half, 6 * w))),
            (shaped((d, 6 * w)), fixed((d, 6 * w))),
        ],
        [pltpu.VMEM((d, 6 * w), f32)],
    )


def sum_parts(order, name, us, parts, weights, lanes, block, tokens, apart=False, tt=256):
    d = weights[0].shape[0]
    t = parts[0].shape[0] // 2
    n = len(parts)
    steps = t // tt
    k = len(tokens)

    def body(*refs):
        step = pl.program_id(0)
        total = None
        for part, weight in zip(refs[:n], refs[n : 2 * n]):
            s = nt(part[...], weight[...])
            total = s if total is None else total + s
        for out, (first, count, _) in zip(refs[2 * n :], outs):

            @pl.when((step >= first) & (step < first + count))
            def _():
                out[...] = total.astype(out.dtype)

    def spec(first, count):
        return pl.BlockSpec((tt, d), lambda i: (jnp.clip(i - first, 0, count - 1), 0))

    outs = []
    for at, half in enumerate(tokens):
        if half and apart:
            outs += [(at * steps + k, 1, bf16) for k in range(steps)]
        else:
            outs.append((at * steps, steps, bf16 if half else f32))

    start = tokens[0] * steps
    return call(
        order,
        body,
        name,
        us,
        k * steps,
        [(p, pl.BlockSpec((tt, p.shape[1]), lambda i: ((i + start) % (2 * steps), 0))) for p in parts]
        + [(w, pl.BlockSpec((d, n), lambda i: (0, block))) for w, n in zip(weights, lanes)],
        [(shaped((count * tt, d), kind), spec(first, count)) for first, count, kind in outs],
    )


def turn_back(order, dn2, dn2_other, residual, cotangent, gain, full_output, inverse_sums):
    t, d = residual.shape
    n = len(inverse_sums)

    steps = len(dn2_other)

    def body(dn2, resid, dy, gain, w, *refs):
        others, refs = refs[:steps], refs[steps:]
        sums, (d_resid, d_attn, grad_gain), scaled, other = refs[:n], refs[n : n + 3], refs[n + 3 : -1], refs[-1]
        step = pl.program_id(0)
        for k, ref in enumerate(others):

            @pl.when(step == k)
            def _():
                other[...] = ref[...]

        @pl.when(step == 0)
        def _():
            grad_gain[...] = jnp.zeros_like(grad_gain)

        up = dn2[...] + other[...].astype(f32)
        grad, gains = norm_back(resid[...], gain[...], up)
        grad_gain[...] += gains
        total = dy[...].astype(f32) + grad
        d_resid[...] = total
        low = total.astype(bf16)
        d_attn[...] = low
        d_mixed = nt(low, w[...]).astype(bf16).astype(f32)
        lo = 0
        for linv, out in zip(sums, scaled):
            hi = lo + linv.shape[1]
            out[...] = (d_mixed[:, lo:hi] * linv[...]).astype(bf16)
            lo = hi

    rows = by_rows(TILE, d)
    return call(
        order,
        body,
        "turn_back",
        8,
        steps,
        [(a, rows) for a in (dn2, residual, cotangent)]
        + [(gain, fixed(gain.shape)), (full_output, fixed(full_output.shape))]
        + [(a, fixed(a.shape)) for a in dn2_other]
        + [(a, by_rows(TILE, a.shape[1])) for a in inverse_sums],
        [(shaped((t, d), f32), rows), (shaped((t, d)), rows), (shaped((1, d), f32), fixed((1, d)))]
        + [(shaped((t, a.shape[1])), by_rows(TILE, a.shape[1])) for a in inverse_sums],
        [pltpu.VMEM((TILE, d), bf16)],
    )


def weight_grads(order, where, us, pairs):
    d = sum(a.shape[1] for a in pairs[0][0])
    width = sum(g.shape[1] for _, g in pairs)
    own = d // 4
    lefts = []
    for pieces, _ in pairs:
        lefts += [a for a in pieces if not any(a is b for b in lefts)]
    rights = [g for _, g in pairs]
    place = [[next(i for i, b in enumerate(lefts) if b is a) for a in pieces] for pieces, _ in pairs]

    def body(where, *refs):
        left, right, (keep, send) = refs[: len(lefts)], refs[len(lefts) : -2], refs[-2:]
        c = where[CORE]
        lo = 0
        for spots, g in zip(place, right):
            hi = lo + g.shape[1]
            grad = jnp.concatenate([tn(left[i][...], g[...]).astype(bf16) for i in spots], 0)
            for core in (0, 1):
                rows = jnp.concatenate([grad[core * own : (core + 1) * own], grad[(2 + core) * own : (3 + core) * own]], 0)

                @pl.when(c == core)
                def _():
                    keep[:, lo:hi] = rows

                @pl.when(c != core)
                def _():
                    send[:, lo:hi] = rows

            lo = hi

    out = (shaped((2 * own, width)), fixed((2 * own, width)))
    return call(
        order, body, "weight_grads", us, 1, [(where, SCALARS)] + [(a, fixed(a.shape)) for a in (*lefts, *rights)], [out, out]
    )


def finish_tokens(order, tokens, gain, d_parts, full_qkv, d_resid):
    t, d = tokens.shape
    n = len(d_parts)
    width = full_qkv.shape[1]

    def body(tokens, gain, w, d_resid, *refs):
        parts, out, grad_gain, sums = refs[:n], refs[n], refs[n + 1], refs[n + 2]

        @pl.when(pl.program_id(0) == 0)
        def _():
            grad_gain[...] = jnp.zeros_like(grad_gain)
            sums[...] = jnp.zeros_like(sums)

        total, lo = None, 0
        for part in parts:
            hi = lo + part.shape[1]
            p = part[...]
            sums[:, lo:hi] += jnp.sum(p.astype(f32), axis=0, keepdims=True)
            s = nt(p, w[:, lo:hi])
            total = s if total is None else total + s
            lo = hi
        grad, gains = norm_back(tokens[...].astype(f32), gain[...], total)
        grad_gain[...] += gains
        out[...] = d_resid[...] + grad

    rows = by_rows(TILE, d)
    return call(
        order,
        body,
        "finish_tokens",
        8,
        t // TILE,
        [(tokens, rows), (gain, fixed(gain.shape)), (full_qkv, fixed(full_qkv.shape)), (d_resid, rows)]
        + [(p, by_rows(TILE, p.shape[1])) for p in d_parts],
        [(shaped((t, d), f32), rows), (shaped((1, d), f32), fixed((1, d))), (shaped((1, width), f32), fixed((1, width)))],
    )


def assemble(order, where, halves, others, cores, cuts, ff):
    own = halves[0].shape[0]
    d = 4 * own
    n = len(cuts)
    steps = d // 128
    block = own // steps

    def body(where, *refs):
        halves, others, cores = refs[:n], refs[n : 2 * n], refs[2 * n : 3 * n]
        gate, up, down, down_t = refs[3 * n :]
        step = pl.program_id(0)
        c, y = where[1], where[2]
        rows = pl.ds(pl.multiple_of(step * block, 16), block)

        @pl.when(step == 0)
        def _():
            for (w, off), a, b in zip(cuts, halves, others):
                for ref, h in ((a, y), (b, 1 - y)):
                    for part in (0, 1):
                        at = pl.ds(pl.multiple_of((2 * part + h) * own, 16), own)
                        down_t[at, off : off + w] = ref[:, (4 + part) * w : (5 + part) * w]

        for core in (0, 1):
            for (w, off), a, b, o in zip(cuts, halves, others, cores):

                def put(ref, to):
                    for m, out in enumerate((gate, up)):
                        for side in (0, 1):
                            at = (2 * side + to) * ff + off
                            lo = (2 * m + side) * w
                            out[:, at : at + w] = ref[rows, lo : lo + w].astype(f32)

                @pl.when((c == core) & (c == y))
                def _():
                    put(a, core)

                @pl.when((c == core) & (c != y))
                def _():
                    put(b, core)

                @pl.when(c != core)
                def _():
                    put(o, core)

        down[...] = down_t[pl.ds(pl.multiple_of(step * 128, 128), 128), :].astype(f32).T

    whole = lambda a: (a, fixed(a.shape))
    return call(
        order,
        body,
        "assemble",
        11,
        steps,
        [(where, SCALARS)] + [whole(a) for a in (*halves, *others, *cores)],
        [
            (shaped((own, 4 * ff), f32), by_rows(block, 4 * ff)),
            (shaped((own, 4 * ff), f32), by_rows(block, 4 * ff)),
            (shaped((ff, d), f32), pl.BlockSpec((ff, 128), lambda i: (0, i))),
        ],
        [pltpu.VMEM((d, ff), bf16)],
    )


class Links:
    def __init__(self, shards, replicas):
        self.shards, self.replicas = shards, replicas
        s, r = lax.axis_index("shard"), lax.axis_index("replica")
        self.where = jnp.stack([s // 2, s % 2, r % 2, r // 2 % 2]).astype(jnp.int32)

    def core(self, v):
        return lax.ppermute(v, "shard", [(i, i ^ 1) for i in range(self.shards)])

    def across(self, v):
        return lax.ppermute(v, "shard", [(i, i ^ 2) for i in range(self.shards)])

    def beside(self, v):
        return lax.ppermute(v, "replica", [(i, i ^ 1) for i in range(self.replicas)])

    def far(self, v, bit):
        return lax.ppermute(v, "replica", [(i, i ^ bit) for i in range(self.replicas)])

    def along(self, v):
        return lax.psum(v, "replica", axis_index_groups=[list(range(y, self.replicas, 2)) for y in (0, 1)])

    def bits(self):
        bit = 2
        while bit < self.replicas:
            yield bit
            bit *= 2


def split_sum(axis, keep, got):
    half = keep.shape[0] // 2
    shape = shaped((half, keep.shape[1]), keep.dtype)

    def body(where, keep, got, mine, send):
        n = where[axis]
        for ref, h in ((mine, n), (send, 1 - n)):
            at = pl.ds(pl.multiple_of(h * half, 16), half)
            ref[...] = (keep[at, :].astype(f32) + got[at, :].astype(f32)).astype(ref.dtype)

    return body, [(keep, fixed(keep.shape)), (got, fixed(got.shape))], [shape, shape]


def whole_sum(v, got):
    def body(where, v, got, out):
        out[...] = (v[...].astype(f32) + got[...].astype(f32)).astype(out.dtype)

    return body, [(v, fixed(v.shape)), (got, fixed(got.shape))], [shaped(v.shape, v.dtype)]


def in_order(axis, mine, other, dtype=bf16):
    rows, width = mine.shape

    def body(where, mine, other, out):
        n = where[axis]
        out[pl.ds(pl.multiple_of(n * rows, 16), rows), :] = mine[...].astype(dtype)
        out[pl.ds(pl.multiple_of((1 - n) * rows, 16), rows), :] = other[...].astype(dtype)

    return body, [(mine, fixed(mine.shape)), (other, fixed(other.shape))], [shaped((2 * rows, width), dtype)]


def rows_for_core(half, other, lanes):
    spec = fixed((half.shape[0], lanes))

    def body(where, half, other, out):
        same = where[CORE] == where[Y]

        @pl.when(same)
        def _():
            out[...] = other[...]

        @pl.when(jnp.logical_not(same))
        def _():
            out[...] = half[...]

    return body, [(half, spec), (other, spec)], [shaped((half.shape[0], lanes))]


GATE = "gate"


def advance(order, where, chains):
    chains = [chain for chain in chains if chain.asked is not None]
    for chain in [chain for chain in chains if chain.asked[0] == GATE]:
        chains.remove(chain)
        chain.give([gate(order, chain.asked[1])])
    if not chains:
        return
    asked = [chain.asked for chain in chains]
    n_in = sum(len(ins) for _, ins, _ in asked)

    def body(where, *refs):
        ins, outs = refs[:n_in], refs[n_in:]
        for part, i, o in asked:
            part(where, *ins[: len(i)], *outs[: len(o)])
            ins, outs = ins[len(i) :], outs[len(o) :]

    results = call(
        order,
        body,
        "sums",
        2,
        1,
        [(where, SCALARS)] + [pair for _, i, _ in asked for pair in i],
        [(shape, fixed(shape.shape)) for _, _, o in asked for shape in o],
    )
    for chain, (_, _, o) in zip(chains, asked):
        chain.give(results[: len(o)])
        results = results[len(o) :]


class Chain:
    def __init__(self, steps):
        self.steps = steps
        self.result = None
        self.asked = next(steps)

    def give(self, results):
        try:
            self.asked = self.steps.send(results)
        except StopIteration as stop:
            self.asked, self.result = None, stop.value


def replica_steps(order, links, mine, send, how):
    bits = list(links.bits())
    if how == "halves" and bits:
        mine, send = yield split_sum(Z, mine, links.beside(send))
        (mine,) = yield whole_sum(mine, links.far(send, bits[0]))
        for bit in bits[1:]:
            (mine,) = yield whole_sum(mine, links.far(mine, bit))
        (mine,) = yield in_order(Z, mine, links.far(mine, bits[0]))
    else:
        (mine,) = yield whole_sum(mine, links.beside(send))
        if how == "offload":
            (mine,) = yield GATE, links.along(mine)
        else:
            for bit in bits:
                (mine,) = yield whole_sum(mine, links.far(mine, bit))
    return mine, links.beside(mine)


def ffn_steps(order, links, keep, send, w, how):
    mine, send = yield split_sum(Y, keep, links.across(send))
    half, other = yield from replica_steps(order, links, mine, send, how)
    (rows,) = yield rows_for_core(half, other, 4 * w)
    return half, other, links.core(rows)


def owned_steps(order, links, keep, send, how):
    mine, send = yield split_sum(X, keep, links.core(send))
    mine, send = yield split_sum(Y, mine, links.across(send))
    half, other = yield from replica_steps(order, links, mine, send, how)
    (rows,) = yield in_order(Y, half, other, f32)
    return rows


def small_steps(links, v):
    for move in (links.core, links.across, links.beside):
        (v,) = yield whole_sum(v, move(v))
    for bit in links.bits():
        (v,) = yield whole_sum(v, links.far(v, bit))
    return v


def norm_back(values, gain_vector, upstream):
    inverse = lax.rsqrt(jnp.mean(values * values, axis=-1, keepdims=True) + epsilon)
    scaled = upstream * gain_vector
    grad_gain = jnp.sum(upstream * values * inverse, axis=0, keepdims=True)
    correction = jnp.sum(scaled * values, axis=-1, keepdims=True) / values.shape[-1]
    return inverse * scaled - values * (inverse * inverse * inverse) * correction, grad_gain


def position_tables(doc_ids):
    t = doc_ids.shape[0]
    earlier = jnp.sum((doc_ids[None, :] < doc_ids[:, None]).astype(jnp.int32), axis=1)
    places = jnp.arange(t, dtype=jnp.int32) - earlier
    frequency = rope_base ** (-jnp.arange(0, HD, 2).astype(f32) / HD)
    angles = places.astype(f32)[:, None] * frequency[None, :]
    cosine, sine = jnp.cos(angles), jnp.sin(angles)
    return jnp.tile(cosine, (1, 4)), jnp.tile(jnp.concatenate([-sine, sine], 1), (1, 2))


def on_device(
    links_shape,
    tokens,
    segments,
    cotangent,
    gain_attn,
    gain_ffn,
    w_query,
    bias_query,
    w_key,
    bias_key,
    w_value,
    bias_value,
    w_output,
    w_gate,
    w_up,
    w_down,
):
    links = Links(*links_shape)
    order = Order()
    where = links.where
    t, d = tokens.shape
    qw, kw = w_query.shape[1], w_key.shape[1]
    doc_ids = segments[0]
    ff = w_down.shape[0]
    cuts = widths_of(ff)
    cos, sin = position_tables(doc_ids)
    gain_attn, gain_ffn = gain_attn[None, :], gain_ffn[None, :]
    pieces = range(len(cuts))
    stages = [[[0]], [[1], list(pieces[2:])]] if len(cuts) > 2 else [[[n] for n in pieces]]
    group_of = [number for number, group in enumerate(g for stage in stages for g in stage) for _ in group]

    own_qkv = jnp.concatenate([w_query, w_key, w_value], 1)
    across_qkv, core_qkv = links.across(own_qkv), links.core(own_qkv)
    dy = (cotangent, links.core(cotangent))
    core_output = links.core(w_output)
    mine, downs, core_rows, at6 = [], [], [], []
    order.wait(cos, sin)
    for number, stage in enumerate(stages):
        chosen = [cuts[n] for group in stage for n in group]
        k = len(chosen)
        parts = split_weights(order, where, w_gate, w_up, w_down, chosen)
        core_rows.append([links.core(v) for v in parts[: 2 * k]])
        mine.append(parts[2 * k : 3 * k])
        downs.append(parts[3 * k :])
        for group in stage:
            at6 += [sum(6 * cuts[m][0] for m in group[:k]) for k in range(len(group))]
        if number == 0:
            across_qkv = gate(order, across_qkv)
            far_qkv = links.core(across_qkv)
    x_rows = []
    for number, stage in enumerate(stages):
        sizes = [len(group) for group in stage]
        local = [list(range(sum(sizes[:k]), sum(sizes[: k + 1]))) for k in range(len(sizes))]
        packed = pack_weights(
            order,
            where,
            core_rows[number],
            mine[number],
            downs[number],
            local,
            [w_output, core_output] if number == 0 else [],
        )
        if number == 0:
            *packed, joined = packed
            across_output = links.across(joined)
        x_rows += [links.across(v) for v in packed]
    mine, downs, core_rows = ([v for part in parts for v in part] for parts in (mine, downs, core_rows))

    bias = jnp.concatenate([bias_query, bias_key, bias_value])[None, :]
    order.wait(dy[1])
    normed, queries, kx, vx, vz, full_qkv = project(
        order, where, tokens, gain_attn, own_qkv, across_qkv, core_qkv, far_qkv, bias, cos, sin
    )
    middle = 3
    y_rows = []

    def forward_rows(*groups):
        for g in groups:
            if g < len(x_rows) and g == len(y_rows):
                x_rows[g] = gate(order, x_rows[g])
                y_rows.append(links.beside(x_rows[g]))

    first_part = attend(order, doc_ids, queries, kx, vx, 0, middle)
    forward_rows(0)
    second_part = attend(order, doc_ids, queries, kx, vx, middle, PAIRS)
    forward_rows(1)
    order.wait(y_rows[0])
    mixed, mixed_rest, inverse_sums = zip(first_part[:3], second_part[:3])
    probs = (first_part[3:], second_part[3:])
    residual, normed_two, full_output = join_output(
        order, where, tokens, mixed, w_output, across_output, core_output, gain_ffn
    )
    n2 = (normed_two, links.core(normed_two))

    chains, hids, dgus, weights = [], [], [], []
    how = ["whole"] * len(cuts)

    def step(*which):
        advance(order, where, [chains[n] for n in which if n < len(chains)])

    for n in pieces:
        g = group_of[n]
        forward_rows(g)
        if n >= 2:
            step(0)
        hid, dgu, keep, send, weight = ffn_part(
            order, where, n2, dy, mine[n], core_rows[2 * n : 2 * n + 2], x_rows[g], y_rows[g], downs[n], cuts[n], at6[n]
        )
        hids.append(hid), dgus.append(dgu), weights.append(weight)
        chains.append(Chain(ffn_steps(order, links, keep, send, cuts[n][0], how[n])))
        if n == 0:
            forward_rows(2)

    step(0, 1)
    *dn2_send, dn2 = sum_parts(order, "back_tokens", 24, dgus, weights, [4 * w for w, _ in cuts], 0, (1, 0), True)
    dn2_other = [links.core(v) for v in dn2_send]
    step(0, 1, 2)
    d_resid, d_attn, grad_gain_ffn, *scaled = turn_back(
        order, dn2, dn2_other, residual, cotangent, gain_ffn, full_output, inverse_sums
    )
    step(0, 1, 3)

    both = [
        (queries, scaled[n], mixed[n], mixed_rest[n], kx, vz, cos, sin, probs[n], *span)
        for n, span in enumerate(((0, middle), (middle, PAIRS)))
    ]
    dq_first, *running = attend_back(order, *both[0], ())
    step(2, 3)
    chains.append(
        Chain(owned_steps(order, links, *weight_grads(order, where, 5, [(mixed, d_attn)]), "whole"))
    )
    out_n = len(chains) - 1
    dq_second, d_key, d_value = attend_back(order, *both[1], running)
    step(1, 2, out_n)
    d_parts = [dq_first, dq_second, d_key, d_value]
    chains.append(
        Chain(owned_steps(order, links, *weight_grads(order, where, 8, [((normed,), p) for p in d_parts]), "whole"))
    )
    qkv_n = out_n + 1
    step(1, 3, out_n, qkv_n)
    grad_tokens, grad_gain_attn, grad_biases = finish_tokens(order, tokens, gain_attn, d_parts, full_qkv, d_resid)
    chains.append(Chain(small_steps(links, jnp.concatenate([grad_gain_attn, grad_gain_ffn, grad_biases], 1))))
    small_n = qkv_n + 1
    step(2, out_n, qkv_n)
    down_lanes = [2 * w for w, _ in cuts]
    (out_send,) = sum_parts(order, "down_tokens", 11, hids, weights, down_lanes, 2, (1,))
    out_other = links.core(out_send)
    step(2, 3, out_n, qkv_n, small_n)
    (out,) = sum_parts(order, "down_tokens", 11, hids, weights, down_lanes, 2, (0,))
    output = (residual + out + out_other.astype(f32)).astype(bf16)
    while any(chain.result is None for chain in chains[: len(cuts)]):
        step(*range(len(chains)))
    grad_gate, grad_up, grad_down = assemble(order, where, *zip(*(chain.result for chain in chains[: len(cuts)])), cuts, ff)
    while any(chain.result is None for chain in chains):
        step(*range(len(chains)))
    grad_output, grad_qkv, small = (chain.result for chain in chains[len(cuts) :])
    small = small[0]
    return (
        output,
        grad_tokens,
        small[:d],
        small[d : 2 * d],
        grad_qkv[:, :qw],
        small[2 * d : 2 * d + qw],
        grad_qkv[:, qw : qw + kw],
        small[2 * d + qw : 2 * d + qw + kw],
        grad_qkv[:, qw + kw :],
        small[2 * d + qw + kw :],
        grad_output,
        grad_gate,
        grad_up,
        grad_down,
    )


def solution(mesh):
    tokens, rows, whole = P(("shard", "replica"), None), P("shard", None), P()
    return jax.shard_map(
        functools.partial(on_device, (mesh.shape["shard"], mesh.shape["replica"])),
        mesh=mesh,
        in_specs=(tokens, tokens, tokens, whole, whole, rows, whole, rows, whole, rows, whole, rows, rows, rows, rows),
        out_specs=(tokens, tokens, whole, whole, rows, whole, rows, whole, rows, whole, rows, rows, rows, rows),
        check_vma=False,
    )
```

```python
import functools

import jax
import jax.numpy as jnp
from jax import lax
from jax.experimental import pallas as pl
from jax.experimental.pallas import tpu as pltpu
from jax.sharding import PartitionSpec as P

HEADS, KVHEADS, HD = 14, 2, 64
GROUP = HEADS // KVHEADS
PAIRS = HEADS // 2
TILE = 256
BLK = 256
VMEM_CAP = (64 << 20) - (1 << 16)
bf16, f32 = jnp.bfloat16, jnp.float32
epsilon = 1e-06
rope_base = 1000000.0


def nn(a, b):
    return lax.dot_general(a, b, (((1,), (0,)), ((), ())), preferred_element_type=f32)


def nt(a, b):
    return lax.dot_general(a, b, (((1,), (1,)), ((), ())), preferred_element_type=f32)


def tn(a, b):
    return lax.dot_general(a, b, (((0,), (0,)), ((), ())), preferred_element_type=f32)


def shaped(shape, dtype=bf16):
    return jax.ShapeDtypeStruct(shape, dtype)


def fixed(shape):
    return pl.BlockSpec(shape, lambda i: (0,) * len(shape))


def by_rows(rows, columns, first=0):
    return pl.BlockSpec((rows, columns), lambda i: (i + first, 0))


SCALARS = pl.BlockSpec(memory_space=pltpu.SMEM)
X, CORE, Y, Z = range(4)


FLOPS_PER_US = 500 * 10**6


class Order:
    def __init__(self):
        self.due = []

    def wait(self, *arrays):
        self.due += arrays


def call(order, body, name, us, grid, ins, outs, scratch=(), aliases=()):
    after = order.due
    n = len(after)

    def kernel(*refs):
        body(*refs[n:])

    result = pl.pallas_call(
        kernel,
        grid=(grid,),
        in_specs=[pl.BlockSpec(memory_space=pl.ANY)] * n + [s for _, s in ins],
        out_specs=[s for _, s in outs],
        out_shape=[s for s, _ in outs],
        scratch_shapes=list(scratch),
        input_output_aliases={n + a: b for a, b in aliases},
        compiler_params=pltpu.CompilerParams(vmem_limit_bytes=VMEM_CAP),
        cost_estimate=pl.CostEstimate(flops=int(us * FLOPS_PER_US), bytes_accessed=10**5, transcendentals=0),
        name=name,
    )(*after, *[a for a, _ in ins])
    order.due = [result[0]]
    return result


def first_lanes(order, v, lanes):
    def body(v, out):
        out[...] = v[...]

    spec = fixed((v.shape[0], lanes))
    return call(order, body, "first_lanes", 0.1, 1, [(v, spec)], [(shaped((v.shape[0], lanes)), spec)])[0]


def gate(order, v):
    anywhere = pl.BlockSpec(memory_space=pl.ANY)

    def body(v, out):
        pass

    return call(order, body, "gate", 1, 1, [(v, anywhere)], [(shaped(v.shape, v.dtype), anywhere)], (), [(0, 0)])[0]


def widths_of(rows):
    if rows == 1216:
        return [(256, 0), (384, 256), (384, 640), (192, 1024)]
    cuts, at = [], 0
    while at < rows:
        w = min(256, rows - at)
        cuts.append((w, at))
        at += w
    return cuts


def split_weights(order, where, w_gate, w_up, w_down, cuts):
    own, d = w_gate.shape[0], w_down.shape[1]
    ff = w_down.shape[0]
    n = len(cuts)

    def body(where, gate, up, down, *refs):
        sends, mine, downs = refs[:n], refs[n : 2 * n], refs[2 * n :]

        def put(ref, core, cut):
            w, off = cut
            for m, src in enumerate((gate, up)):
                for side in (0, 1):
                    lo = (2 * m + side) * w
                    a = (2 * side + core) * ff + off
                    ref[:, lo : lo + w] = src[:, a : a + w]

        for core in (0, 1):

            @pl.when(where[CORE] == core)
            def _():
                for cut, ref, send in zip(cuts, mine, sends):
                    put(ref, core, cut)
                    put(send, 1 - core, cut)

        for (w, off), part in zip(cuts, downs):
            for lo in range(0, w, 128):
                hi = min(lo + 128, w)
                part[:, lo:hi] = down[off + lo : off + hi, :].T

    whole = lambda a: (a, fixed(a.shape))
    return call(
        order,
        body,
        "split_weights",
        0.1,
        1,
        [(where, SCALARS)] + [whole(a) for a in (w_gate, w_up, w_down)],
        [(shaped((own, 4 * w)), fixed((own, 4 * w))) for w, _ in cuts]
        + [(shaped((own, 4 * w)), fixed((own, 4 * w))) for w, _ in cuts]
        + [(shaped((d, w)), fixed((d, w))) for w, _ in cuts],
    )


def pack_weights(order, where, core_rows, mine, downs, groups, extra=()):
    own = mine[0].shape[0]
    widths = [m.shape[1] // 4 for m in mine]
    n = len(mine)

    def body(where, *refs):
        cores, refs = refs[:n], refs[n:]
        mine, downs, extras, outs = refs[:n], refs[n : 2 * n], refs[2 * n : 2 * n + len(extra)], refs[2 * n + len(extra) :]
        for group, out in zip(groups, outs):
            at6 = 0
            for k in group:
                w = widths[k]

                @pl.when(where[CORE] == where[Y])
                def _():
                    out[:, at6 : at6 + 4 * w] = mine[k][...]

                @pl.when(where[CORE] != where[Y])
                def _():
                    out[:, at6 : at6 + 4 * w] = cores[k][...]

                for h in (0, 1):
                    rows = pl.ds(pl.multiple_of((2 * where[Y] + h) * own, 16), own)
                    out[:, at6 + (4 + h) * w : at6 + (5 + h) * w] = downs[k][rows, :]
                at6 += 6 * w
        at6 = sum(6 * widths[k] for k in groups[0])
        for e in extras:
            outs[0][:, at6 : at6 + e.shape[1]] = e[...]
            at6 += e.shape[1]

    whole = lambda a: (a, fixed(a.shape))
    totals = [sum(6 * widths[k] for k in group) for group in groups]
    totals[0] += sum(e.shape[1] for e in extra)
    return call(
        order,
        body,
        "pack_weights",
        0.1,
        1,
        [(where, SCALARS)] + [whole(a) for a in (*core_rows, *mine, *downs, *extra)],
        [(shaped((own, m)), fixed((own, m))) for m in totals],
    )


def side_by_side(order, parts):
    rows, width = parts[0].shape[0], sum(p.shape[1] for p in parts)

    def body(*refs):
        lo = 0
        for ref in refs[:-1]:
            refs[-1][:, lo : lo + ref.shape[1]] = ref[...]
            lo += ref.shape[1]

    return call(
        order,
        body,
        "side_by_side",
        1,
        1,
        [(p, fixed(p.shape)) for p in parts],
        [(shaped((rows, width)), fixed((rows, width)))],
    )[0]


def place_rows(where, refs, rows, target):
    x, c = where[0], where[1]
    for ref, s in zip(refs, (2 * x + c, 2 * (1 - x) + c, 2 * x + 1 - c, 2 * (1 - x) + 1 - c)):
        target[pl.ds(pl.multiple_of(s * rows, 16), rows), :] = ref


def project(order, where, tokens, gain, own_w, across_w, core_w, far_w, bias, cos, sin):
    t, d = tokens.shape
    rows, width = own_w.shape
    kw = KVHEADS * HD
    qw = width - 2 * kw

    def body(where, tokens, gain, own_w, across_w, core_w, far_w, bias, cos, sin, normed, q, kx, vx, vz, w):
        @pl.when(pl.program_id(0) == 0)
        def _():
            place_rows(where, (own_w[...], across_w[...], core_w[...], far_w[...]), rows, w)

        v = tokens[...].astype(f32)
        inverse = lax.rsqrt(jnp.mean(v * v, axis=-1, keepdims=True) + epsilon)
        n = (v * inverse * gain[...]).astype(bf16)
        normed[...] = n
        lanes = lax.broadcasted_iota(jnp.int32, (TILE, 2 * HD), 1)
        left = lanes < HD
        c, s = cos[...], sin[...]
        for p in range(width // 128):
            at = slice(p * 128, p * 128 + 128)
            u = nn(n, w[:, at]) + bias[:, at]
            if p * 128 < qw + kw:
                u = (u * c + swap_halves(u, lanes) * s).astype(bf16)
            if p * 128 < qw:
                q[:, at] = (u.astype(f32) * 0.125).astype(bf16)
                continue
            u = u.astype(f32)
            turned = pltpu.roll(u, HD, 1)
            first, second = (kx, 0.0), (vx, 1.0)
            for ref, fill in (first,) if p * 128 < qw + kw else (second, (vz, 0.0)):
                ref[0] = jnp.where(left, u, fill).astype(bf16)
                ref[1] = jnp.where(left, fill, turned).astype(bf16)
                ref[2] = jnp.where(left, turned, fill).astype(bf16)
                ref[3] = jnp.where(left, fill, u).astype(bf16)

    heads = (shaped((4, t, 2 * HD)), pl.BlockSpec((4, TILE, 2 * HD), lambda i: (0, i, 0)))
    return call(
        order,
        body,
        "project",
        0.1,
        t // TILE,
        [
            (where, SCALARS),
            (tokens, by_rows(TILE, d)),
            (gain, fixed(gain.shape)),
            (own_w, fixed(own_w.shape)),
            (across_w, fixed(across_w.shape)),
            (core_w, fixed(core_w.shape)),
            (far_w, fixed(far_w.shape)),
            (bias, fixed(bias.shape)),
            (cos, by_rows(TILE, 2 * HD)),
            (sin, by_rows(TILE, 2 * HD)),
        ],
        [
            (shaped((t, d)), by_rows(TILE, d)),
            (shaped((t, qw)), by_rows(TILE, qw)),
            heads,
            heads,
            heads,
            (shaped((d, width)), fixed((d, width))),
        ],
    )


def swap_halves(v, lanes):
    half = HD // 2
    return jnp.where(lanes % HD < half, pltpu.roll(v, v.shape[1] - half, 1), pltpu.roll(v, half, 1))


def kinds_of(pair):
    return [2 * (2 * pair + side >= GROUP).astype(jnp.int32) + side for side in (0, 1)]


def attend(order, segments, q, kx, vx, first, last):
    t = q.shape[0]
    tiles = t // TILE

    def body(segc, segr, q, kx, vx, o, o_rest, linv, *rest):
        probs, bias = rest[:tiles], rest[tiles]
        step = pl.program_id(0)
        pair = step + first

        @pl.when(step == 0)
        def _():
            for i in range(tiles):
                w = (i + 1) * TILE
                rows = lax.broadcasted_iota(jnp.int32, (TILE, w), 0) + i * TILE
                cols = lax.broadcasted_iota(jnp.int32, (TILE, w), 1)
                ok = (segc[i * TILE : w, :] == segr[:, :w]) & (cols <= rows)
                bias[i * TILE : w, :w] = jnp.where(ok, 0.0, -1e30)

        left = lax.broadcasted_iota(jnp.int32, (TILE, 2 * HD), 1) < HD
        kinds = kinds_of(pair)
        for i in range(tiles):
            w = (i + 1) * TILE
            block = q[i * TILE : w, :]
            mixed = []
            for side in (0, 1):
                s = nt(block, kx[kinds[side], :w, :]) + bias[i * TILE : w, :w]
                e = jnp.exp(s - jnp.max(s, axis=-1, keepdims=True)).astype(bf16)
                for j in range(i + 1):
                    probs[j][side, (i - j) * TILE : (i - j + 1) * TILE, :] = e[:, j * TILE : (j + 1) * TILE]
                mixed.append(nn(e, vx[kinds[side], :w, :]))
            totals = jnp.where(left, pltpu.roll(mixed[0], HD, 1), pltpu.roll(mixed[1], HD, 1))
            inverse = 1.0 / totals
            out = jnp.where(left, mixed[0], mixed[1]) * inverse
            low = out.astype(bf16)
            o[i * TILE : w, :] = low
            o_rest[i * TILE : w, :] = (out - low.astype(f32)).astype(bf16)
            linv[i * TILE : w, :] = inverse

    count = last - first
    lane = pl.BlockSpec((t, 2 * HD), lambda p: (0, p + first))
    out_lane = pl.BlockSpec((t, 2 * HD), lambda p: (0, p))
    out = (t, count * 2 * HD)
    pshape = [(2 * count, t - j * TILE, TILE) for j in range(tiles)]
    return call(
        order,
        body,
        "attend",
        0.1,
        count,
        [
            (segments.reshape(t, 1), fixed((t, 1))),
            (segments.reshape(1, t), fixed((1, t))),
            (q, lane),
            (kx, fixed(kx.shape)),
            (vx, fixed(vx.shape)),
        ],
        [(shaped(out), out_lane), (shaped(out), out_lane), (shaped(out, f32), out_lane)]
        + [(shaped(s), pl.BlockSpec((2,) + s[1:], lambda p: (p, 0, 0))) for s in pshape],
        [pltpu.VMEM((t, t), f32)],
    )


def attend_back(order, q, do, o, o_rest, kx, vz, cos, sin, probs, first, last, running=()):
    t = q.shape[0]
    tiles = t // TILE
    count = last - first

    def body(q, do, o, o_rest, kx, vz, cos, sin, *rest):
        probs, rest = rest[:tiles], rest[tiles:]
        if running:
            dk_in, dv_in, rest = rest[0], rest[1], rest[2:]
        dq, dk, dv, ds0, ds1, dkacc, dvacc = rest
        step = pl.program_id(0)
        pair = step + first

        @pl.when(step == 0)
        def _():
            dkacc[...] = jnp.zeros_like(dkacc)
            dvacc[...] = jnp.zeros_like(dvacc)

        left = lax.broadcasted_iota(jnp.int32, (t, 2 * HD), 1) < HD
        along = do[...].astype(f32) * (o[...].astype(f32) + o_rest[...].astype(f32))
        inner = [
            jnp.sum(jnp.where(left, along, 0.0), axis=-1, keepdims=True),
            jnp.sum(jnp.where(left, 0.0, along), axis=-1, keepdims=True),
        ]
        kinds = kinds_of(pair)
        for side, ds in ((0, ds0), (1, ds1)):
            kind = kinds[side]
            for j in range(tiles):
                lo = j * TILE
                p = probs[j][side]
                dp = nt(do[lo:, :], vz[kind, lo : lo + TILE, :])
                d = (p.astype(f32) * (dp - inner[side][lo:])).astype(bf16)
                ds[lo:, lo : lo + TILE] = d
                dkacc[kind, lo : lo + TILE, :] += tn(d, q[lo:, :])
                dvacc[kind, lo : lo + TILE, :] += tn(p, do[lo:, :])
        lanes = lax.broadcasted_iota(jnp.int32, (TILE, 2 * HD), 1)
        for i in range(tiles):
            w = (i + 1) * TILE
            at = slice(i * TILE, w)
            g = (nn(ds0[at, :w], kx[kinds[0], :w, :]) + nn(ds1[at, :w], kx[kinds[1], :w, :])) * 0.125
            dq[at, :] = (g * cos[at, :] - swap_halves(g, lanes) * sin[at, :]).astype(bf16)

        @pl.when(step == count - 1)
        def _():
            one = lambda a: jnp.where(left, a[0] + pltpu.roll(a[1], HD, 1), pltpu.roll(a[2], HD, 1) + a[3])
            if not running:
                dk[...] = one(dkacc)
                dv[...] = one(dvacc)
                return
            lanes = lax.broadcasted_iota(jnp.int32, (t, 2 * HD), 1)
            g = one(dkacc) + dk_in[...]
            dk[...] = (g * cos[...] - swap_halves(g, lanes) * sin[...]).astype(bf16)
            dv[...] = (one(dvacc) + dv_in[...]).astype(bf16)

    lane = pl.BlockSpec((t, 2 * HD), lambda p: (0, p + first))
    out_lane = pl.BlockSpec((t, 2 * HD), lambda p: (0, p))
    wide = (4, t, 2 * HD)
    sums = (shaped((t, 2 * HD), bf16 if running else f32), fixed((t, 2 * HD)))
    return call(
        order,
        body,
        "attend_back",
        1 + count,
        count,
        [(q, lane), (do, out_lane), (o, out_lane), (o_rest, out_lane), (kx, fixed(wide)), (vz, fixed(wide))]
        + [(cos, fixed(cos.shape)), (sin, fixed(sin.shape))]
        + [(p, pl.BlockSpec((2,) + p.shape[1:], lambda i: (i, 0, 0))) for p in probs]
        + [(r, fixed(r.shape)) for r in running],
        [(shaped((t, count * 2 * HD)), out_lane), sums, sums],
        [pltpu.VMEM((t, t), bf16)] * 2 + [pltpu.VMEM(wide, f32)] * 2,
    )


def join_output(order, where, tokens, mixed, own_w, across, core, gain):
    t, d = tokens.shape
    steps = t // TILE
    rows = own_w.shape[0]
    n = len(mixed)

    def body(where, tokens, own_w, across, core, gain, *refs):
        mixed, resid, w, normed = refs[:n], refs[n], refs[n + 1], refs[n + 2 :]

        @pl.when(pl.program_id(0) == 0)
        def _():
            lo = across.shape[1] - 2 * d
            place_rows(where, (own_w[...], across[:, lo : lo + d], core[...], across[:, lo + d :]), rows, w)

        v, lo = tokens[...].astype(f32), 0
        for m in mixed:
            v = v + nn(m[...], w[lo : lo + m.shape[1], :])
            lo += m.shape[1]
        resid[...] = v
        inverse = lax.rsqrt(jnp.mean(v * v, axis=-1, keepdims=True) + epsilon)
        low = (v * inverse * gain[...]).astype(bf16)
        for k, out in enumerate(normed):

            @pl.when(pl.program_id(0) // (steps // 2) == k)
            def _():
                out[...] = low

    return call(
        order,
        body,
        "join_output",
        0.1,
        steps,
        [(where, SCALARS), (tokens, by_rows(TILE, d))]
        + [(a, fixed(a.shape)) for a in (own_w, across, core, gain)]
        + [(m, by_rows(TILE, m.shape[1])) for m in mixed],
        [
            (shaped((t, d), f32), by_rows(TILE, d)),
            (shaped((4 * rows, d)), fixed((4 * rows, d))),
        ]
        + [
            (shaped((t // 2, d)), pl.BlockSpec((TILE, d), lambda i, k=k: (jnp.clip(i - k * steps // 2, 0, steps // 2 - 1), 0)))
            for k in (0, 1)
        ],
    )


def ffn_part(order, where, n2, dy, mine, core_rows, x_rows, y_rows, down, cut, at6):
    t, d = dy[0].shape
    w, off = cut
    tt = t // 2
    own = mine.shape[0]
    half = d // 2
    steps = t // tt

    def body(where, dya, dyb, mine, core_rows, x_rows, y_rows, down, *refs):
        n2, (hid, dgu, keep, send, weights, acc, wt, tokens, copied) = refs[: len(refs) - 9], refs[-9:]
        step = pl.program_id(0)
        x, c, y = where[0], where[1], where[2]
        copy_out = pltpu.make_async_copy(wt, weights, copied)
        for k, ref in enumerate(n2):

            @pl.when(step == k)
            def _():
                tokens[...] = ref[...]

        @pl.when(step == 0)
        def _():
            def put(ref, s, at=at6):
                wt[pl.ds(pl.multiple_of(s * own, 16), own), : 4 * w] = ref[:, at : at + 4 * w]

            put(mine, 2 * x + c, 0)
            put(core_rows, 2 * x + 1 - c, 0)
            put(x_rows, 2 * (1 - x) + y)
            put(y_rows, 2 * (1 - x) + 1 - y)
            for side in (0, 1):

                @pl.when(x == side)
                def _():
                    wt[:, (4 + side) * w : (5 + side) * w] = down[...]
                    lo = (5 - side) * w
                    for ref, h in ((x_rows, y), (y_rows, 1 - y)):
                        for part in (0, 1):
                            at = pl.ds(pl.multiple_of((2 * h + part) * own, 16), own)
                            wt[at, lo : lo + w] = ref[:, at6 + (4 + part) * w : at6 + (5 + part) * w]

            copy_out.start()
            acc[...] = jnp.zeros_like(acc)

        a = tokens[...]
        b = jnp.where(step < steps, dya[...], dyb[...])
        for lo in range(0, 2 * w, BLK):
            hi = min(lo + BLK, 2 * w)
            g, u, v = slice(lo, hi), slice(2 * w + lo, 2 * w + hi), slice(4 * w + lo, 4 * w + hi)
            gate, up, dh = nn(a, wt[:, g]), nn(a, wt[:, u]), nn(b, wt[:, v])
            sig = jax.nn.sigmoid(gate)
            silu = gate * sig
            h = (silu * up).astype(bf16)
            d_gate = (dh * up * (sig + silu * (1.0 - sig))).astype(bf16)
            d_up = (dh * silu).astype(bf16)
            hid[:, g] = h
            dgu[:, g] = d_gate
            dgu[:, u] = d_up
            acc[:, v] += tn(b, h)
            acc[:, g] += tn(a, d_gate)
            acc[:, u] += tn(a, d_up)

        @pl.when(step == 2 * steps - 1)
        def _():
            copy_out.wait()
            for ref, side in ((keep, x), (send, 1 - x)):
                at = pl.ds(pl.multiple_of(side * half, 16), half)
                ref[:, : 4 * w] = acc[at, : 4 * w].astype(bf16)
            for side in (0, 1):

                @pl.when(x == side)
                def _():
                    for ref, s in ((keep, side), (send, 1 - side)):
                        lanes = slice((4 + s) * w, (5 + s) * w)
                        ref[:, 4 * w : 5 * w] = acc[:half, lanes].astype(bf16)
                        ref[:, 5 * w :] = acc[half:, lanes].astype(bf16)

    whole = lambda a: (a, fixed(a.shape))
    early = pl.BlockSpec((tt, d), lambda i: (jnp.minimum(i, steps - 1), 0))
    late = pl.BlockSpec((tt, d), lambda i: (jnp.maximum(i - steps, 0), 0))
    return call(
        order,
        body,
        "ffn_part",
        5 + w // 16 if off else 0.1,
        2 * steps,
        [(where, SCALARS), (dy[0], early), (dy[1], late)]
        + [whole(a) for a in (mine, core_rows, x_rows, y_rows, down, *n2)],
        [
            (shaped((2 * t, 2 * w)), by_rows(tt, 2 * w)),
            (shaped((2 * t, 4 * w)), by_rows(tt, 4 * w)),
            (shaped((half, 6 * w)), fixed((half, 6 * w))),
            (shaped((half, 6 * w)), fixed((half, 6 * w))),
            (shaped((d, 6 * w)), pl.BlockSpec(memory_space=pl.ANY)),
        ],
        [
            pltpu.VMEM((d, 6 * w), f32),
            pltpu.VMEM((d, 6 * w), bf16),
            pltpu.VMEM((tt, d), bf16),
            pltpu.SemaphoreType.DMA(()),
        ],
    )


def sum_parts(order, name, us, parts, weights, lanes, block, tokens, apart=False, add=None, pieces=(), tt=256):
    d = weights[0].shape[0]
    t = parts[0].shape[0] // 2
    n = len(parts)
    steps = t // tt
    k = len(tokens)

    def body(*refs):
        step = pl.program_id(0)
        total = None
        for part, weight in zip(refs[:n], refs[n : 2 * n]):
            s = nt(part[...], weight[...])
            total = s if total is None else total + s
        refs = refs[2 * n :]
        if pieces:
            more, others, refs = refs[0], refs[1 : 1 + len(pieces)], refs[1 + len(pieces) :]
            other = refs[-1]
            for at, ref in enumerate(others):

                @pl.when(step == at)
                def _():
                    other[...] = ref[...]

            total = total + more[...] + other[...].astype(f32)
        for out, (first, count, _) in zip(refs, outs):

            @pl.when((step >= first) & (step < first + count))
            def _():
                out[...] = total.astype(out.dtype)

    def spec(first, count):
        return pl.BlockSpec((tt, d), lambda i: (jnp.clip(i - first, 0, count - 1), 0))

    outs = []
    for at, half in enumerate(tokens):
        if half and apart:
            outs += [(at * steps + k, 1, bf16) for k in range(steps)]
        else:
            outs.append((at * steps, steps, bf16 if half or pieces else f32))

    start = tokens[0] * steps
    return call(
        order,
        body,
        name,
        us,
        k * steps,
        [(p, pl.BlockSpec((tt, p.shape[1]), lambda i: ((i + start) % (2 * steps), 0))) for p in parts]
        + [(w, pl.BlockSpec((d, n), lambda i: (0, block))) for w, n in zip(weights, lanes)]
        + ([(add, by_rows(tt, d))] if pieces else [])
        + [(p, fixed(p.shape)) for p in pieces],
        [(shaped((count * tt, d), kind), spec(first, count)) for first, count, kind in outs],
        [pltpu.VMEM((tt, d), bf16)] if pieces else [],
    )


def turn_back(order, dn2, dn2_other, residual, cotangent, gain, full_output, inverse_sums):
    t, d = residual.shape
    n = len(inverse_sums)

    steps = len(dn2_other)

    def body(dn2, resid, dy, gain, w, *refs):
        others, refs = refs[:steps], refs[steps:]
        sums, (d_resid, d_attn, grad_gain), scaled, other = refs[:n], refs[n : n + 3], refs[n + 3 : -1], refs[-1]
        step = pl.program_id(0)
        for k, ref in enumerate(others):

            @pl.when(step == k)
            def _():
                other[...] = ref[...]

        @pl.when(step == 0)
        def _():
            grad_gain[...] = jnp.zeros_like(grad_gain)

        up = dn2[...] + other[...].astype(f32)
        grad, gains = norm_back(resid[...], gain[...], up)
        grad_gain[...] += gains
        total = dy[...].astype(f32) + grad
        d_resid[...] = total
        low = total.astype(bf16)
        d_attn[...] = low
        d_mixed = nt(low, w[...]).astype(bf16).astype(f32)
        lo = 0
        for linv, out in zip(sums, scaled):
            hi = lo + linv.shape[1]
            out[...] = (d_mixed[:, lo:hi] * linv[...]).astype(bf16)
            lo = hi

    rows = by_rows(TILE, d)
    return call(
        order,
        body,
        "turn_back",
        8,
        steps,
        [(a, rows) for a in (dn2, residual, cotangent)]
        + [(gain, fixed(gain.shape)), (full_output, fixed(full_output.shape))]
        + [(a, fixed(a.shape)) for a in dn2_other]
        + [(a, by_rows(TILE, a.shape[1])) for a in inverse_sums],
        [(shaped((t, d), f32), rows), (shaped((t, d)), rows), (shaped((1, d), f32), fixed((1, d)))]
        + [(shaped((t, a.shape[1])), by_rows(TILE, a.shape[1])) for a in inverse_sums],
        [pltpu.VMEM((TILE, d), bf16)],
    )


def weight_grads(order, where, pairs, shares):
    d = sum(a.shape[1] for a in pairs[0][0])
    width = sum(g.shape[1] for _, g in pairs)
    own = d // 4
    lefts = []
    for pieces, _ in pairs:
        lefts += [a for a in pieces if not any(a is b for b in lefts)]
    rights = [g for _, g in pairs]
    place = [[next(i for i, b in enumerate(lefts) if b is a) for a in pieces] for pieces, _ in pairs]

    def body(where, *refs):
        left, right, refs = refs[: len(lefts)], refs[len(lefts) : len(lefts) + len(rights)], refs[len(lefts) + len(rights) :]
        keep, sends, grad = refs[0], refs[1:-1], refs[-1]
        c = where[CORE]
        lo = 0
        for spots, g in zip(place, right):
            hi = lo + g.shape[1]
            at = 0
            for i in spots:
                grad[at : at + left[i].shape[1], lo:hi] = tn(left[i][...], g[...]).astype(bf16)
                at += left[i].shape[1]
            lo = hi
        for side in (0, 1):
            rows = lambda core: pl.ds(pl.multiple_of((2 * side + core) * own, 16), own)
            at = slice(side * own, (side + 1) * own)
            keep[at, :] = grad[rows(c), :]
            lo = 0
            for ref in sends:
                ref[at, :] = grad[rows(1 - c), lo : lo + ref.shape[1]]
                lo += ref.shape[1]

    out = lambda lanes: (shaped((2 * own, lanes)), fixed((2 * own, lanes)))
    return call(
        order,
        body,
        "weight_grads",
        0.1,
        1,
        [(where, SCALARS)] + [(a, fixed(a.shape)) for a in (*lefts, *rights)],
        [out(lanes) for lanes in (width, *shares)],
        [pltpu.VMEM((d, width), bf16)],
    )


def finish_tokens(order, tokens, gain, d_parts, full_qkv, d_resid):
    t, d = tokens.shape
    n = len(d_parts)
    width = full_qkv.shape[1]

    def body(tokens, gain, w, d_resid, *refs):
        parts, out, grad_gain, sums = refs[:n], refs[n], refs[n + 1], refs[n + 2]

        @pl.when(pl.program_id(0) == 0)
        def _():
            grad_gain[...] = jnp.zeros_like(grad_gain)
            sums[...] = jnp.zeros_like(sums)

        total, lo = None, 0
        for part in parts:
            hi = lo + part.shape[1]
            p = part[...]
            sums[:, lo:hi] += jnp.sum(p.astype(f32), axis=0, keepdims=True)
            s = nt(p, w[:, lo:hi])
            total = s if total is None else total + s
            lo = hi
        grad, gains = norm_back(tokens[...].astype(f32), gain[...], total)
        grad_gain[...] += gains
        out[...] = d_resid[...] + grad

    rows = by_rows(TILE, d)
    return call(
        order,
        body,
        "finish_tokens",
        0.1,
        t // TILE,
        [(tokens, rows), (gain, fixed(gain.shape)), (full_qkv, fixed(full_qkv.shape)), (d_resid, rows)]
        + [(p, by_rows(TILE, p.shape[1])) for p in d_parts],
        [(shaped((t, d), f32), rows), (shaped((1, d), f32), fixed((1, d))), (shaped((1, width), f32), fixed((1, width)))],
    )


def assemble(order, where, halves, others, cores, cuts, ff):
    own = halves[0].shape[0]
    d = 4 * own
    n = len(cuts)
    steps = d // 128
    block = own // steps

    def body(where, *refs):
        halves, others, cores = refs[:n], refs[n : 2 * n], refs[2 * n : 3 * n]
        gate, up, down, down_t = refs[3 * n :]
        step = pl.program_id(0)
        c, y = where[1], where[2]
        rows = pl.ds(pl.multiple_of(step * block, 16), block)

        @pl.when(step == 0)
        def _():
            for (w, off), a, b in zip(cuts, halves, others):
                for ref, h in ((a, y), (b, 1 - y)):
                    for part in (0, 1):
                        at = pl.ds(pl.multiple_of((2 * part + h) * own, 16), own)
                        down_t[at, off : off + w] = ref[:, (4 + part) * w : (5 + part) * w]

        for core in (0, 1):
            for (w, off), a, b, o in zip(cuts, halves, others, cores):

                def put(ref, to):
                    for m, out in enumerate((gate, up)):
                        for side in (0, 1):
                            at = (2 * side + to) * ff + off
                            lo = (2 * m + side) * w
                            out[:, at : at + w] = ref[rows, lo : lo + w].astype(f32)

                @pl.when((c == core) & (c == y))
                def _():
                    put(a, core)

                @pl.when((c == core) & (c != y))
                def _():
                    put(b, core)

                @pl.when(c != core)
                def _():
                    put(o, core)

        down[...] = down_t[pl.ds(pl.multiple_of(step * 128, 128), 128), :].astype(f32).T

    whole = lambda a: (a, fixed(a.shape))
    return call(
        order,
        body,
        "assemble",
        11,
        steps,
        [(where, SCALARS)] + [whole(a) for a in (*halves, *others, *cores)],
        [
            (shaped((own, 4 * ff), f32), by_rows(block, 4 * ff)),
            (shaped((own, 4 * ff), f32), by_rows(block, 4 * ff)),
            (shaped((ff, d), f32), pl.BlockSpec((ff, 128), lambda i: (0, i))),
        ],
        [pltpu.VMEM((d, ff), bf16)],
    )


class Links:
    def __init__(self, shards, replicas):
        self.shards, self.replicas = shards, replicas
        s, r = lax.axis_index("shard"), lax.axis_index("replica")
        self.where = jnp.stack([s // 2, s % 2, r % 2, r // 2 % 2]).astype(jnp.int32)

    def core(self, v):
        return lax.ppermute(v, "shard", [(i, i ^ 1) for i in range(self.shards)])

    def across(self, v):
        return lax.ppermute(v, "shard", [(i, i ^ 2) for i in range(self.shards)])

    def beside(self, v):
        return lax.ppermute(v, "replica", [(i, i ^ 1) for i in range(self.replicas)])

    def far(self, v, bit):
        return lax.ppermute(v, "replica", [(i, i ^ bit) for i in range(self.replicas)])

    def along(self, v):
        return lax.psum(v, "replica", axis_index_groups=[list(range(y, self.replicas, 2)) for y in (0, 1)])

    def bits(self):
        bit = 2
        while bit < self.replicas:
            yield bit
            bit *= 2


def split_sum(axis, keep, *got):
    half = keep.shape[0] // 2
    shape = shaped((half, keep.shape[1]), keep.dtype)

    def body(where, keep, *refs):
        *got, mine, send = refs
        n = where[axis]
        for ref, h in ((mine, n), (send, 1 - n)):
            at = pl.ds(pl.multiple_of(h * half, 16), half)
            lo = 0
            for g in got:
                hi = lo + g.shape[1]
                ref[:, lo:hi] = (keep[at, lo:hi].astype(f32) + g[at, :].astype(f32)).astype(ref.dtype)
                lo = hi

    return body, [(a, fixed(a.shape)) for a in (keep, *got)], [shape, shape]


def whole_sum(v, got):
    def body(where, v, got, out):
        out[...] = (v[...].astype(f32) + got[...].astype(f32)).astype(out.dtype)

    return body, [(v, fixed(v.shape)), (got, fixed(got.shape))], [shaped(v.shape, v.dtype)]


def in_order(axis, mine, other, dtype=bf16):
    rows, width = mine.shape

    def body(where, mine, other, out):
        n = where[axis]
        out[pl.ds(pl.multiple_of(n * rows, 16), rows), :] = mine[...].astype(dtype)
        out[pl.ds(pl.multiple_of((1 - n) * rows, 16), rows), :] = other[...].astype(dtype)

    return body, [(mine, fixed(mine.shape)), (other, fixed(other.shape))], [shaped((2 * rows, width), dtype)]


def in_order_lanes(axis, mine, other, widths):
    rows = mine.shape[0]

    def body(where, mine, other, *outs):
        n = where[axis]
        lo = 0
        for out in outs:
            hi = lo + out.shape[1]
            out[pl.ds(pl.multiple_of(n * rows, 16), rows), :] = mine[:, lo:hi].astype(f32)
            out[pl.ds(pl.multiple_of((1 - n) * rows, 16), rows), :] = other[:, lo:hi].astype(f32)
            lo = hi

    return (
        body,
        [(mine, fixed(mine.shape)), (other, fixed(other.shape))],
        [shaped((2 * rows, w), f32) for w in widths],
    )


def lanes_sum(v, got, widths):
    def body(where, v, got, *outs):
        lo = 0
        for out in outs:
            hi = lo + out.shape[0]
            out[...] = (v[:, lo:hi] + got[:, lo:hi])[0]
            lo = hi

    return body, [(v, fixed(v.shape)), (got, fixed(got.shape))], [shaped((w,), v.dtype) for w in widths]


def rows_for_core(half, other, lanes):
    spec = fixed((half.shape[0], lanes))

    def body(where, half, other, out):
        same = where[CORE] == where[Y]

        @pl.when(same)
        def _():
            out[...] = other[...]

        @pl.when(jnp.logical_not(same))
        def _():
            out[...] = half[...]

    return body, [(half, spec), (other, spec)], [shaped((half.shape[0], lanes))]


GATE = "gate"


def advance(order, where, chains):
    chains = [chain for chain in chains if chain.asked is not None]
    for chain in [chain for chain in chains if chain.asked[0] == GATE]:
        chains.remove(chain)
        chain.give([gate(order, chain.asked[1])])
    if not chains:
        return
    asked = [chain.asked for chain in chains]
    n_in = sum(len(ins) for _, ins, _ in asked)

    def body(where, *refs):
        ins, outs = refs[:n_in], refs[n_in:]
        for part, i, o in asked:
            part(where, *ins[: len(i)], *outs[: len(o)])
            ins, outs = ins[len(i) :], outs[len(o) :]

    results = call(
        order,
        body,
        "sums",
        2,
        1,
        [(where, SCALARS)] + [pair for _, i, _ in asked for pair in i],
        [(shape, fixed(shape.shape)) for _, _, o in asked for shape in o],
    )
    for chain, (_, _, o) in zip(chains, asked):
        chain.give(results[: len(o)])
        results = results[len(o) :]


class Chain:
    def __init__(self, steps):
        self.steps = steps
        self.result = None
        self.asked = next(steps)

    def give(self, results):
        try:
            self.asked = self.steps.send(results)
        except StopIteration as stop:
            self.asked, self.result = None, stop.value


def replica_steps(order, links, mine, send, how):
    bits = list(links.bits())
    if how == "halves" and bits:
        mine, send = yield split_sum(Z, mine, links.beside(send))
        (mine,) = yield whole_sum(mine, links.far(send, bits[0]))
        for bit in bits[1:]:
            (mine,) = yield whole_sum(mine, links.far(mine, bit))
        (mine,) = yield in_order(Z, mine, links.far(mine, bits[0]))
    else:
        (mine,) = yield whole_sum(mine, links.beside(send))
        if how == "offload":
            (mine,) = yield GATE, links.along(mine)
        else:
            for bit in bits:
                (mine,) = yield whole_sum(mine, links.far(mine, bit))
    return mine, links.beside(mine)


def ffn_steps(order, links, keep, send, w, how):
    mine, send = yield split_sum(Y, keep, links.across(send))
    half, other = yield from replica_steps(order, links, mine, send, how)
    (rows,) = yield rows_for_core(half, other, 4 * w)
    return half, other, links.core(rows)


def owned_steps(order, links, keep, sends, how, widths):
    mine, send = yield split_sum(X, keep, *[links.core(send) for send in sends])
    mine, send = yield split_sum(Y, mine, links.across(send))
    half, other = yield from replica_steps(order, links, mine, send, how)
    return (yield in_order_lanes(Y, half, other, widths))


def small_steps(links, v, widths):
    moves = [links.core, links.beside, links.across]
    moves += [functools.partial(links.far, bit=bit) for bit in links.bits()]
    for move in moves[:-1]:
        (v,) = yield whole_sum(v, move(v))
    return (yield lanes_sum(v, moves[-1](v), widths))


def norm_back(values, gain_vector, upstream):
    inverse = lax.rsqrt(jnp.mean(values * values, axis=-1, keepdims=True) + epsilon)
    scaled = upstream * gain_vector
    grad_gain = jnp.sum(upstream * values * inverse, axis=0, keepdims=True)
    correction = jnp.sum(scaled * values, axis=-1, keepdims=True) / values.shape[-1]
    return inverse * scaled - values * (inverse * inverse * inverse) * correction, grad_gain


def position_tables(doc_ids):
    t = doc_ids.shape[0]
    earlier = jnp.sum((doc_ids[None, :] < doc_ids[:, None]).astype(jnp.int32), axis=1)
    places = jnp.arange(t, dtype=jnp.int32) - earlier
    frequency = rope_base ** (-jnp.arange(0, HD, 2).astype(f32) / HD)
    angles = places.astype(f32)[:, None] * frequency[None, :]
    cosine, sine = jnp.cos(angles), jnp.sin(angles)
    return jnp.tile(cosine, (1, 4)), jnp.tile(jnp.concatenate([-sine, sine], 1), (1, 2))


def on_device(
    links_shape,
    tokens,
    segments,
    cotangent,
    gain_attn,
    gain_ffn,
    w_query,
    bias_query,
    w_key,
    bias_key,
    w_value,
    bias_value,
    w_output,
    w_gate,
    w_up,
    w_down,
):
    links = Links(*links_shape)
    order = Order()
    where = links.where
    t, d = tokens.shape
    qw, kw = w_query.shape[1], w_key.shape[1]
    doc_ids = segments[0]
    ff = w_down.shape[0]
    cuts = widths_of(ff)
    cos, sin = position_tables(doc_ids)
    gain_attn, gain_ffn = gain_attn[None, :], gain_ffn[None, :]
    pieces = range(len(cuts))
    stages = [[[0]], [[1], list(pieces[2:])]] if len(cuts) > 2 else [[[n] for n in pieces]]
    group_of = [number for number, group in enumerate(g for stage in stages for g in stage) for _ in group]

    own_qkv = side_by_side(order, [w_query, w_key, w_value])
    across_qkv, core_qkv = links.across(own_qkv), links.core(own_qkv)
    dy = (cotangent, links.core(cotangent))
    order.wait(cos, sin)
    mine, downs, core_rows, x_rows, y_rows, at6 = [], [], [], [], [], []

    def split_stage(stage):
        chosen = [cuts[n] for group in stage for n in group]
        k = len(chosen)
        parts = split_weights(order, where, w_gate, w_up, w_down, chosen)
        core_rows.extend(links.core(v) for v in parts[:k])
        mine.extend(parts[k : 2 * k])
        downs.extend(parts[2 * k :])

    def pack_stage(stage, extra=()):
        chosen = [n for group in stage for n in group]
        first = chosen[0]
        packed = pack_weights(
            order,
            where,
            [core_rows[n] for n in chosen],
            [mine[n] for n in chosen],
            [downs[n] for n in chosen],
            [[n - first for n in group] for group in stage],
            extra,
        )
        for group in stage:
            at6.extend(sum(6 * cuts[m][0] for m in group[:k]) for k in range(len(group)))
        x_rows.extend(links.across(v) for v in packed)

    def forward_rows(*groups):
        for g in groups:
            if g < len(x_rows) and g == len(y_rows):
                if g == 0:
                    forwarded = first_lanes(order, x_rows[0], sum(6 * cuts[n][0] for n in stages[0][0]))
                else:
                    forwarded = x_rows[g] = gate(order, x_rows[g])
                y_rows.append(links.beside(forwarded))

    split_stage(stages[0])
    core_output = links.core(w_output)
    across_qkv = gate(order, across_qkv)
    far_qkv = links.core(across_qkv)
    pack_stage(stages[0], [w_output, core_output])

    bias = jnp.concatenate([bias_query, bias_key, bias_value])[None, :]
    order.wait(dy[1])
    normed, queries, kx, vx, vz, full_qkv = project(
        order, where, tokens, gain_attn, own_qkv, across_qkv, core_qkv, far_qkv, bias, cos, sin
    )
    middle = 3
    for stage in stages[1:]:
        split_stage(stage)
    first_part = attend(order, doc_ids, queries, kx, vx, 0, middle)
    forward_rows(0)
    for stage in stages[1:]:
        pack_stage(stage)
    second_part = attend(order, doc_ids, queries, kx, vx, middle, PAIRS)
    order.wait(y_rows[0])
    mixed, mixed_rest, inverse_sums = zip(first_part[:3], second_part[:3])
    probs = (first_part[3:], second_part[3:])
    residual, full_output, *normed_two = join_output(
        order, where, tokens, mixed, w_output, x_rows[0], core_output, gain_ffn
    )
    n2 = [*normed_two, *[links.core(v) for v in normed_two]]

    forward_rows(1)

    chains, hids, dgus, weights = [], [], [], []
    how = ["whole"] + ["halves"] * (len(cuts) - 2) + ["whole"]

    def step(*which):
        advance(order, where, [chains[n] for n in which if n < len(chains)])

    for n in pieces:
        g = group_of[n]
        forward_rows(g)
        if n >= 2:
            step(0)
        hid, dgu, keep, send, weight = ffn_part(
            order, where, n2, dy, mine[n], core_rows[n], x_rows[g], y_rows[g], downs[n], cuts[n], at6[n]
        )
        hids.append(hid), dgus.append(dgu), weights.append(weight)
        chains.append(Chain(ffn_steps(order, links, keep, send, cuts[n][0], how[n])))
        if n == 0:
            forward_rows(2)

    step(0, 1)
    *dn2_send, dn2 = sum_parts(order, "back_tokens", 24, dgus, weights, [4 * w for w, _ in cuts], 0, (1, 0), True)
    dn2_other = [links.core(v) for v in dn2_send]
    step(0, 1, 2)
    d_resid, d_attn, grad_gain_ffn, *scaled = turn_back(
        order, dn2, dn2_other, residual, cotangent, gain_ffn, full_output, inverse_sums
    )
    step(1)

    both = [
        (queries, scaled[n], mixed[n], mixed_rest[n], kx, vz, cos, sin, probs[n], *span)
        for n, span in enumerate(((0, middle), (middle, PAIRS)))
    ]
    dq_first, *running = attend_back(order, *both[0], ())
    step(1, 2, 3)
    out_keep, *out_sends = weight_grads(order, where, [(mixed, d_attn)], [d // 2 // 128 * 128, d - d // 2 // 128 * 128])
    out_chain = Chain(owned_steps(order, links, out_keep, out_sends, "whole", [d]))
    dq_second, d_key, d_value = attend_back(order, *both[1], running)
    chains.append(out_chain)
    n_out = len(chains) - 1
    step(0, 1, 2, 3, n_out)
    d_parts = [dq_first, dq_second, d_key, d_value]
    share = (qw + 2 * kw) // 3 // 128 * 128
    qkv_keep, *qkv_sends = weight_grads(
        order, where, [((normed,), p) for p in d_parts], [share, share, qw + 2 * kw - 2 * share]
    )
    chains.append(Chain(owned_steps(order, links, qkv_keep, qkv_sends, "whole", [qw, kw, kw])))
    n_qkv = n_out + 1
    step(3, n_out, n_qkv)
    grad_tokens, grad_gain_attn, grad_biases = finish_tokens(order, tokens, gain_attn, d_parts, full_qkv, d_resid)
    chains.append(
        Chain(small_steps(links, jnp.concatenate([grad_gain_attn, grad_gain_ffn, grad_biases], 1), [d, d, qw, kw, kw]))
    )
    n_small = n_qkv + 1
    step(1, 2, n_qkv, n_small)
    down_lanes = [2 * w for w, _ in cuts]
    out_other = [links.core(v) for v in sum_parts(order, "down_tokens", 0.1, hids, weights, down_lanes, 2, (1,), True)]
    step(2, n_out, n_qkv)
    (output,) = sum_parts(order, "down_tokens", 0.1, hids, weights, down_lanes, 2, (0,), False, residual, out_other)
    step(3, n_out, n_qkv, n_small)
    step(2, n_small)
    step(3, n_out, n_qkv, n_small)
    while any(chain.result is None for chain in chains[: len(cuts)]):
        step(*range(len(chains)))
    grad_gate, grad_up, grad_down = assemble(order, where, *zip(*(chain.result for chain in chains[: len(cuts)])), cuts, ff)
    while any(chain.result is None for chain in chains):
        step(*range(len(chains)))
    (grad_output,), grad_qkv, small = (chain.result for chain in chains[len(cuts) :])
    return (
        output,
        grad_tokens,
        small[0],
        small[1],
        grad_qkv[0],
        small[2],
        grad_qkv[1],
        small[3],
        grad_qkv[2],
        small[4],
        grad_output,
        grad_gate,
        grad_up,
        grad_down,
    )


def solution(mesh):
    tokens, rows, whole = P(("shard", "replica"), None), P("shard", None), P()
    return jax.shard_map(
        functools.partial(on_device, (mesh.shape["shard"], mesh.shape["replica"])),
        mesh=mesh,
        in_specs=(tokens, tokens, tokens, whole, whole, rows, whole, rows, whole, rows, whole, rows, rows, rows, rows),
        out_specs=(tokens, tokens, whole, whole, rows, whole, rows, whole, rows, whole, rows, rows, rows, rows),
        check_vma=False,
    )
```

```python
import functools

import jax
import jax.numpy as jnp
from jax import lax
from jax.experimental import pallas as pl
from jax.experimental.pallas import tpu as pltpu
from jax.sharding import PartitionSpec as P

HEADS, KVHEADS, HD = 14, 2, 64
GROUP = HEADS // KVHEADS
PAIRS = HEADS // 2
TILE = 256
BLK = 256
VMEM_CAP = (64 << 20) - (1 << 16)
bf16, f32 = jnp.bfloat16, jnp.float32
epsilon = 1e-06
rope_base = 1000000.0


def nn(a, b):
    return lax.dot_general(a, b, (((1,), (0,)), ((), ())), preferred_element_type=f32)


def nt(a, b):
    return lax.dot_general(a, b, (((1,), (1,)), ((), ())), preferred_element_type=f32)


def tn(a, b):
    return lax.dot_general(a, b, (((0,), (0,)), ((), ())), preferred_element_type=f32)


def shaped(shape, dtype=bf16):
    return jax.ShapeDtypeStruct(shape, dtype)


def fixed(shape):
    return pl.BlockSpec(shape, lambda i: (0,) * len(shape))


def by_rows(rows, columns, first=0):
    return pl.BlockSpec((rows, columns), lambda i: (i + first, 0))


SCALARS = pl.BlockSpec(memory_space=pltpu.SMEM)
X, CORE, Y, Z = range(4)


FLOPS_PER_US = 500 * 10**6


class Order:
    def __init__(self):
        self.due = []

    def wait(self, *arrays):
        self.due += arrays


def call(order, body, name, us, grid, ins, outs, scratch=(), aliases=()):
    after = order.due
    n = len(after)

    def kernel(*refs):
        body(*refs[n:])

    result = pl.pallas_call(
        kernel,
        grid=(grid,),
        in_specs=[pl.BlockSpec(memory_space=pl.ANY)] * n + [s for _, s in ins],
        out_specs=[s for _, s in outs],
        out_shape=[s for s, _ in outs],
        scratch_shapes=list(scratch),
        input_output_aliases={n + a: b for a, b in aliases},
        compiler_params=pltpu.CompilerParams(vmem_limit_bytes=VMEM_CAP),
        cost_estimate=pl.CostEstimate(flops=int(us * FLOPS_PER_US), bytes_accessed=10**5, transcendentals=0),
        name=name,
    )(*after, *[a for a, _ in ins])
    order.due = [result[0]]
    return result


def first_lanes(order, v, lanes):
    def body(v, out):
        out[...] = v[...]

    spec = fixed((v.shape[0], lanes))
    return call(order, body, "first_lanes", 0.1, 1, [(v, spec)], [(shaped((v.shape[0], lanes)), spec)])[0]


def gate(order, v):
    anywhere = pl.BlockSpec(memory_space=pl.ANY)

    def body(v, out):
        pass

    return call(order, body, "gate", 1, 1, [(v, anywhere)], [(shaped(v.shape, v.dtype), anywhere)], (), [(0, 0)])[0]


def widths_of(rows):
    if rows == 1216:
        return [(256, 0), (384, 256), (384, 640), (192, 1024)]
    cuts, at = [], 0
    while at < rows:
        w = min(256, rows - at)
        cuts.append((w, at))
        at += w
    return cuts


def split_weights(order, where, w_gate, w_up, w_down, cuts):
    own, d = w_gate.shape[0], w_down.shape[1]
    ff = w_down.shape[0]
    n = len(cuts)

    def body(where, gate, up, down, *refs):
        sends, mine, downs = refs[:n], refs[n : 2 * n], refs[2 * n :]

        def put(ref, core, cut):
            w, off = cut
            for m, src in enumerate((gate, up)):
                for side in (0, 1):
                    lo = (2 * m + side) * w
                    a = (2 * side + core) * ff + off
                    ref[:, lo : lo + w] = src[:, a : a + w]

        for core in (0, 1):

            @pl.when(where[CORE] == core)
            def _():
                for cut, ref, send in zip(cuts, mine, sends):
                    put(ref, core, cut)
                    put(send, 1 - core, cut)

        for (w, off), part in zip(cuts, downs):
            for lo in range(0, w, 128):
                hi = min(lo + 128, w)
                part[:, lo:hi] = down[off + lo : off + hi, :].T

    whole = lambda a: (a, fixed(a.shape))
    return call(
        order,
        body,
        "split_weights",
        0.1,
        1,
        [(where, SCALARS)] + [whole(a) for a in (w_gate, w_up, w_down)],
        [(shaped((own, 4 * w)), fixed((own, 4 * w))) for w, _ in cuts]
        + [(shaped((own, 4 * w)), fixed((own, 4 * w))) for w, _ in cuts]
        + [(shaped((d, w)), fixed((d, w))) for w, _ in cuts],
    )


def pack_weights(order, where, core_rows, mine, downs, groups, extra=()):
    own = mine[0].shape[0]
    widths = [m.shape[1] // 4 for m in mine]
    n = len(mine)

    def body(where, *refs):
        cores, refs = refs[:n], refs[n:]
        mine, downs, extras, outs = refs[:n], refs[n : 2 * n], refs[2 * n : 2 * n + len(extra)], refs[2 * n + len(extra) :]
        for group, out in zip(groups, outs):
            at6 = 0
            for k in group:
                w = widths[k]

                @pl.when(where[CORE] == where[Y])
                def _():
                    out[:, at6 : at6 + 4 * w] = mine[k][...]

                @pl.when(where[CORE] != where[Y])
                def _():
                    out[:, at6 : at6 + 4 * w] = cores[k][...]

                for h in (0, 1):
                    rows = pl.ds(pl.multiple_of((2 * where[Y] + h) * own, 16), own)
                    out[:, at6 + (4 + h) * w : at6 + (5 + h) * w] = downs[k][rows, :]
                at6 += 6 * w
        at6 = sum(6 * widths[k] for k in groups[0])
        for e in extras:
            outs[0][:, at6 : at6 + e.shape[1]] = e[...]
            at6 += e.shape[1]

    whole = lambda a: (a, fixed(a.shape))
    totals = [sum(6 * widths[k] for k in group) for group in groups]
    totals[0] += sum(e.shape[1] for e in extra)
    return call(
        order,
        body,
        "pack_weights",
        0.1,
        1,
        [(where, SCALARS)] + [whole(a) for a in (*core_rows, *mine, *downs, *extra)],
        [(shaped((own, m)), fixed((own, m))) for m in totals],
    )


def side_by_side(order, parts):
    rows, width = parts[0].shape[0], sum(p.shape[1] for p in parts)

    def body(*refs):
        lo = 0
        for ref in refs[:-1]:
            refs[-1][:, lo : lo + ref.shape[1]] = ref[...]
            lo += ref.shape[1]

    return call(
        order,
        body,
        "side_by_side",
        1,
        1,
        [(p, fixed(p.shape)) for p in parts],
        [(shaped((rows, width)), fixed((rows, width)))],
    )[0]


def place_rows(where, refs, rows, target):
    x, c = where[0], where[1]
    for ref, s in zip(refs, (2 * x + c, 2 * (1 - x) + c, 2 * x + 1 - c, 2 * (1 - x) + 1 - c)):
        target[pl.ds(pl.multiple_of(s * rows, 16), rows), :] = ref


def project(order, where, tokens, gain, own_w, across_w, core_w, far_w, bias, cos, sin):
    t, d = tokens.shape
    rows, width = own_w.shape
    kw = KVHEADS * HD
    qw = width - 2 * kw

    def body(where, tokens, gain, own_w, across_w, core_w, far_w, bias, cos, sin, normed, q, kx, vx, vz, w):
        @pl.when(pl.program_id(0) == 0)
        def _():
            place_rows(where, (own_w[...], across_w[...], core_w[...], far_w[...]), rows, w)

        v = tokens[...].astype(f32)
        inverse = lax.rsqrt(jnp.mean(v * v, axis=-1, keepdims=True) + epsilon)
        n = (v * inverse * gain[...]).astype(bf16)
        normed[...] = n
        lanes = lax.broadcasted_iota(jnp.int32, (TILE, 2 * HD), 1)
        left = lanes < HD
        c, s = cos[...], sin[...]
        for p in range(width // 128):
            at = slice(p * 128, p * 128 + 128)
            if p % 2 == 0:
                two = nn(n, w[:, p * 128 : p * 128 + 256])
            u = two[:, p % 2 * 128 : p % 2 * 128 + 128] + bias[:, at]
            if p * 128 < qw + kw:
                u = (u * c + swap_halves(u, lanes) * s).astype(bf16)
            if p * 128 < qw:
                q[:, at] = (u.astype(f32) * 0.125).astype(bf16)
                continue
            u = u.astype(f32)
            turned = pltpu.roll(u, HD, 1)
            first, second = (kx, 0.0), (vx, 1.0)
            for ref, fill in (first,) if p * 128 < qw + kw else (second, (vz, 0.0)):
                ref[0] = jnp.where(left, u, fill).astype(bf16)
                ref[1] = jnp.where(left, fill, turned).astype(bf16)
                ref[2] = jnp.where(left, turned, fill).astype(bf16)
                ref[3] = jnp.where(left, fill, u).astype(bf16)

    heads = (shaped((4, t, 2 * HD)), pl.BlockSpec((4, TILE, 2 * HD), lambda i: (0, i, 0)))
    return call(
        order,
        body,
        "project",
        0.1,
        t // TILE,
        [
            (where, SCALARS),
            (tokens, by_rows(TILE, d)),
            (gain, fixed(gain.shape)),
            (own_w, fixed(own_w.shape)),
            (across_w, fixed(across_w.shape)),
            (core_w, fixed(core_w.shape)),
            (far_w, fixed(far_w.shape)),
            (bias, fixed(bias.shape)),
            (cos, by_rows(TILE, 2 * HD)),
            (sin, by_rows(TILE, 2 * HD)),
        ],
        [
            (shaped((t, d)), by_rows(TILE, d)),
            (shaped((t, qw)), by_rows(TILE, qw)),
            heads,
            heads,
            heads,
            (shaped((d, width)), fixed((d, width))),
        ],
    )


def swap_halves(v, lanes):
    half = HD // 2
    return jnp.where(lanes % HD < half, pltpu.roll(v, v.shape[1] - half, 1), pltpu.roll(v, half, 1))


def kinds_of(pair):
    return [2 * (2 * pair + side >= GROUP).astype(jnp.int32) + side for side in (0, 1)]


def attend(order, segments, q, kx, vx, first, last):
    t = q.shape[0]
    tiles = t // TILE

    def body(segc, segr, q, kx, vx, o, o_rest, linv, *rest):
        probs, bias = rest[:tiles], rest[tiles]
        step = pl.program_id(0)
        pair = step + first

        @pl.when(step == 0)
        def _():
            for i in range(tiles):
                w = (i + 1) * TILE
                rows = lax.broadcasted_iota(jnp.int32, (TILE, w), 0) + i * TILE
                cols = lax.broadcasted_iota(jnp.int32, (TILE, w), 1)
                ok = (segc[i * TILE : w, :] == segr[:, :w]) & (cols <= rows)
                bias[i * TILE : w, :w] = jnp.where(ok, 0.0, -1e30)

        left = lax.broadcasted_iota(jnp.int32, (TILE, 2 * HD), 1) < HD
        kinds = kinds_of(pair)
        for i in range(tiles):
            w = (i + 1) * TILE
            block = q[i * TILE : w, :]
            mixed = []
            for side in (0, 1):
                s = nt(block, kx[kinds[side], :w, :]) + bias[i * TILE : w, :w]
                e = jnp.exp(s - jnp.max(s, axis=-1, keepdims=True)).astype(bf16)
                for j in range(i + 1):
                    probs[j][side, (i - j) * TILE : (i - j + 1) * TILE, :] = e[:, j * TILE : (j + 1) * TILE]
                mixed.append(nn(e, vx[kinds[side], :w, :]))
            totals = jnp.where(left, pltpu.roll(mixed[0], HD, 1), pltpu.roll(mixed[1], HD, 1))
            inverse = 1.0 / totals
            out = jnp.where(left, mixed[0], mixed[1]) * inverse
            low = out.astype(bf16)
            o[i * TILE : w, :] = low
            o_rest[i * TILE : w, :] = (out - low.astype(f32)).astype(bf16)
            linv[i * TILE : w, :] = inverse

    count = last - first
    lane = pl.BlockSpec((t, 2 * HD), lambda p: (0, p + first))
    out_lane = pl.BlockSpec((t, 2 * HD), lambda p: (0, p))
    out = (t, count * 2 * HD)
    pshape = [(2 * count, t - j * TILE, TILE) for j in range(tiles)]
    return call(
        order,
        body,
        "attend",
        0.1,
        count,
        [
            (segments.reshape(t, 1), fixed((t, 1))),
            (segments.reshape(1, t), fixed((1, t))),
            (q, lane),
            (kx, fixed(kx.shape)),
            (vx, fixed(vx.shape)),
        ],
        [(shaped(out), out_lane), (shaped(out), out_lane), (shaped(out, f32), out_lane)]
        + [(shaped(s), pl.BlockSpec((2,) + s[1:], lambda p: (p, 0, 0))) for s in pshape],
        [pltpu.VMEM((t, t), f32)],
    )


def attend_back(order, q, do, o, o_rest, kx, vz, cos, sin, probs, base, first, last, running=(), finish=False):
    t = q.shape[0]
    tiles = t // TILE
    count = last - first

    def body(q, do, o, o_rest, kx, vz, cos, sin, *rest):
        probs, rest = rest[:tiles], rest[tiles:]
        if running:
            dk_in, dv_in, rest = rest[0], rest[1], rest[2:]
        dq, dk, dv, ds0, ds1, dkacc, dvacc = rest
        step = pl.program_id(0)
        pair = step + first

        @pl.when(step == 0)
        def _():
            dkacc[...] = jnp.zeros_like(dkacc)
            dvacc[...] = jnp.zeros_like(dvacc)

        left = lax.broadcasted_iota(jnp.int32, (t, 2 * HD), 1) < HD
        along = do[...].astype(f32) * (o[...].astype(f32) + o_rest[...].astype(f32))
        inner = [
            jnp.sum(jnp.where(left, along, 0.0), axis=-1, keepdims=True),
            jnp.sum(jnp.where(left, 0.0, along), axis=-1, keepdims=True),
        ]
        kinds = kinds_of(pair)
        for side, ds in ((0, ds0), (1, ds1)):
            kind = kinds[side]
            for j in range(tiles):
                lo = j * TILE
                p = probs[j][side]
                dp = nt(do[lo:, :], vz[kind, lo : lo + TILE, :])
                d = (p.astype(f32) * (dp - inner[side][lo:])).astype(bf16)
                ds[lo:, lo : lo + TILE] = d
                dkacc[kind, lo : lo + TILE, :] += tn(d, q[lo:, :])
                dvacc[kind, lo : lo + TILE, :] += tn(p, do[lo:, :])
        lanes = lax.broadcasted_iota(jnp.int32, (TILE, 2 * HD), 1)
        for i in range(tiles):
            w = (i + 1) * TILE
            at = slice(i * TILE, w)
            g = (nn(ds0[at, :w], kx[kinds[0], :w, :]) + nn(ds1[at, :w], kx[kinds[1], :w, :])) * 0.125
            dq[at, :] = (g * cos[at, :] - swap_halves(g, lanes) * sin[at, :]).astype(bf16)

        @pl.when(step == count - 1)
        def _():
            one = lambda a: jnp.where(left, a[0] + pltpu.roll(a[1], HD, 1), pltpu.roll(a[2], HD, 1) + a[3])
            g, gv = one(dkacc), one(dvacc)
            if running:
                g, gv = g + dk_in[...], gv + dv_in[...]
            if finish:
                lanes = lax.broadcasted_iota(jnp.int32, (t, 2 * HD), 1)
                g = g * cos[...] - swap_halves(g, lanes) * sin[...]
            dk[...] = g.astype(dk.dtype)
            dv[...] = gv.astype(dv.dtype)

    lane = pl.BlockSpec((t, 2 * HD), lambda p: (0, p + first))
    out_lane = pl.BlockSpec((t, 2 * HD), lambda p: (0, p))
    part_lane = pl.BlockSpec((t, 2 * HD), lambda p: (0, p + first - base))
    wide = (4, t, 2 * HD)
    sums = (shaped((t, 2 * HD), bf16 if finish else f32), fixed((t, 2 * HD)))
    return call(
        order,
        body,
        "attend_back",
        0.1,
        count,
        [(q, lane), (do, part_lane), (o, part_lane), (o_rest, part_lane), (kx, fixed(wide)), (vz, fixed(wide))]
        + [(cos, fixed(cos.shape)), (sin, fixed(sin.shape))]
        + [(p, pl.BlockSpec((2,) + p.shape[1:], lambda i: (i + first - base, 0, 0))) for p in probs]
        + [(r, fixed(r.shape)) for r in running],
        [(shaped((t, count * 2 * HD)), out_lane), sums, sums],
        [pltpu.VMEM((t, t), bf16)] * 2 + [pltpu.VMEM(wide, f32)] * 2,
    )


def join_output(order, where, tokens, mixed, own_w, across, core, gain):
    t, d = tokens.shape
    steps = t // TILE
    rows = own_w.shape[0]
    n = len(mixed)

    def body(where, tokens, own_w, across, core, gain, *refs):
        mixed, resid, w, normed = refs[:n], refs[n], refs[n + 1], refs[n + 2 :]

        @pl.when(pl.program_id(0) == 0)
        def _():
            lo = across.shape[1] - 2 * d
            place_rows(where, (own_w[...], across[:, lo : lo + d], core[...], across[:, lo + d :]), rows, w)

        v, lo = tokens[...].astype(f32), 0
        for m in mixed:
            v = v + nn(m[...], w[lo : lo + m.shape[1], :])
            lo += m.shape[1]
        resid[...] = v
        inverse = lax.rsqrt(jnp.mean(v * v, axis=-1, keepdims=True) + epsilon)
        low = (v * inverse * gain[...]).astype(bf16)
        for k, out in enumerate(normed):

            @pl.when(pl.program_id(0) // (steps // 2) == k)
            def _():
                out[...] = low

    return call(
        order,
        body,
        "join_output",
        0.1,
        steps,
        [(where, SCALARS), (tokens, by_rows(TILE, d))]
        + [(a, fixed(a.shape)) for a in (own_w, across, core, gain)]
        + [(m, by_rows(TILE, m.shape[1])) for m in mixed],
        [
            (shaped((t, d), f32), by_rows(TILE, d)),
            (shaped((4 * rows, d)), fixed((4 * rows, d))),
        ]
        + [
            (shaped((t // 2, d)), pl.BlockSpec((TILE, d), lambda i, k=k: (jnp.clip(i - k * steps // 2, 0, steps // 2 - 1), 0)))
            for k in (0, 1)
        ],
    )


def ffn_part(order, where, n2, dy, mine, core_rows, x_rows, y_rows, down, cut, at6):
    t, d = dy[0].shape
    w, off = cut
    tt = t // 2
    own = mine.shape[0]
    half = d // 2
    steps = t // tt

    def body(where, dya, dyb, mine, core_rows, x_rows, y_rows, down, *refs):
        n2, (hid, dgu, keep, send, weights, acc, wt, tokens, copied, arrived) = refs[: len(refs) - 10], refs[-10:]
        step = pl.program_id(0)
        x, c, y = where[0], where[1], where[2]
        copy_out = pltpu.make_async_copy(wt, weights, copied)

        def fetch(k):
            return pltpu.make_async_copy(n2[k], tokens.at[k % 2], arrived.at[k % 2])

        @pl.when(step == 0)
        def _():
            fetch(0).start()

        for k in range(1, len(n2)):

            @pl.when(step == k - 1)
            def _():
                fetch(k).start()

        @pl.when(step == 0)
        def _():
            def put(ref, s, at=at6):
                wt[pl.ds(pl.multiple_of(s * own, 16), own), : 4 * w] = ref[:, at : at + 4 * w]

            put(mine, 2 * x + c, 0)
            put(core_rows, 2 * x + 1 - c, 0)
            put(x_rows, 2 * (1 - x) + y)
            put(y_rows, 2 * (1 - x) + 1 - y)
            for side in (0, 1):

                @pl.when(x == side)
                def _():
                    wt[:, (4 + side) * w : (5 + side) * w] = down[...]
                    lo = (5 - side) * w
                    for ref, h in ((x_rows, y), (y_rows, 1 - y)):
                        for part in (0, 1):
                            at = pl.ds(pl.multiple_of((2 * h + part) * own, 16), own)
                            wt[at, lo : lo + w] = ref[:, at6 + (4 + part) * w : at6 + (5 + part) * w]

            copy_out.start()

        for k in range(len(n2)):

            @pl.when(step == k)
            def _():
                fetch(k).wait()

        a = tokens[lax.rem(step, 2)]
        old = lambda at: jnp.where(step == 0, 0.0, acc[:, at])
        b = jnp.where(step < steps, dya[...], dyb[...])
        for lo in range(0, 2 * w, BLK):
            hi = min(lo + BLK, 2 * w)
            g, u, v = slice(lo, hi), slice(2 * w + lo, 2 * w + hi), slice(4 * w + lo, 4 * w + hi)
            gate, up, dh = nn(a, wt[:, g]), nn(a, wt[:, u]), nn(b, wt[:, v])
            sig = jax.nn.sigmoid(gate)
            silu = gate * sig
            h = (silu * up).astype(bf16)
            d_gate = (dh * up * (sig + silu * (1.0 - sig))).astype(bf16)
            d_up = (dh * silu).astype(bf16)
            hid[:, g] = h
            dgu[:, g] = d_gate
            dgu[:, u] = d_up
            acc[:, v] = old(v) + tn(b, h)
            acc[:, g] = old(g) + tn(a, d_gate)
            acc[:, u] = old(u) + tn(a, d_up)

        @pl.when(step == 2 * steps - 1)
        def _():
            copy_out.wait()
            for ref, side in ((keep, x), (send, 1 - x)):
                at = pl.ds(pl.multiple_of(side * half, 16), half)
                ref[:, : 4 * w] = acc[at, : 4 * w].astype(bf16)
            for side in (0, 1):

                @pl.when(x == side)
                def _():
                    for ref, s in ((keep, side), (send, 1 - side)):
                        lanes = slice((4 + s) * w, (5 + s) * w)
                        ref[:, 4 * w : 5 * w] = acc[:half, lanes].astype(bf16)
                        ref[:, 5 * w :] = acc[half:, lanes].astype(bf16)

    whole = lambda a: (a, fixed(a.shape))
    early = pl.BlockSpec((tt, d), lambda i: (jnp.minimum(i, steps - 1), 0))
    late = pl.BlockSpec((tt, d), lambda i: (jnp.maximum(i - steps, 0), 0))
    return call(
        order,
        body,
        "ffn_part",
        5 + w // 16 if off else 0.1,
        2 * steps,
        [(where, SCALARS), (dy[0], early), (dy[1], late)]
        + [whole(a) for a in (mine, core_rows, x_rows, y_rows, down)]
        + [(a, pl.BlockSpec(memory_space=pl.ANY)) for a in n2],
        [
            (shaped((2 * t, 2 * w)), by_rows(tt, 2 * w)),
            (shaped((2 * t, 4 * w)), by_rows(tt, 4 * w)),
            (shaped((half, 6 * w)), fixed((half, 6 * w))),
            (shaped((half, 6 * w)), fixed((half, 6 * w))),
            (shaped((d, 6 * w)), pl.BlockSpec(memory_space=pl.ANY)),
        ],
        [
            pltpu.VMEM((d, 6 * w), f32),
            pltpu.VMEM((d, 6 * w), bf16),
            pltpu.VMEM((2, tt, d), bf16),
            pltpu.SemaphoreType.DMA(()),
            pltpu.SemaphoreType.DMA((2,)),
        ],
    )


def sum_parts(order, name, us, parts, weights, lanes, block, tokens, apart=False, add=None, pieces=(), tt=256):
    d = weights[0].shape[0]
    t = parts[0].shape[0] // 2
    n = len(parts)
    steps = t // tt
    k = len(tokens)

    def body(*refs):
        step = pl.program_id(0)
        total = None
        for part, weight in zip(refs[:n], refs[n : 2 * n]):
            s = nt(part[...], weight[...])
            total = s if total is None else total + s
        refs = refs[2 * n :]
        if pieces:
            more, others, refs = refs[0], refs[1 : 1 + len(pieces)], refs[1 + len(pieces) :]
            other = refs[-1]
            for at, ref in enumerate(others):

                @pl.when(step == at)
                def _():
                    other[...] = ref[...]

            total = total + more[...] + other[...].astype(f32)
        for out, (first, count, _) in zip(refs, outs):

            @pl.when((step >= first) & (step < first + count))
            def _():
                out[...] = total.astype(out.dtype)

    def spec(first, count):
        return pl.BlockSpec((tt, d), lambda i: (jnp.clip(i - first, 0, count - 1), 0))

    outs = []
    for at, half in enumerate(tokens):
        if half and apart:
            outs += [(at * steps + k, 1, bf16) for k in range(steps)]
        else:
            outs.append((at * steps, steps, bf16 if half or pieces else f32))

    start = tokens[0] * steps
    return call(
        order,
        body,
        name,
        us,
        k * steps,
        [(p, pl.BlockSpec((tt, p.shape[1]), lambda i: ((i + start) % (2 * steps), 0))) for p in parts]
        + [(w, pl.BlockSpec((d, n), lambda i: (0, block))) for w, n in zip(weights, lanes)]
        + ([(add, by_rows(tt, d))] if pieces else [])
        + [(p, fixed(p.shape)) for p in pieces],
        [(shaped((count * tt, d), kind), spec(first, count)) for first, count, kind in outs],
        [pltpu.VMEM((tt, d), bf16)] if pieces else [],
    )


def turn_back(order, dn2, dn2_other, residual, cotangent, gain, full_output, inverse_sums):
    t, d = residual.shape
    n = len(inverse_sums)

    steps = len(dn2_other)

    def body(dn2, resid, dy, gain, w, *refs):
        others, refs = refs[:steps], refs[steps:]
        sums, (d_resid, d_attn, grad_gain), scaled, other = refs[:n], refs[n : n + 3], refs[n + 3 : -1], refs[-1]
        step = pl.program_id(0)
        for k, ref in enumerate(others):

            @pl.when(step == k)
            def _():
                other[...] = ref[...]

        @pl.when(step == 0)
        def _():
            grad_gain[...] = jnp.zeros_like(grad_gain)

        up = dn2[...] + other[...].astype(f32)
        grad, gains = norm_back(resid[...], gain[...], up)
        grad_gain[...] += gains
        total = dy[...].astype(f32) + grad
        d_resid[...] = total
        low = total.astype(bf16)
        d_attn[...] = low
        d_mixed = nt(low, w[...]).astype(bf16).astype(f32)
        lo = 0
        for linv, out in zip(sums, scaled):
            hi = lo + linv.shape[1]
            out[...] = (d_mixed[:, lo:hi] * linv[...]).astype(bf16)
            lo = hi

    rows = by_rows(TILE, d)
    return call(
        order,
        body,
        "turn_back",
        8,
        steps,
        [(a, rows) for a in (dn2, residual, cotangent)]
        + [(gain, fixed(gain.shape)), (full_output, fixed(full_output.shape))]
        + [(a, fixed(a.shape)) for a in dn2_other]
        + [(a, by_rows(TILE, a.shape[1])) for a in inverse_sums],
        [(shaped((t, d), f32), rows), (shaped((t, d)), rows), (shaped((1, d), f32), fixed((1, d)))]
        + [(shaped((t, a.shape[1])), by_rows(TILE, a.shape[1])) for a in inverse_sums],
        [pltpu.VMEM((TILE, d), bf16)],
    )


def weight_grads(order, where, pairs, shares):
    d = sum(a.shape[1] for a in pairs[0][0])
    width = sum(g.shape[1] for _, g in pairs)
    own = d // 4
    lefts = []
    for pieces, _ in pairs:
        lefts += [a for a in pieces if not any(a is b for b in lefts)]
    rights = [g for _, g in pairs]
    place = [[next(i for i, b in enumerate(lefts) if b is a) for a in pieces] for pieces, _ in pairs]

    def body(where, *refs):
        left, right, refs = refs[: len(lefts)], refs[len(lefts) : len(lefts) + len(rights)], refs[len(lefts) + len(rights) :]
        keep, sends, grad = refs[0], refs[1:-1], refs[-1]
        c = where[CORE]
        lo = 0
        for spots, g in zip(place, right):
            hi = lo + g.shape[1]
            at = 0
            for i in spots:
                grad[at : at + left[i].shape[1], lo:hi] = tn(left[i][...], g[...]).astype(bf16)
                at += left[i].shape[1]
            lo = hi
        for side in (0, 1):
            rows = lambda core: pl.ds(pl.multiple_of((2 * side + core) * own, 16), own)
            at = slice(side * own, (side + 1) * own)
            keep[at, :] = grad[rows(c), :]
            lo = 0
            for ref in sends:
                ref[at, :] = grad[rows(1 - c), lo : lo + ref.shape[1]]
                lo += ref.shape[1]

    out = lambda lanes: (shaped((2 * own, lanes)), fixed((2 * own, lanes)))
    return call(
        order,
        body,
        "weight_grads",
        0.1,
        1,
        [(where, SCALARS)] + [(a, fixed(a.shape)) for a in (*lefts, *rights)],
        [out(lanes) for lanes in (width, *shares)],
        [pltpu.VMEM((d, width), bf16)],
    )


def finish_tokens(order, tokens, gain, d_parts, full_qkv, d_resid):
    t, d = tokens.shape
    n = len(d_parts)
    width = full_qkv.shape[1]

    def body(tokens, gain, w, d_resid, *refs):
        parts, out, grad_gain, sums = refs[:n], refs[n], refs[n + 1], refs[n + 2]

        @pl.when(pl.program_id(0) == 0)
        def _():
            grad_gain[...] = jnp.zeros_like(grad_gain)
            sums[...] = jnp.zeros_like(sums)

        total, lo = None, 0
        for part in parts:
            hi = lo + part.shape[1]
            p = part[...]
            sums[:, lo:hi] += jnp.sum(p.astype(f32), axis=0, keepdims=True)
            s = nt(p, w[:, lo:hi])
            total = s if total is None else total + s
            lo = hi
        grad, gains = norm_back(tokens[...].astype(f32), gain[...], total)
        grad_gain[...] += gains
        out[...] = d_resid[...] + grad

    rows = by_rows(TILE, d)
    return call(
        order,
        body,
        "finish_tokens",
        0.1,
        t // TILE,
        [(tokens, rows), (gain, fixed(gain.shape)), (full_qkv, fixed(full_qkv.shape)), (d_resid, rows)]
        + [(p, by_rows(TILE, p.shape[1])) for p in d_parts],
        [(shaped((t, d), f32), rows), (shaped((1, d), f32), fixed((1, d))), (shaped((1, width), f32), fixed((1, width)))],
    )


def assemble(order, where, halves, others, cores, cuts, ff):
    own = halves[0].shape[0]
    d = 4 * own
    n = len(cuts)
    steps = d // 128
    block = own // steps

    def body(where, *refs):
        halves, others, cores = refs[:n], refs[n : 2 * n], refs[2 * n : 3 * n]
        gate, up, down, down_t = refs[3 * n :]
        step = pl.program_id(0)
        c, y = where[1], where[2]
        rows = pl.ds(pl.multiple_of(step * block, 16), block)

        @pl.when(step == 0)
        def _():
            for (w, off), a, b in zip(cuts, halves, others):
                for ref, h in ((a, y), (b, 1 - y)):
                    for part in (0, 1):
                        at = pl.ds(pl.multiple_of((2 * part + h) * own, 16), own)
                        down_t[at, off : off + w] = ref[:, (4 + part) * w : (5 + part) * w]

        for core in (0, 1):
            for (w, off), a, b, o in zip(cuts, halves, others, cores):

                def put(ref, to):
                    for m, out in enumerate((gate, up)):
                        for side in (0, 1):
                            at = (2 * side + to) * ff + off
                            lo = (2 * m + side) * w
                            out[:, at : at + w] = ref[rows, lo : lo + w].astype(f32)

                @pl.when((c == core) & (c == y))
                def _():
                    put(a, core)

                @pl.when((c == core) & (c != y))
                def _():
                    put(b, core)

                @pl.when(c != core)
                def _():
                    put(o, core)

        down[...] = down_t[pl.ds(pl.multiple_of(step * 128, 128), 128), :].astype(f32).T

    whole = lambda a: (a, fixed(a.shape))
    return call(
        order,
        body,
        "assemble",
        11,
        steps,
        [(where, SCALARS)] + [whole(a) for a in (*halves, *others, *cores)],
        [
            (shaped((own, 4 * ff), f32), by_rows(block, 4 * ff)),
            (shaped((own, 4 * ff), f32), by_rows(block, 4 * ff)),
            (shaped((ff, d), f32), pl.BlockSpec((ff, 128), lambda i: (0, i))),
        ],
        [pltpu.VMEM((d, ff), bf16)],
    )


class Links:
    def __init__(self, shards, replicas):
        self.shards, self.replicas = shards, replicas
        s, r = lax.axis_index("shard"), lax.axis_index("replica")
        self.where = jnp.stack([s // 2, s % 2, r % 2, r // 2 % 2]).astype(jnp.int32)

    def core(self, v):
        return lax.ppermute(v, "shard", [(i, i ^ 1) for i in range(self.shards)])

    def across(self, v):
        return lax.ppermute(v, "shard", [(i, i ^ 2) for i in range(self.shards)])

    def beside(self, v):
        return lax.ppermute(v, "replica", [(i, i ^ 1) for i in range(self.replicas)])

    def far(self, v, bit):
        return lax.ppermute(v, "replica", [(i, i ^ bit) for i in range(self.replicas)])

    def along(self, v):
        return lax.psum(v, "replica", axis_index_groups=[list(range(y, self.replicas, 2)) for y in (0, 1)])

    def bits(self):
        bit = 2
        while bit < self.replicas:
            yield bit
            bit *= 2


def split_sum(axis, keep, *got):
    half = keep.shape[0] // 2
    shape = shaped((half, keep.shape[1]), keep.dtype)

    def body(where, keep, *refs):
        *got, mine, send = refs
        n = where[axis]
        for ref, h in ((mine, n), (send, 1 - n)):
            at = pl.ds(pl.multiple_of(h * half, 16), half)
            lo = 0
            for g in got:
                hi = lo + g.shape[1]
                ref[:, lo:hi] = (keep[at, lo:hi].astype(f32) + g[at, :].astype(f32)).astype(ref.dtype)
                lo = hi

    return body, [(a, fixed(a.shape)) for a in (keep, *got)], [shape, shape]


def whole_sum(v, got):
    def body(where, v, got, out):
        out[...] = (v[...].astype(f32) + got[...].astype(f32)).astype(out.dtype)

    return body, [(v, fixed(v.shape)), (got, fixed(got.shape))], [shaped(v.shape, v.dtype)]


def in_order(axis, mine, other, dtype=bf16):
    rows, width = mine.shape

    def body(where, mine, other, out):
        n = where[axis]
        out[pl.ds(pl.multiple_of(n * rows, 16), rows), :] = mine[...].astype(dtype)
        out[pl.ds(pl.multiple_of((1 - n) * rows, 16), rows), :] = other[...].astype(dtype)

    return body, [(mine, fixed(mine.shape)), (other, fixed(other.shape))], [shaped((2 * rows, width), dtype)]


def in_order_lanes(axis, mine, other, widths):
    rows = mine.shape[0]

    def body(where, mine, other, *outs):
        n = where[axis]
        lo = 0
        for out in outs:
            hi = lo + out.shape[1]
            out[pl.ds(pl.multiple_of(n * rows, 16), rows), :] = mine[:, lo:hi].astype(f32)
            out[pl.ds(pl.multiple_of((1 - n) * rows, 16), rows), :] = other[:, lo:hi].astype(f32)
            lo = hi

    return (
        body,
        [(mine, fixed(mine.shape)), (other, fixed(other.shape))],
        [shaped((2 * rows, w), f32) for w in widths],
    )


def lanes_sum(v, got, widths):
    def body(where, v, got, *outs):
        lo = 0
        for out in outs:
            hi = lo + out.shape[0]
            out[...] = (v[:, lo:hi] + got[:, lo:hi])[0]
            lo = hi

    return body, [(v, fixed(v.shape)), (got, fixed(got.shape))], [shaped((w,), v.dtype) for w in widths]


def rows_for_core(half, other, lanes):
    spec = fixed((half.shape[0], lanes))

    def body(where, half, other, out):
        same = where[CORE] == where[Y]

        @pl.when(same)
        def _():
            out[...] = other[...]

        @pl.when(jnp.logical_not(same))
        def _():
            out[...] = half[...]

    return body, [(half, spec), (other, spec)], [shaped((half.shape[0], lanes))]


GATE = "gate"


def advance(order, where, chains, us=2):
    chains = [chain for chain in chains if chain.asked is not None]
    for chain in [chain for chain in chains if chain.asked[0] == GATE]:
        chains.remove(chain)
        chain.give([gate(order, chain.asked[1])])
    if not chains:
        return
    asked = [chain.asked for chain in chains]
    n_in = sum(len(ins) for _, ins, _ in asked)

    def body(where, *refs):
        ins, outs = refs[:n_in], refs[n_in:]
        for part, i, o in asked:
            part(where, *ins[: len(i)], *outs[: len(o)])
            ins, outs = ins[len(i) :], outs[len(o) :]

    results = call(
        order,
        body,
        "sums",
        us,
        1,
        [(where, SCALARS)] + [pair for _, i, _ in asked for pair in i],
        [(shape, fixed(shape.shape)) for _, _, o in asked for shape in o],
    )
    for chain, (_, _, o) in zip(chains, asked):
        chain.give(results[: len(o)])
        results = results[len(o) :]


class Chain:
    def __init__(self, steps):
        self.steps = steps
        self.result = None
        self.asked = next(steps)

    def give(self, results):
        try:
            self.asked = self.steps.send(results)
        except StopIteration as stop:
            self.asked, self.result = None, stop.value


def replica_steps(order, links, mine, send, how):
    bits = list(links.bits())
    if how == "halves" and bits:
        mine, send = yield split_sum(Z, mine, links.beside(send))
        (mine,) = yield whole_sum(mine, links.far(send, bits[0]))
        for bit in bits[1:]:
            (mine,) = yield whole_sum(mine, links.far(mine, bit))
        (mine,) = yield in_order(Z, mine, links.far(mine, bits[0]))
    else:
        (mine,) = yield whole_sum(mine, links.beside(send))
        if how == "offload":
            (mine,) = yield GATE, links.along(mine)
        else:
            for bit in bits:
                (mine,) = yield whole_sum(mine, links.far(mine, bit))
    return mine, links.beside(mine)


def ffn_steps(order, links, keep, send, w, how):
    mine, send = yield split_sum(Y, keep, links.across(send))
    half, other = yield from replica_steps(order, links, mine, send, how)
    (rows,) = yield rows_for_core(half, other, 4 * w)
    (cores,) = yield GATE, links.core(rows)
    return half, other, cores


def owned_steps(order, links, keep, sends, how, widths):
    mine, send = yield split_sum(X, keep, *[links.core(send) for send in sends])
    mine, send = yield split_sum(Y, mine, links.across(send))
    half, other = yield from replica_steps(order, links, mine, send, how)
    return (yield in_order_lanes(Y, half, other, widths))


def beside_each_other(parts):
    def body(where, *refs):
        lo = 0
        for ref in refs[:-1]:
            refs[-1][:, lo : lo + ref.shape[1]] = ref[...]
            lo += ref.shape[1]

    width = sum(p.shape[1] for p in parts)
    return body, [(p, fixed(p.shape)) for p in parts], [shaped((parts[0].shape[0], width), parts[0].dtype)]


def small_steps(links, parts, widths):
    (v,) = yield beside_each_other(parts)
    moves = [links.core, links.across]
    moves += [functools.partial(links.far, bit=bit) for bit in links.bits()]
    moves.append(links.beside)
    for move in moves[:-1]:
        (v,) = yield whole_sum(v, move(v))
    return (yield lanes_sum(v, moves[-1](v), widths))


def norm_back(values, gain_vector, upstream):
    inverse = lax.rsqrt(jnp.mean(values * values, axis=-1, keepdims=True) + epsilon)
    scaled = upstream * gain_vector
    grad_gain = jnp.sum(upstream * values * inverse, axis=0, keepdims=True)
    correction = jnp.sum(scaled * values, axis=-1, keepdims=True) / values.shape[-1]
    return inverse * scaled - values * (inverse * inverse * inverse) * correction, grad_gain


def position_tables(doc_ids):
    t = doc_ids.shape[0]
    earlier = jnp.sum((doc_ids[None, :] < doc_ids[:, None]).astype(jnp.int32), axis=1)
    places = jnp.arange(t, dtype=jnp.int32) - earlier
    frequency = rope_base ** (-jnp.arange(0, HD, 2).astype(f32) / HD)
    angles = places.astype(f32)[:, None] * frequency[None, :]
    cosine, sine = jnp.cos(angles), jnp.sin(angles)
    return jnp.tile(cosine, (1, 4)), jnp.tile(jnp.concatenate([-sine, sine], 1), (1, 2))


def on_device(
    links_shape,
    tokens,
    segments,
    cotangent,
    gain_attn,
    gain_ffn,
    w_query,
    bias_query,
    w_key,
    bias_key,
    w_value,
    bias_value,
    w_output,
    w_gate,
    w_up,
    w_down,
):
    links = Links(*links_shape)
    order = Order()
    where = links.where
    t, d = tokens.shape
    qw, kw = w_query.shape[1], w_key.shape[1]
    doc_ids = segments[0]
    ff = w_down.shape[0]
    cuts = widths_of(ff)
    cos, sin = position_tables(doc_ids)
    gain_attn, gain_ffn = gain_attn[None, :], gain_ffn[None, :]
    pieces = range(len(cuts))
    stages = [[[0]], [[1], list(pieces[2:])]] if len(cuts) > 2 else [[[n] for n in pieces]]
    group_of = [number for number, group in enumerate(g for stage in stages for g in stage) for _ in group]

    own_qkv = side_by_side(order, [w_query, w_key, w_value])
    across_qkv, core_qkv = links.across(own_qkv), links.core(own_qkv)
    dy = (cotangent, links.core(cotangent))
    order.wait(cos, sin)
    mine, downs, core_rows, x_rows, y_rows, at6 = [], [], [], [], [], []

    def split_stage(stage):
        chosen = [cuts[n] for group in stage for n in group]
        k = len(chosen)
        parts = split_weights(order, where, w_gate, w_up, w_down, chosen)
        core_rows.extend(links.core(v) for v in parts[:k])
        mine.extend(parts[k : 2 * k])
        downs.extend(parts[2 * k :])

    def pack_stage(stage, extra=()):
        chosen = [n for group in stage for n in group]
        first = chosen[0]
        packed = pack_weights(
            order,
            where,
            [core_rows[n] for n in chosen],
            [mine[n] for n in chosen],
            [downs[n] for n in chosen],
            [[n - first for n in group] for group in stage],
            extra,
        )
        for group in stage:
            at6.extend(sum(6 * cuts[m][0] for m in group[:k]) for k in range(len(group)))
        x_rows.extend(links.across(v) for v in packed)

    def forward_rows(*groups):
        for g in groups:
            if g < len(x_rows) and g == len(y_rows):
                if g == 0:
                    forwarded = first_lanes(order, x_rows[0], sum(6 * cuts[n][0] for n in stages[0][0]))
                else:
                    forwarded = x_rows[g] = gate(order, x_rows[g])
                y_rows.append(links.beside(forwarded))

    split_stage(stages[0])
    core_output = links.core(w_output)
    across_qkv = gate(order, across_qkv)
    far_qkv = links.core(across_qkv)
    pack_stage(stages[0], [w_output, core_output])

    bias = jnp.concatenate([bias_query, bias_key, bias_value])[None, :]
    order.wait(dy[1])
    normed, queries, kx, vx, vz, full_qkv = project(
        order, where, tokens, gain_attn, own_qkv, across_qkv, core_qkv, far_qkv, bias, cos, sin
    )
    middle = 3
    for stage in stages[1:]:
        split_stage(stage)
    first_part = attend(order, doc_ids, queries, kx, vx, 0, middle)
    forward_rows(0)
    for stage in stages[1:]:
        pack_stage(stage)
    second_part = attend(order, doc_ids, queries, kx, vx, middle, PAIRS)
    order.wait(y_rows[0])
    mixed, mixed_rest, inverse_sums = zip(first_part[:3], second_part[:3])
    probs = (first_part[3:], second_part[3:])
    residual, full_output, *normed_two = join_output(
        order, where, tokens, mixed, w_output, x_rows[0], core_output, gain_ffn
    )
    n2 = [*normed_two, *[links.core(v) for v in normed_two]]

    forward_rows(1)

    chains, hids, dgus, weights = [], [], [], []
    how = ["whole"] + ["halves"] * (len(cuts) - 2) + ["whole"]

    def step(*which, us=2):
        advance(order, where, [chains[n] for n in which if n < len(chains)], us)

    for n in pieces:
        g = group_of[n]
        forward_rows(g)
        if n >= 2:
            step(0)
        hid, dgu, keep, send, weight = ffn_part(
            order, where, n2, dy, mine[n], core_rows[n], x_rows[g], y_rows[g], downs[n], cuts[n], at6[n]
        )
        hids.append(hid), dgus.append(dgu), weights.append(weight)
        chains.append(Chain(ffn_steps(order, links, keep, send, cuts[n][0], how[n])))
        if n == 0:
            forward_rows(2)

    step(0, 1)
    *dn2_send, dn2 = sum_parts(order, "back_tokens", 24, dgus, weights, [4 * w for w, _ in cuts], 0, (1, 0), True)
    dn2_other = [links.core(v) for v in dn2_send]
    step(0, 1, 2)
    d_resid, d_attn, grad_gain_ffn, *scaled = turn_back(
        order, dn2, dn2_other, residual, cotangent, gain_ffn, full_output, inverse_sums
    )
    step(1)

    out_keep, *out_sends = weight_grads(order, where, [(mixed, d_attn)], [d // 2 // 128 * 128, d - d // 2 // 128 * 128])
    n_out, n_qkv, n_small = (len(cuts) + n for n in range(3))
    chains.append(Chain(owned_steps(order, links, out_keep, out_sends, "whole", [d])))

    both = [(queries, scaled[n], mixed[n], mixed_rest[n], kx, vz, cos, sin, probs[n]) for n in (0, 1)]
    late = middle + (PAIRS - middle) // 2
    dq_first, *running = attend_back(order, *both[0], 0, 0, middle)
    step(2, 3, n_out, us=0.1)
    dq_second, *running = attend_back(order, *both[1], middle, middle, late, running)
    step(1, 2, us=0.1)
    dq_third, d_key, d_value = attend_back(order, *both[1], middle, late, PAIRS, running, True)
    d_parts = [dq_first, dq_second, dq_third, d_key, d_value]
    share = (qw + 2 * kw) // 3 // 128 * 128
    qkv_keep, *qkv_sends = weight_grads(
        order, where, [((normed,), p) for p in d_parts], [share, share, qw + 2 * kw - 2 * share]
    )
    chains.append(Chain(owned_steps(order, links, qkv_keep, qkv_sends, "whole", [qw, kw, kw])))
    step(0, 1, 2, 3, n_out, us=0.1)
    step(n_qkv, us=0.1)
    grad_tokens, grad_gain_attn, grad_biases = finish_tokens(order, tokens, gain_attn, d_parts, full_qkv, d_resid)
    chains.append(Chain(small_steps(links, [grad_gain_attn, grad_gain_ffn, grad_biases], [d, d, qw, kw, kw])))
    down_lanes = [2 * w for w, _ in cuts]
    out_other = [links.core(v) for v in sum_parts(order, "down_tokens", 0.1, hids, weights, down_lanes, 2, (1,), True)]
    step(0, 1, 2, 3, n_out, n_qkv, n_small, us=0.1)
    (output,) = sum_parts(order, "down_tokens", 20, hids, weights, down_lanes, 2, (0,), False, residual, out_other)
    step(n_qkv, n_small, us=20)
    step(1, 2, 3, n_qkv, n_small, us=20)
    step(3, n_out, n_qkv, n_small, us=20)
    while any(chain.result is None for chain in chains[: len(cuts)]):
        step(*range(len(cuts)), us=20)
    grad_gate, grad_up, grad_down = assemble(order, where, *zip(*(chain.result for chain in chains[: len(cuts)])), cuts, ff)
    while any(chain.result is None for chain in chains):
        step(*range(len(chains)), us=20)
    (grad_output,), grad_qkv, small = (chain.result for chain in chains[len(cuts) :])
    return (
        output,
        grad_tokens,
        small[0],
        small[1],
        grad_qkv[0],
        small[2],
        grad_qkv[1],
        small[3],
        grad_qkv[2],
        small[4],
        grad_output,
        grad_gate,
        grad_up,
        grad_down,
    )


def solution(mesh):
    tokens, rows, whole = P(("shard", "replica"), None), P("shard", None), P()
    return jax.shard_map(
        functools.partial(on_device, (mesh.shape["shard"], mesh.shape["replica"])),
        mesh=mesh,
        in_specs=(tokens, tokens, tokens, whole, whole, rows, whole, rows, whole, rows, whole, rows, rows, rows, rows),
        out_specs=(tokens, tokens, whole, whole, rows, whole, rows, whole, rows, whole, rows, rows, rows, rows),
        check_vma=False,
    )
```

```python
import functools

import jax
import jax.numpy as jnp
from jax import lax
from jax.experimental import pallas as pl
from jax.experimental.pallas import tpu as pltpu
from jax.sharding import PartitionSpec as P

HEADS, KVHEADS, HD = 14, 2, 64
GROUP = HEADS // KVHEADS
PAIRS = HEADS // 2
TILE = 256
BLK = 256
VMEM_CAP = (64 << 20) - (1 << 16)
bf16, f32 = jnp.bfloat16, jnp.float32
epsilon = 1e-06
rope_base = 1000000.0


def nn(a, b):
    return lax.dot_general(a, b, (((1,), (0,)), ((), ())), preferred_element_type=f32)


def nt(a, b):
    return lax.dot_general(a, b, (((1,), (1,)), ((), ())), preferred_element_type=f32)


def tn(a, b):
    return lax.dot_general(a, b, (((0,), (0,)), ((), ())), preferred_element_type=f32)


def shaped(shape, dtype=bf16):
    return jax.ShapeDtypeStruct(shape, dtype)


def fixed(shape):
    return pl.BlockSpec(shape, lambda i: (0,) * len(shape))


def by_rows(rows, columns, first=0):
    return pl.BlockSpec((rows, columns), lambda i: (i + first, 0))


SCALARS = pl.BlockSpec(memory_space=pltpu.SMEM)
X, CORE, Y, Z = range(4)


FLOPS_PER_US = 500 * 10**6


class Order:
    def __init__(self):
        self.due = []

    def wait(self, *arrays):
        self.due += arrays


def call(order, body, name, us, grid, ins, outs, scratch=(), aliases=()):
    after = order.due
    n = len(after)

    def kernel(*refs):
        body(*refs[n:])

    result = pl.pallas_call(
        kernel,
        grid=(grid,),
        in_specs=[pl.BlockSpec(memory_space=pl.ANY)] * n + [s for _, s in ins],
        out_specs=[s for _, s in outs],
        out_shape=[s for s, _ in outs],
        scratch_shapes=list(scratch),
        input_output_aliases={n + a: b for a, b in aliases},
        compiler_params=pltpu.CompilerParams(vmem_limit_bytes=VMEM_CAP),
        cost_estimate=pl.CostEstimate(flops=int(us * FLOPS_PER_US), bytes_accessed=10**5, transcendentals=0),
        name=name,
    )(*after, *[a for a, _ in ins])
    order.due = [result[0]]
    return result


def first_lanes(order, v, lanes):
    def body(v, out):
        out[...] = v[...]

    spec = fixed((v.shape[0], lanes))
    return call(order, body, "first_lanes", 0.1, 1, [(v, spec)], [(shaped((v.shape[0], lanes)), spec)])[0]


def gate(order, v):
    anywhere = pl.BlockSpec(memory_space=pl.ANY)

    def body(v, out):
        pass

    return call(order, body, "gate", 1, 1, [(v, anywhere)], [(shaped(v.shape, v.dtype), anywhere)], (), [(0, 0)])[0]


def widths_of(rows):
    if rows == 1216:
        return [(256, 0), (384, 256), (384, 640), (192, 1024)]
    cuts, at = [], 0
    while at < rows:
        w = min(256, rows - at)
        cuts.append((w, at))
        at += w
    return cuts


def split_weights(order, where, w_gate, w_up, w_down, cuts):
    own, d = w_gate.shape[0], w_down.shape[1]
    ff = w_down.shape[0]
    n = len(cuts)

    def body(where, gate, up, down, *refs):
        sends, mine, downs = refs[:n], refs[n : 2 * n], refs[2 * n :]

        def put(ref, core, cut):
            w, off = cut
            for m, src in enumerate((gate, up)):
                for side in (0, 1):
                    lo = (2 * m + side) * w
                    a = (2 * side + core) * ff + off
                    ref[:, lo : lo + w] = src[:, a : a + w]

        for core in (0, 1):

            @pl.when(where[CORE] == core)
            def _():
                for cut, ref, send in zip(cuts, mine, sends):
                    put(ref, core, cut)
                    put(send, 1 - core, cut)

        for (w, off), part in zip(cuts, downs):
            for lo in range(0, w, 128):
                hi = min(lo + 128, w)
                part[:, lo:hi] = down[off + lo : off + hi, :].T

    whole = lambda a: (a, fixed(a.shape))
    return call(
        order,
        body,
        "split_weights",
        0.1,
        1,
        [(where, SCALARS)] + [whole(a) for a in (w_gate, w_up, w_down)],
        [(shaped((own, 4 * w)), fixed((own, 4 * w))) for w, _ in cuts]
        + [(shaped((own, 4 * w)), fixed((own, 4 * w))) for w, _ in cuts]
        + [(shaped((d, w)), fixed((d, w))) for w, _ in cuts],
    )


def pack_weights(order, where, core_rows, mine, downs, groups, extra=()):
    own = mine[0].shape[0]
    widths = [m.shape[1] // 4 for m in mine]
    n = len(mine)

    def body(where, *refs):
        cores, refs = refs[:n], refs[n:]
        mine, downs, extras, outs = refs[:n], refs[n : 2 * n], refs[2 * n : 2 * n + len(extra)], refs[2 * n + len(extra) :]
        for group, out in zip(groups, outs):
            at6 = 0
            for k in group:
                w = widths[k]

                @pl.when(where[CORE] == where[Y])
                def _():
                    out[:, at6 : at6 + 4 * w] = mine[k][...]

                @pl.when(where[CORE] != where[Y])
                def _():
                    out[:, at6 : at6 + 4 * w] = cores[k][...]

                for h in (0, 1):
                    rows = pl.ds(pl.multiple_of((2 * where[Y] + h) * own, 16), own)
                    out[:, at6 + (4 + h) * w : at6 + (5 + h) * w] = downs[k][rows, :]
                at6 += 6 * w
        at6 = sum(6 * widths[k] for k in groups[0])
        for e in extras:
            outs[0][:, at6 : at6 + e.shape[1]] = e[...]
            at6 += e.shape[1]

    whole = lambda a: (a, fixed(a.shape))
    totals = [sum(6 * widths[k] for k in group) for group in groups]
    totals[0] += sum(e.shape[1] for e in extra)
    return call(
        order,
        body,
        "pack_weights",
        0.1,
        1,
        [(where, SCALARS)] + [whole(a) for a in (*core_rows, *mine, *downs, *extra)],
        [(shaped((own, m)), fixed((own, m))) for m in totals],
    )


def side_by_side(order, parts):
    rows, width = parts[0].shape[0], sum(p.shape[1] for p in parts)

    def body(*refs):
        lo = 0
        for ref in refs[:-1]:
            refs[-1][:, lo : lo + ref.shape[1]] = ref[...]
            lo += ref.shape[1]

    return call(
        order,
        body,
        "side_by_side",
        1,
        1,
        [(p, fixed(p.shape)) for p in parts],
        [(shaped((rows, width)), fixed((rows, width)))],
    )[0]


def place_rows(where, refs, rows, target):
    x, c = where[0], where[1]
    for ref, s in zip(refs, (2 * x + c, 2 * (1 - x) + c, 2 * x + 1 - c, 2 * (1 - x) + 1 - c)):
        target[pl.ds(pl.multiple_of(s * rows, 16), rows), :] = ref


def project(order, where, tokens, gain, own_w, across_w, core_w, far_w, bias, cos, sin):
    t, d = tokens.shape
    rows, width = own_w.shape
    kw = KVHEADS * HD
    qw = width - 2 * kw

    def body(where, tokens, gain, own_w, across_w, core_w, far_w, bias, cos, sin, normed, q, kx, vx, vz, w):
        @pl.when(pl.program_id(0) == 0)
        def _():
            place_rows(where, (own_w[...], across_w[...], core_w[...], far_w[...]), rows, w)

        v = tokens[...].astype(f32)
        inverse = lax.rsqrt(jnp.mean(v * v, axis=-1, keepdims=True) + epsilon)
        n = (v * inverse * gain[...]).astype(bf16)
        normed[...] = n
        lanes = lax.broadcasted_iota(jnp.int32, (TILE, 2 * HD), 1)
        left = lanes < HD
        c, s = cos[...], sin[...]
        for p in range(width // 128):
            at = slice(p * 128, p * 128 + 128)
            if p % 2 == 0:
                two = nn(n, w[:, p * 128 : p * 128 + 256])
            u = two[:, p % 2 * 128 : p % 2 * 128 + 128] + bias[:, at]
            if p * 128 < qw + kw:
                u = (u * c + swap_halves(u, lanes) * s).astype(bf16)
            if p * 128 < qw:
                q[:, at] = (u.astype(f32) * 0.125).astype(bf16)
                continue
            u = u.astype(f32)
            turned = pltpu.roll(u, HD, 1)
            first, second = (kx, 0.0), (vx, 1.0)
            for ref, fill in (first,) if p * 128 < qw + kw else (second, (vz, 0.0)):
                ref[0] = jnp.where(left, u, fill).astype(bf16)
                ref[1] = jnp.where(left, fill, turned).astype(bf16)
                ref[2] = jnp.where(left, turned, fill).astype(bf16)
                ref[3] = jnp.where(left, fill, u).astype(bf16)

    heads = (shaped((4, t, 2 * HD)), pl.BlockSpec((4, TILE, 2 * HD), lambda i: (0, i, 0)))
    return call(
        order,
        body,
        "project",
        0.1,
        t // TILE,
        [
            (where, SCALARS),
            (tokens, by_rows(TILE, d)),
            (gain, fixed(gain.shape)),
            (own_w, fixed(own_w.shape)),
            (across_w, fixed(across_w.shape)),
            (core_w, fixed(core_w.shape)),
            (far_w, fixed(far_w.shape)),
            (bias, fixed(bias.shape)),
            (cos, by_rows(TILE, 2 * HD)),
            (sin, by_rows(TILE, 2 * HD)),
        ],
        [
            (shaped((t, d)), by_rows(TILE, d)),
            (shaped((t, qw)), by_rows(TILE, qw)),
            heads,
            heads,
            heads,
            (shaped((d, width)), fixed((d, width))),
        ],
    )


def swap_halves(v, lanes):
    half = HD // 2
    return jnp.where(lanes % HD < half, pltpu.roll(v, v.shape[1] - half, 1), pltpu.roll(v, half, 1))


def kinds_of(pair):
    return [2 * (2 * pair + side >= GROUP).astype(jnp.int32) + side for side in (0, 1)]


def attend(order, segments, q, kx, vx, first, last):
    t = q.shape[0]
    tiles = t // TILE

    def body(segc, segr, q, kx, vx, o, o_rest, linv, *rest):
        probs, bias = rest[:tiles], rest[tiles]
        step = pl.program_id(0)
        pair = step + first

        @pl.when(step == 0)
        def _():
            for i in range(tiles):
                w = (i + 1) * TILE
                rows = lax.broadcasted_iota(jnp.int32, (TILE, w), 0) + i * TILE
                cols = lax.broadcasted_iota(jnp.int32, (TILE, w), 1)
                ok = (segc[i * TILE : w, :] == segr[:, :w]) & (cols <= rows)
                bias[i * TILE : w, :w] = jnp.where(ok, 0.0, -1e30)

        left = lax.broadcasted_iota(jnp.int32, (TILE, 2 * HD), 1) < HD
        kinds = kinds_of(pair)
        for i in range(tiles):
            w = (i + 1) * TILE
            block = q[i * TILE : w, :]
            mixed = []
            for side in (0, 1):
                s = nt(block, kx[kinds[side], :w, :]) + bias[i * TILE : w, :w]
                e = jnp.exp(s - jnp.max(s, axis=-1, keepdims=True)).astype(bf16)
                for j in range(i + 1):
                    probs[j][side, (i - j) * TILE : (i - j + 1) * TILE, :] = e[:, j * TILE : (j + 1) * TILE]
                mixed.append(nn(e, vx[kinds[side], :w, :]))
            totals = jnp.where(left, pltpu.roll(mixed[0], HD, 1), pltpu.roll(mixed[1], HD, 1))
            inverse = 1.0 / totals
            out = jnp.where(left, mixed[0], mixed[1]) * inverse
            low = out.astype(bf16)
            o[i * TILE : w, :] = low
            o_rest[i * TILE : w, :] = (out - low.astype(f32)).astype(bf16)
            linv[i * TILE : w, :] = inverse

    count = last - first
    lane = pl.BlockSpec((t, 2 * HD), lambda p: (0, p + first))
    out_lane = pl.BlockSpec((t, 2 * HD), lambda p: (0, p))
    out = (t, count * 2 * HD)
    pshape = [(2 * count, t - j * TILE, TILE) for j in range(tiles)]
    return call(
        order,
        body,
        "attend",
        0.1,
        count,
        [
            (segments.reshape(t, 1), fixed((t, 1))),
            (segments.reshape(1, t), fixed((1, t))),
            (q, lane),
            (kx, fixed(kx.shape)),
            (vx, fixed(vx.shape)),
        ],
        [(shaped(out), out_lane), (shaped(out), out_lane), (shaped(out, f32), out_lane)]
        + [(shaped(s), pl.BlockSpec((2,) + s[1:], lambda p: (p, 0, 0))) for s in pshape],
        [pltpu.VMEM((t, t), f32)],
    )


def attend_back(order, q, do, o, o_rest, kx, vz, cos, sin, probs, base, first, last, running=(), finish=False):
    t = q.shape[0]
    tiles = t // TILE
    count = last - first

    def body(q, do, o, o_rest, kx, vz, cos, sin, *rest):
        probs, rest = rest[:tiles], rest[tiles:]
        if running:
            dk_in, dv_in, rest = rest[0], rest[1], rest[2:]
        dq, dk, dv, ds0, ds1, dkacc, dvacc = rest
        step = pl.program_id(0)
        pair = step + first

        @pl.when(step == 0)
        def _():
            dkacc[...] = jnp.zeros_like(dkacc)
            dvacc[...] = jnp.zeros_like(dvacc)

        left = lax.broadcasted_iota(jnp.int32, (t, 2 * HD), 1) < HD
        along = do[...].astype(f32) * (o[...].astype(f32) + o_rest[...].astype(f32))
        inner = [
            jnp.sum(jnp.where(left, along, 0.0), axis=-1, keepdims=True),
            jnp.sum(jnp.where(left, 0.0, along), axis=-1, keepdims=True),
        ]
        kinds = kinds_of(pair)
        for side, ds in ((0, ds0), (1, ds1)):
            kind = kinds[side]
            for j in range(tiles):
                lo = j * TILE
                p = probs[j][side]
                dp = nt(do[lo:, :], vz[kind, lo : lo + TILE, :])
                d = (p.astype(f32) * (dp - inner[side][lo:])).astype(bf16)
                ds[lo:, lo : lo + TILE] = d
                dkacc[kind, lo : lo + TILE, :] += tn(d, q[lo:, :])
                dvacc[kind, lo : lo + TILE, :] += tn(p, do[lo:, :])
        lanes = lax.broadcasted_iota(jnp.int32, (TILE, 2 * HD), 1)
        for i in range(tiles):
            w = (i + 1) * TILE
            at = slice(i * TILE, w)
            g = (nn(ds0[at, :w], kx[kinds[0], :w, :]) + nn(ds1[at, :w], kx[kinds[1], :w, :])) * 0.125
            dq[at, :] = (g * cos[at, :] - swap_halves(g, lanes) * sin[at, :]).astype(bf16)

        @pl.when(step == count - 1)
        def _():
            one = lambda a: jnp.where(left, a[0] + pltpu.roll(a[1], HD, 1), pltpu.roll(a[2], HD, 1) + a[3])
            g, gv = one(dkacc), one(dvacc)
            if running:
                g, gv = g + dk_in[...], gv + dv_in[...]
            if finish:
                lanes = lax.broadcasted_iota(jnp.int32, (t, 2 * HD), 1)
                g = g * cos[...] - swap_halves(g, lanes) * sin[...]
            dk[...] = g.astype(dk.dtype)
            dv[...] = gv.astype(dv.dtype)

    lane = pl.BlockSpec((t, 2 * HD), lambda p: (0, p + first))
    out_lane = pl.BlockSpec((t, 2 * HD), lambda p: (0, p))
    part_lane = pl.BlockSpec((t, 2 * HD), lambda p: (0, p + first - base))
    wide = (4, t, 2 * HD)
    sums = (shaped((t, 2 * HD), bf16 if finish else f32), fixed((t, 2 * HD)))
    return call(
        order,
        body,
        "attend_back",
        0.1,
        count,
        [(q, lane), (do, part_lane), (o, part_lane), (o_rest, part_lane), (kx, fixed(wide)), (vz, fixed(wide))]
        + [(cos, fixed(cos.shape)), (sin, fixed(sin.shape))]
        + [(p, pl.BlockSpec((2,) + p.shape[1:], lambda i: (i + first - base, 0, 0))) for p in probs]
        + [(r, fixed(r.shape)) for r in running],
        [(shaped((t, count * 2 * HD)), out_lane), sums, sums],
        [pltpu.VMEM((t, t), bf16)] * 2 + [pltpu.VMEM(wide, f32)] * 2,
    )


def join_output(order, where, tokens, mixed, own_w, across, core, gain):
    t, d = tokens.shape
    steps = t // TILE
    rows = own_w.shape[0]
    n = len(mixed)

    def body(where, tokens, own_w, across, core, gain, *refs):
        mixed, resid, w, normed = refs[:n], refs[n], refs[n + 1], refs[n + 2 :]

        @pl.when(pl.program_id(0) == 0)
        def _():
            lo = across.shape[1] - 2 * d
            place_rows(where, (own_w[...], across[:, lo : lo + d], core[...], across[:, lo + d :]), rows, w)

        v, lo = tokens[...].astype(f32), 0
        for m in mixed:
            v = v + nn(m[...], w[lo : lo + m.shape[1], :])
            lo += m.shape[1]
        resid[...] = v
        inverse = lax.rsqrt(jnp.mean(v * v, axis=-1, keepdims=True) + epsilon)
        low = (v * inverse * gain[...]).astype(bf16)
        for k, out in enumerate(normed):

            @pl.when(pl.program_id(0) // (steps // 2) == k)
            def _():
                out[...] = low

    return call(
        order,
        body,
        "join_output",
        0.1,
        steps,
        [(where, SCALARS), (tokens, by_rows(TILE, d))]
        + [(a, fixed(a.shape)) for a in (own_w, across, core, gain)]
        + [(m, by_rows(TILE, m.shape[1])) for m in mixed],
        [
            (shaped((t, d), f32), by_rows(TILE, d)),
            (shaped((4 * rows, d)), fixed((4 * rows, d))),
        ]
        + [
            (shaped((t // 2, d)), pl.BlockSpec((TILE, d), lambda i, k=k: (jnp.clip(i - k * steps // 2, 0, steps // 2 - 1), 0)))
            for k in (0, 1)
        ],
    )


def ffn_part(order, where, n2, dy, mine, core_rows, x_rows, y_rows, down, cut, at6):
    t, d = dy[0].shape
    w, off = cut
    tt = t // 2
    own = mine.shape[0]
    half = d // 2
    steps = t // tt

    def body(where, dya, dyb, mine, core_rows, x_rows, y_rows, down, *refs):
        n2, (hid, dgu, keep, send, weights, acc, wt, tokens, copied, arrived) = refs[: len(refs) - 10], refs[-10:]
        step = pl.program_id(0)
        x, c, y = where[0], where[1], where[2]
        copy_out = pltpu.make_async_copy(wt, weights, copied)

        def fetch(k):
            return pltpu.make_async_copy(n2[k], tokens.at[k % 2], arrived.at[k % 2])

        @pl.when(step == 0)
        def _():
            fetch(0).start()

        for k in range(1, len(n2)):

            @pl.when(step == k - 1)
            def _():
                fetch(k).start()

        @pl.when(step == 0)
        def _():
            def put(ref, s, at=at6):
                wt[pl.ds(pl.multiple_of(s * own, 16), own), : 4 * w] = ref[:, at : at + 4 * w]

            put(mine, 2 * x + c, 0)
            put(core_rows, 2 * x + 1 - c, 0)
            put(x_rows, 2 * (1 - x) + y)
            put(y_rows, 2 * (1 - x) + 1 - y)
            for side in (0, 1):

                @pl.when(x == side)
                def _():
                    wt[:, (4 + side) * w : (5 + side) * w] = down[...]
                    lo = (5 - side) * w
                    for ref, h in ((x_rows, y), (y_rows, 1 - y)):
                        for part in (0, 1):
                            at = pl.ds(pl.multiple_of((2 * h + part) * own, 16), own)
                            wt[at, lo : lo + w] = ref[:, at6 + (4 + part) * w : at6 + (5 + part) * w]

            copy_out.start()

        for k in range(len(n2)):

            @pl.when(step == k)
            def _():
                fetch(k).wait()

        a = tokens[lax.rem(step, 2)]
        old = lambda at: jnp.where(step == 0, 0.0, acc[:, at])
        b = jnp.where(step < steps, dya[...], dyb[...])
        for lo in range(0, 2 * w, BLK):
            hi = min(lo + BLK, 2 * w)
            g, u, v = slice(lo, hi), slice(2 * w + lo, 2 * w + hi), slice(4 * w + lo, 4 * w + hi)
            both = nn(a, jnp.concatenate([wt[:, g], wt[:, u]], 1))
            gate, up, dh = both[:, : hi - lo], both[:, hi - lo :], nn(b, wt[:, v])
            sig = jax.nn.sigmoid(gate)
            silu = gate * sig
            h = (silu * up).astype(bf16)
            d_gate = (dh * up * (sig + silu * (1.0 - sig))).astype(bf16)
            d_up = (dh * silu).astype(bf16)
            hid[:, g] = h
            dgu[:, g] = d_gate
            dgu[:, u] = d_up
            acc[:, v] = old(v) + tn(b, h)
            acc[:, g] = old(g) + tn(a, d_gate)
            acc[:, u] = old(u) + tn(a, d_up)

        @pl.when(step == 2 * steps - 1)
        def _():
            copy_out.wait()
            for ref, side in ((keep, x), (send, 1 - x)):
                at = pl.ds(pl.multiple_of(side * half, 16), half)
                ref[:, : 4 * w] = acc[at, : 4 * w].astype(bf16)
            for side in (0, 1):

                @pl.when(x == side)
                def _():
                    for ref, s in ((keep, side), (send, 1 - side)):
                        lanes = slice((4 + s) * w, (5 + s) * w)
                        ref[:, 4 * w : 5 * w] = acc[:half, lanes].astype(bf16)
                        ref[:, 5 * w :] = acc[half:, lanes].astype(bf16)

    whole = lambda a: (a, fixed(a.shape))
    early = pl.BlockSpec((tt, d), lambda i: (jnp.minimum(i, steps - 1), 0))
    late = pl.BlockSpec((tt, d), lambda i: (jnp.maximum(i - steps, 0), 0))
    return call(
        order,
        body,
        "ffn_part",
        5 + w // 16 if off else 0.1,
        2 * steps,
        [(where, SCALARS), (dy[0], early), (dy[1], late)]
        + [whole(a) for a in (mine, core_rows, x_rows, y_rows, down)]
        + [(a, pl.BlockSpec(memory_space=pl.ANY)) for a in n2],
        [
            (shaped((2 * t, 2 * w)), by_rows(tt, 2 * w)),
            (shaped((2 * t, 4 * w)), by_rows(tt, 4 * w)),
            (shaped((half, 6 * w)), fixed((half, 6 * w))),
            (shaped((half, 6 * w)), fixed((half, 6 * w))),
            (shaped((d, 6 * w)), pl.BlockSpec(memory_space=pl.ANY)),
        ],
        [
            pltpu.VMEM((d, 6 * w), f32),
            pltpu.VMEM((d, 6 * w), bf16),
            pltpu.VMEM((2, tt, d), bf16),
            pltpu.SemaphoreType.DMA(()),
            pltpu.SemaphoreType.DMA((2,)),
        ],
    )


def sum_parts(order, name, us, parts, weights, lanes, block, tokens, apart=False, add=None, pieces=(), tt=256):
    d = weights[0].shape[0]
    t = parts[0].shape[0] // 2
    n = len(parts)
    steps = t // tt
    k = len(tokens)

    def body(*refs):
        step = pl.program_id(0)
        total = None
        for part, weight in zip(refs[:n], refs[n : 2 * n]):
            s = nt(part[...], weight[...])
            total = s if total is None else total + s
        refs = refs[2 * n :]
        if pieces:
            more, others, refs = refs[0], refs[1 : 1 + len(pieces)], refs[1 + len(pieces) :]
            other = refs[-1]
            for at, ref in enumerate(others):

                @pl.when(step == at)
                def _():
                    other[...] = ref[...]

            total = total + more[...] + other[...].astype(f32)
        for out, (first, count, _) in zip(refs, outs):

            @pl.when((step >= first) & (step < first + count))
            def _():
                out[...] = total.astype(out.dtype)

    def spec(first, count):
        return pl.BlockSpec((tt, d), lambda i: (jnp.clip(i - first, 0, count - 1), 0))

    outs = []
    for at, half in enumerate(tokens):
        if half and apart:
            outs += [(at * steps + k, 1, bf16) for k in range(steps)]
        else:
            outs.append((at * steps, steps, bf16 if half or pieces else f32))

    start = tokens[0] * steps
    return call(
        order,
        body,
        name,
        us,
        k * steps,
        [(p, pl.BlockSpec((tt, p.shape[1]), lambda i: ((i + start) % (2 * steps), 0))) for p in parts]
        + [(w, pl.BlockSpec((d, n), lambda i: (0, block))) for w, n in zip(weights, lanes)]
        + ([(add, by_rows(tt, d))] if pieces else [])
        + [(p, fixed(p.shape)) for p in pieces],
        [(shaped((count * tt, d), kind), spec(first, count)) for first, count, kind in outs],
        [pltpu.VMEM((tt, d), bf16)] if pieces else [],
    )


def turn_back(order, dn2, dn2_other, residual, cotangent, gain, full_output, inverse_sums):
    t, d = residual.shape
    n = len(inverse_sums)

    steps = len(dn2_other)

    def body(dn2, resid, dy, gain, w, *refs):
        others, refs = refs[:steps], refs[steps:]
        sums, (d_resid, d_attn, grad_gain), scaled, other = refs[:n], refs[n : n + 3], refs[n + 3 : -1], refs[-1]
        step = pl.program_id(0)
        for k, ref in enumerate(others):

            @pl.when(step == k)
            def _():
                other[...] = ref[...]

        @pl.when(step == 0)
        def _():
            grad_gain[...] = jnp.zeros_like(grad_gain)

        up = dn2[...] + other[...].astype(f32)
        grad, gains = norm_back(resid[...], gain[...], up)
        grad_gain[...] += gains
        total = dy[...].astype(f32) + grad
        d_resid[...] = total
        low = total.astype(bf16)
        d_attn[...] = low
        d_mixed = nt(low, w[...]).astype(bf16).astype(f32)
        lo = 0
        for linv, out in zip(sums, scaled):
            hi = lo + linv.shape[1]
            out[...] = (d_mixed[:, lo:hi] * linv[...]).astype(bf16)
            lo = hi

    rows = by_rows(TILE, d)
    return call(
        order,
        body,
        "turn_back",
        8,
        steps,
        [(a, rows) for a in (dn2, residual, cotangent)]
        + [(gain, fixed(gain.shape)), (full_output, fixed(full_output.shape))]
        + [(a, fixed(a.shape)) for a in dn2_other]
        + [(a, by_rows(TILE, a.shape[1])) for a in inverse_sums],
        [(shaped((t, d), f32), rows), (shaped((t, d)), rows), (shaped((1, d), f32), fixed((1, d)))]
        + [(shaped((t, a.shape[1])), by_rows(TILE, a.shape[1])) for a in inverse_sums],
        [pltpu.VMEM((TILE, d), bf16)],
    )


def weight_grads(order, where, pairs, shares):
    d = sum(a.shape[1] for a in pairs[0][0])
    width = sum(g.shape[1] for _, g in pairs)
    own = d // 4
    lefts = []
    for pieces, _ in pairs:
        lefts += [a for a in pieces if not any(a is b for b in lefts)]
    rights = [g for _, g in pairs]
    place = [[next(i for i, b in enumerate(lefts) if b is a) for a in pieces] for pieces, _ in pairs]

    def body(where, *refs):
        left, right, refs = refs[: len(lefts)], refs[len(lefts) : len(lefts) + len(rights)], refs[len(lefts) + len(rights) :]
        keep, sends, grad = refs[0], refs[1:-1], refs[-1]
        c = where[CORE]
        lo = 0
        for spots, g in zip(place, right):
            hi = lo + g.shape[1]
            at = 0
            for i in spots:
                grad[at : at + left[i].shape[1], lo:hi] = tn(left[i][...], g[...]).astype(bf16)
                at += left[i].shape[1]
            lo = hi
        for side in (0, 1):
            rows = lambda core: pl.ds(pl.multiple_of((2 * side + core) * own, 16), own)
            at = slice(side * own, (side + 1) * own)
            keep[at, :] = grad[rows(c), :]
            lo = 0
            for ref in sends:
                ref[at, :] = grad[rows(1 - c), lo : lo + ref.shape[1]]
                lo += ref.shape[1]

    out = lambda lanes: (shaped((2 * own, lanes)), fixed((2 * own, lanes)))
    return call(
        order,
        body,
        "weight_grads",
        0.1,
        1,
        [(where, SCALARS)] + [(a, fixed(a.shape)) for a in (*lefts, *rights)],
        [out(lanes) for lanes in (width, *shares)],
        [pltpu.VMEM((d, width), bf16)],
    )


def finish_tokens(order, tokens, gain, d_parts, full_qkv, d_resid):
    t, d = tokens.shape
    n = len(d_parts)
    width = full_qkv.shape[1]

    def body(tokens, gain, w, d_resid, *refs):
        parts, out, grad_gain, sums = refs[:n], refs[n], refs[n + 1], refs[n + 2]

        @pl.when(pl.program_id(0) == 0)
        def _():
            grad_gain[...] = jnp.zeros_like(grad_gain)
            sums[...] = jnp.zeros_like(sums)

        total, lo = None, 0
        for part in parts:
            hi = lo + part.shape[1]
            p = part[...]
            sums[:, lo:hi] += jnp.sum(p.astype(f32), axis=0, keepdims=True)
            s = nt(p, w[:, lo:hi])
            total = s if total is None else total + s
            lo = hi
        grad, gains = norm_back(tokens[...].astype(f32), gain[...], total)
        grad_gain[...] += gains
        out[...] = d_resid[...] + grad

    rows = by_rows(TILE, d)
    return call(
        order,
        body,
        "finish_tokens",
        0.1,
        t // TILE,
        [(tokens, rows), (gain, fixed(gain.shape)), (full_qkv, fixed(full_qkv.shape)), (d_resid, rows)]
        + [(p, by_rows(TILE, p.shape[1])) for p in d_parts],
        [(shaped((t, d), f32), rows), (shaped((1, d), f32), fixed((1, d))), (shaped((1, width), f32), fixed((1, width)))],
    )


def assemble(order, where, halves, others, cores, cuts, ff):
    own = halves[0].shape[0]
    d = 4 * own
    n = len(cuts)
    steps = d // 128
    block = own // steps

    def body(where, *refs):
        halves, others, cores = refs[:n], refs[n : 2 * n], refs[2 * n : 3 * n]
        gate, up, down, down_t = refs[3 * n :]
        step = pl.program_id(0)
        c, y = where[1], where[2]
        rows = pl.ds(pl.multiple_of(step * block, 16), block)

        @pl.when(step == 0)
        def _():
            for (w, off), a, b in zip(cuts, halves, others):
                for ref, h in ((a, y), (b, 1 - y)):
                    for part in (0, 1):
                        at = pl.ds(pl.multiple_of((2 * part + h) * own, 16), own)
                        down_t[at, off : off + w] = ref[:, (4 + part) * w : (5 + part) * w]

        for core in (0, 1):
            for (w, off), a, b, o in zip(cuts, halves, others, cores):

                def put(ref, to):
                    for m, out in enumerate((gate, up)):
                        for side in (0, 1):
                            at = (2 * side + to) * ff + off
                            lo = (2 * m + side) * w
                            out[:, at : at + w] = ref[rows, lo : lo + w].astype(f32)

                @pl.when((c == core) & (c == y))
                def _():
                    put(a, core)

                @pl.when((c == core) & (c != y))
                def _():
                    put(b, core)

                @pl.when(c != core)
                def _():
                    put(o, core)

        down[...] = down_t[pl.ds(pl.multiple_of(step * 128, 128), 128), :].astype(f32).T

    whole = lambda a: (a, fixed(a.shape))
    return call(
        order,
        body,
        "assemble",
        11,
        steps,
        [(where, SCALARS)] + [whole(a) for a in (*halves, *others, *cores)],
        [
            (shaped((own, 4 * ff), f32), by_rows(block, 4 * ff)),
            (shaped((own, 4 * ff), f32), by_rows(block, 4 * ff)),
            (shaped((ff, d), f32), pl.BlockSpec((ff, 128), lambda i: (0, i))),
        ],
        [pltpu.VMEM((d, ff), bf16)],
    )


class Links:
    def __init__(self, shards, replicas):
        self.shards, self.replicas = shards, replicas
        s, r = lax.axis_index("shard"), lax.axis_index("replica")
        self.where = jnp.stack([s // 2, s % 2, r % 2, r // 2 % 2]).astype(jnp.int32)

    def core(self, v):
        return lax.ppermute(v, "shard", [(i, i ^ 1) for i in range(self.shards)])

    def across(self, v):
        return lax.ppermute(v, "shard", [(i, i ^ 2) for i in range(self.shards)])

    def beside(self, v):
        return lax.ppermute(v, "replica", [(i, i ^ 1) for i in range(self.replicas)])

    def far(self, v, bit):
        return lax.ppermute(v, "replica", [(i, i ^ bit) for i in range(self.replicas)])

    def along(self, v):
        return lax.psum(v, "replica", axis_index_groups=[list(range(y, self.replicas, 2)) for y in (0, 1)])

    def bits(self):
        bit = 2
        while bit < self.replicas:
            yield bit
            bit *= 2


def split_sum(axis, keep, *got):
    half = keep.shape[0] // 2
    shape = shaped((half, keep.shape[1]), keep.dtype)

    def body(where, keep, *refs):
        *got, mine, send = refs
        n = where[axis]
        for ref, h in ((mine, n), (send, 1 - n)):
            at = pl.ds(pl.multiple_of(h * half, 16), half)
            lo = 0
            for g in got:
                hi = lo + g.shape[1]
                ref[:, lo:hi] = (keep[at, lo:hi].astype(f32) + g[at, :].astype(f32)).astype(ref.dtype)
                lo = hi

    return body, [(a, fixed(a.shape)) for a in (keep, *got)], [shape, shape]


def whole_sum(v, got):
    def body(where, v, got, out):
        out[...] = (v[...].astype(f32) + got[...].astype(f32)).astype(out.dtype)

    return body, [(v, fixed(v.shape)), (got, fixed(got.shape))], [shaped(v.shape, v.dtype)]


def in_order(axis, mine, other, dtype=bf16):
    rows, width = mine.shape

    def body(where, mine, other, out):
        n = where[axis]
        out[pl.ds(pl.multiple_of(n * rows, 16), rows), :] = mine[...].astype(dtype)
        out[pl.ds(pl.multiple_of((1 - n) * rows, 16), rows), :] = other[...].astype(dtype)

    return body, [(mine, fixed(mine.shape)), (other, fixed(other.shape))], [shaped((2 * rows, width), dtype)]


def in_order_lanes(axis, mine, other, widths):
    rows = mine.shape[0]

    def body(where, mine, other, *outs):
        n = where[axis]
        lo = 0
        for out in outs:
            hi = lo + out.shape[1]
            out[pl.ds(pl.multiple_of(n * rows, 16), rows), :] = mine[:, lo:hi].astype(f32)
            out[pl.ds(pl.multiple_of((1 - n) * rows, 16), rows), :] = other[:, lo:hi].astype(f32)
            lo = hi

    return (
        body,
        [(mine, fixed(mine.shape)), (other, fixed(other.shape))],
        [shaped((2 * rows, w), f32) for w in widths],
    )


def lanes_sum(v, got, widths):
    def body(where, v, got, *outs):
        lo = 0
        for out in outs:
            hi = lo + out.shape[0]
            out[...] = (v[:, lo:hi] + got[:, lo:hi])[0]
            lo = hi

    return body, [(v, fixed(v.shape)), (got, fixed(got.shape))], [shaped((w,), v.dtype) for w in widths]


def rows_for_core(half, other, lanes):
    spec = fixed((half.shape[0], lanes))

    def body(where, half, other, out):
        same = where[CORE] == where[Y]

        @pl.when(same)
        def _():
            out[...] = other[...]

        @pl.when(jnp.logical_not(same))
        def _():
            out[...] = half[...]

    return body, [(half, spec), (other, spec)], [shaped((half.shape[0], lanes))]


GATE = "gate"


def advance(order, where, chains, us=2):
    chains = [chain for chain in chains if chain.asked is not None]
    for chain in [chain for chain in chains if chain.asked[0] == GATE]:
        chains.remove(chain)
        chain.give([gate(order, chain.asked[1])])
    if not chains:
        return
    asked = [chain.asked for chain in chains]
    n_in = sum(len(ins) for _, ins, _ in asked)

    def body(where, *refs):
        ins, outs = refs[:n_in], refs[n_in:]
        for part, i, o in asked:
            part(where, *ins[: len(i)], *outs[: len(o)])
            ins, outs = ins[len(i) :], outs[len(o) :]

    results = call(
        order,
        body,
        "sums",
        us,
        1,
        [(where, SCALARS)] + [pair for _, i, _ in asked for pair in i],
        [(shape, fixed(shape.shape)) for _, _, o in asked for shape in o],
    )
    for chain, (_, _, o) in zip(chains, asked):
        chain.give(results[: len(o)])
        results = results[len(o) :]


class Chain:
    def __init__(self, steps):
        self.steps = steps
        self.result = None
        self.asked = next(steps)

    def give(self, results):
        try:
            self.asked = self.steps.send(results)
        except StopIteration as stop:
            self.asked, self.result = None, stop.value


def replica_steps(order, links, mine, send, how):
    bits = list(links.bits())
    if how == "halves" and bits:
        mine, send = yield split_sum(Z, mine, links.beside(send))
        (mine,) = yield whole_sum(mine, links.far(send, bits[0]))
        for bit in bits[1:]:
            (mine,) = yield whole_sum(mine, links.far(mine, bit))
        (mine,) = yield in_order(Z, mine, links.far(mine, bits[0]))
    else:
        (mine,) = yield whole_sum(mine, links.beside(send))
        if how == "offload":
            (mine,) = yield GATE, links.along(mine)
        else:
            for bit in bits:
                (mine,) = yield whole_sum(mine, links.far(mine, bit))
    return mine, links.beside(mine)


def ffn_steps(order, links, keep, send, w, how):
    mine, send = yield split_sum(Y, keep, links.across(send))
    half, other = yield from replica_steps(order, links, mine, send, how)
    (rows,) = yield rows_for_core(half, other, 4 * w)
    (cores,) = yield GATE, links.core(rows)
    return half, other, cores


def owned_steps(order, links, keep, sends, how, widths):
    mine, send = yield split_sum(X, keep, *[links.core(send) for send in sends])
    mine, send = yield split_sum(Y, mine, links.across(send))
    half, other = yield from replica_steps(order, links, mine, send, how)
    return (yield in_order_lanes(Y, half, other, widths))


def beside_each_other(parts):
    def body(where, *refs):
        lo = 0
        for ref in refs[:-1]:
            refs[-1][:, lo : lo + ref.shape[1]] = ref[...]
            lo += ref.shape[1]

    width = sum(p.shape[1] for p in parts)
    return body, [(p, fixed(p.shape)) for p in parts], [shaped((parts[0].shape[0], width), parts[0].dtype)]


def small_steps(links, parts, widths):
    (v,) = yield beside_each_other(parts)
    moves = [links.core, links.across]
    moves += [functools.partial(links.far, bit=bit) for bit in links.bits()]
    moves.append(links.beside)
    for move in moves[:-1]:
        (v,) = yield whole_sum(v, move(v))
    return (yield lanes_sum(v, moves[-1](v), widths))


def norm_back(values, gain_vector, upstream):
    inverse = lax.rsqrt(jnp.mean(values * values, axis=-1, keepdims=True) + epsilon)
    scaled = upstream * gain_vector
    grad_gain = jnp.sum(upstream * values * inverse, axis=0, keepdims=True)
    correction = jnp.sum(scaled * values, axis=-1, keepdims=True) / values.shape[-1]
    return inverse * scaled - values * (inverse * inverse * inverse) * correction, grad_gain


def position_tables(doc_ids):
    t = doc_ids.shape[0]
    earlier = jnp.sum((doc_ids[None, :] < doc_ids[:, None]).astype(jnp.int32), axis=1)
    places = jnp.arange(t, dtype=jnp.int32) - earlier
    frequency = rope_base ** (-jnp.arange(0, HD, 2).astype(f32) / HD)
    angles = places.astype(f32)[:, None] * frequency[None, :]
    cosine, sine = jnp.cos(angles), jnp.sin(angles)
    return jnp.tile(cosine, (1, 4)), jnp.tile(jnp.concatenate([-sine, sine], 1), (1, 2))


def on_device(
    links_shape,
    tokens,
    segments,
    cotangent,
    gain_attn,
    gain_ffn,
    w_query,
    bias_query,
    w_key,
    bias_key,
    w_value,
    bias_value,
    w_output,
    w_gate,
    w_up,
    w_down,
):
    links = Links(*links_shape)
    order = Order()
    where = links.where
    t, d = tokens.shape
    qw, kw = w_query.shape[1], w_key.shape[1]
    doc_ids = segments[0]
    ff = w_down.shape[0]
    cuts = widths_of(ff)
    cos, sin = position_tables(doc_ids)
    gain_attn, gain_ffn = gain_attn[None, :], gain_ffn[None, :]
    pieces = range(len(cuts))
    stages = [[[0]], [[1], list(pieces[2:])]] if len(cuts) > 2 else [[[n] for n in pieces]]
    group_of = [number for number, group in enumerate(g for stage in stages for g in stage) for _ in group]

    own_qkv = side_by_side(order, [w_query, w_key, w_value])
    across_qkv, core_qkv = links.across(own_qkv), links.core(own_qkv)
    dy = (cotangent, links.core(cotangent))
    order.wait(cos, sin)
    mine, downs, core_rows, x_rows, y_rows, at6 = [], [], [], [], [], []

    def split_stage(stage):
        chosen = [cuts[n] for group in stage for n in group]
        k = len(chosen)
        parts = split_weights(order, where, w_gate, w_up, w_down, chosen)
        core_rows.extend(links.core(v) for v in parts[:k])
        mine.extend(parts[k : 2 * k])
        downs.extend(parts[2 * k :])

    def pack_stage(stage, extra=()):
        chosen = [n for group in stage for n in group]
        first = chosen[0]
        packed = pack_weights(
            order,
            where,
            [core_rows[n] for n in chosen],
            [mine[n] for n in chosen],
            [downs[n] for n in chosen],
            [[n - first for n in group] for group in stage],
            extra,
        )
        for group in stage:
            at6.extend(sum(6 * cuts[m][0] for m in group[:k]) for k in range(len(group)))
        x_rows.extend(links.across(v) for v in packed)

    def forward_rows(*groups):
        for g in groups:
            if g < len(x_rows) and g == len(y_rows):
                if g == 0:
                    forwarded = first_lanes(order, x_rows[0], sum(6 * cuts[n][0] for n in stages[0][0]))
                else:
                    forwarded = x_rows[g] = gate(order, x_rows[g])
                y_rows.append(links.beside(forwarded))

    split_stage(stages[0])
    core_output = links.core(w_output)
    across_qkv = gate(order, across_qkv)
    far_qkv = links.core(across_qkv)
    pack_stage(stages[0], [w_output, core_output])

    bias = jnp.concatenate([bias_query, bias_key, bias_value])[None, :]
    order.wait(dy[1])
    normed, queries, kx, vx, vz, full_qkv = project(
        order, where, tokens, gain_attn, own_qkv, across_qkv, core_qkv, far_qkv, bias, cos, sin
    )
    middle = 3
    for stage in stages[1:]:
        split_stage(stage)
    first_part = attend(order, doc_ids, queries, kx, vx, 0, middle)
    forward_rows(0)
    for stage in stages[1:]:
        pack_stage(stage)
    second_part = attend(order, doc_ids, queries, kx, vx, middle, PAIRS)
    order.wait(y_rows[0])
    mixed, mixed_rest, inverse_sums = zip(first_part[:3], second_part[:3])
    probs = (first_part[3:], second_part[3:])
    residual, full_output, *normed_two = join_output(
        order, where, tokens, mixed, w_output, x_rows[0], core_output, gain_ffn
    )
    n2 = [*normed_two, *[links.core(v) for v in normed_two]]

    forward_rows(1)

    chains, hids, dgus, weights = [], [], [], []
    how = ["whole"] + ["halves"] * (len(cuts) - 2) + ["whole"]

    def step(*which, us=2):
        advance(order, where, [chains[n] for n in which if n < len(chains)], us)

    for n in pieces:
        g = group_of[n]
        forward_rows(g)
        if n >= 2:
            step(0)
        hid, dgu, keep, send, weight = ffn_part(
            order, where, n2, dy, mine[n], core_rows[n], x_rows[g], y_rows[g], downs[n], cuts[n], at6[n]
        )
        hids.append(hid), dgus.append(dgu), weights.append(weight)
        chains.append(Chain(ffn_steps(order, links, keep, send, cuts[n][0], how[n])))
        if n == 0:
            forward_rows(2)

    step(0, 1)
    *dn2_send, dn2 = sum_parts(order, "back_tokens", 24, dgus, weights, [4 * w for w, _ in cuts], 0, (1, 0), True)
    dn2_other = [links.core(v) for v in dn2_send]
    step(0, 1, 2)
    d_resid, d_attn, grad_gain_ffn, *scaled = turn_back(
        order, dn2, dn2_other, residual, cotangent, gain_ffn, full_output, inverse_sums
    )
    step(1)

    out_keep, *out_sends = weight_grads(order, where, [(mixed, d_attn)], [d // 2 // 128 * 128, d - d // 2 // 128 * 128])
    n_out, n_qkv, n_small = (len(cuts) + n for n in range(3))
    chains.append(Chain(owned_steps(order, links, out_keep, out_sends, "whole", [d])))

    both = [(queries, scaled[n], mixed[n], mixed_rest[n], kx, vz, cos, sin, probs[n]) for n in (0, 1)]
    late = middle + (PAIRS - middle) // 2
    dq_first, *running = attend_back(order, *both[0], 0, 0, middle)
    step(2, 3, n_out, us=0.1)
    dq_second, *running = attend_back(order, *both[1], middle, middle, late, running)
    step(1, 2, us=0.1)
    dq_third, d_key, d_value = attend_back(order, *both[1], middle, late, PAIRS, running, True)
    d_parts = [dq_first, dq_second, dq_third, d_key, d_value]
    share = (qw + 2 * kw) // 3 // 128 * 128
    qkv_keep, *qkv_sends = weight_grads(
        order, where, [((normed,), p) for p in d_parts], [share, share, qw + 2 * kw - 2 * share]
    )
    chains.append(Chain(owned_steps(order, links, qkv_keep, qkv_sends, "whole", [qw, kw, kw])))
    step(0, 1, 2, 3, n_out, us=0.1)
    step(n_qkv, us=0.1)
    grad_tokens, grad_gain_attn, grad_biases = finish_tokens(order, tokens, gain_attn, d_parts, full_qkv, d_resid)
    chains.append(Chain(small_steps(links, [grad_gain_attn, grad_gain_ffn, grad_biases], [d, d, qw, kw, kw])))
    down_lanes = [2 * w for w, _ in cuts]
    out_other = [links.core(v) for v in sum_parts(order, "down_tokens", 0.1, hids, weights, down_lanes, 2, (1,), True)]
    step(0, 1, 2, 3, n_out, n_qkv, n_small, us=0.1)
    (output,) = sum_parts(order, "down_tokens", 20, hids, weights, down_lanes, 2, (0,), False, residual, out_other)
    step(n_qkv, n_small, us=20)
    step(1, 2, 3, n_qkv, n_small, us=20)
    step(3, n_out, n_qkv, n_small, us=20)
    while any(chain.result is None for chain in chains[: len(cuts)]):
        step(*range(len(cuts)), us=20)
    grad_gate, grad_up, grad_down = assemble(order, where, *zip(*(chain.result for chain in chains[: len(cuts)])), cuts, ff)
    while any(chain.result is None for chain in chains):
        step(*range(len(chains)), us=20)
    (grad_output,), grad_qkv, small = (chain.result for chain in chains[len(cuts) :])
    return (
        output,
        grad_tokens,
        small[0],
        small[1],
        grad_qkv[0],
        small[2],
        grad_qkv[1],
        small[3],
        grad_qkv[2],
        small[4],
        grad_output,
        grad_gate,
        grad_up,
        grad_down,
    )


def solution(mesh):
    tokens, rows, whole = P(("shard", "replica"), None), P("shard", None), P()
    return jax.shard_map(
        functools.partial(on_device, (mesh.shape["shard"], mesh.shape["replica"])),
        mesh=mesh,
        in_specs=(tokens, tokens, tokens, whole, whole, rows, whole, rows, whole, rows, whole, rows, rows, rows, rows),
        out_specs=(tokens, tokens, whole, whole, rows, whole, rows, whole, rows, whole, rows, rows, rows, rows),
        check_vma=False,
    )
```
